32 devices in a mesh: pipe: 4 (over x, core), seq: 8 (over z, y).
Axes of the slice: x: 2, y: 2, z: 4, core: 2. Of those that a mesh axis runs over, the one named last changes fastest.
Arguments:
- saved_inputs: bfloat16 [4, 2, 2048, 1536], P('pipe', None, 'seq'), may hold values from -54 to 54
- arrived_grad: bfloat16 [4, 2048, 1536], P('pipe', 'seq'), may hold values from -6 to 6
- loss_grad: bfloat16 [1, 2048, 1536], P(None, 'seq'), may hold values from -6 to 6
- norm_gain: float32 [4, 1536], P('pipe'), may hold values from 0.25 to 1.75
- w_gate: bfloat16 [4, 384, 1536], P('pipe'), may hold values from -0.3125 to 0.3125
- w_value: bfloat16 [4, 384, 1536], P('pipe'), may hold values from -0.3125 to 0.3125
- w_out: bfloat16 [4, 384, 1536], P('pipe'), may hold values from -0.3125 to 0.3125
- r_factor: bfloat16 [4, 2048, 256], P('pipe', 'seq'), may hold values from -0.375 to 0.375
- l_factor: bfloat16 [4, 256, 64], P('pipe', 'seq'), may hold values from -2 to 2
Outputs:
- sent_grad: bfloat16 [4, 2, 2048, 1536], P('pipe', None, 'seq')
The draws below stay inside these ranges and needn't reach their ends.
All inputs are finite; a program needn't handle non-finite values.
Results may differ from the reference program's by a relative error of at most 0.008.
Values may be sent and summed in bfloat16 or wider, within the bound.
No kernel may reach another device: no remote copies, remote signals or barrier semaphores. Data moves between devices by JAX's collectives and lax.ppermute only.
A program may use at most 128 MiB of HBM per device.

```python
import math
import jax
import jax.numpy as jnp
from jax import lax

NBLK = 4
BSZ = 384
D = 1536
TOK_DEV = 256
TICKS = 2
SECTIONS = 4
SEQLEN = 2048
N_SEQ = 8


def draw_saved_inputs(key, part):
    key_base, key_column, key_row = jax.random.split(key, 3)
    shape_all = (SECTIONS, TICKS, SEQLEN, D)
    column_scale = jnp.exp(jax.random.uniform(key_column, (1, 1, 1, D), jnp.float32, math.log(0.3), math.log(3.0)))
    row_scale = jnp.exp(jax.random.uniform(key_row, (SECTIONS, TICKS, SEQLEN, 1), jnp.float32, math.log(0.3), math.log(3.0)))
    base_draw = jnp.clip(jax.random.normal(key_base, shape_all, jnp.float32), -6.0, 6.0)
    return (base_draw * column_scale * row_scale).astype(jnp.bfloat16)


def block_scale(rng, shape, shards, smallest, top_value):
    gain = 1.0
    for axis_at, blocks in shards:
        heights = jax.random.uniform(jax.random.fold_in(jax.random.fold_in(rng, 6), axis_at), (blocks,), jnp.float32, smallest / len(shards), top_value / len(shards))
        gain = gain * jnp.repeat(jnp.exp(heights), shape[axis_at] // blocks).reshape((-1,) + (1,) * (len(shape) - 1 - axis_at))
    return gain


def noise(rng, extent, width, bound, cuts=(), kind=jnp.bfloat16):
    entries = jax.random.normal(rng, extent, jnp.float32) * width
    if len(cuts) > 0:
        entries = block_scale(rng, extent, cuts, -0.22, 0.18) * entries
    return jnp.clip(entries, min=-bound, max=bound).astype(kind)


def setup_inputs(seed: int = 0) -> dict:
    seeds = jax.random.split(jax.random.key(seed), 10)
    return {
        "saved_inputs": draw_saved_inputs(jax.random.fold_in(seeds[9], 71), 0),
        "arrived_grad": noise(seeds[1], (SECTIONS, SEQLEN, D), 1.0, 6.0, ((0, 4), (1, 8))),
        "loss_grad": noise(seeds[2], (TICKS - 1, SEQLEN, D), 1.0, 6.0, ((1, 8),)),
        "norm_gain": jnp.clip(1.0 + 0.15 * jax.random.normal(seeds[3], (SECTIONS, D), jnp.float32), 0.25, 1.75),
        "w_gate": noise(seeds[4], (SECTIONS, BSZ, D), BSZ ** -0.5, 0.3125, ((0, 4),)),
        "w_value": noise(seeds[5], (SECTIONS, BSZ, D), BSZ ** -0.5, 0.3125, ((0, 4),)),
        "w_out": noise(seeds[6], (SECTIONS, BSZ, D), BSZ ** -0.5, 0.3125, ((0, 4),)),
        "r_factor": noise(seeds[7], (SECTIONS, SEQLEN, TOK_DEV), TOK_DEV ** -0.5, 0.375, ((0, 4), (1, 8))),
        "l_factor": noise(seeds[8], (SECTIONS, TOK_DEV, N_SEQ * N_SEQ), N_SEQ ** -0.5, 2.0, ((0, 4), (1, 8))),
    }


epsilon = 1e-05

def block_apply(rows_in, weight):
    row_count = rows_in.shape[0]
    left_blocks = rows_in.astype(jnp.float32).reshape(row_count, NBLK, BSZ)
    right_blocks = weight.astype(jnp.float32).reshape(BSZ, NBLK, BSZ)
    return jnp.einsum('rnc,cnb->rnb', left_blocks, right_blocks).reshape(row_count, NBLK * BSZ)

def block_back(rows_in, weight):
    row_count = rows_in.shape[0]
    left_blocks = rows_in.astype(jnp.float32).reshape(row_count, NBLK, BSZ)
    right_blocks = weight.astype(jnp.float32).reshape(BSZ, NBLK, BSZ)
    return jnp.einsum('rnb,cnb->rnc', left_blocks, right_blocks).reshape(row_count, NBLK * BSZ)

def section_backward(layer_in, out_grad, gain_row, gate_weight, value_weight, out_weight, r_section, l_section):
    inputs_f = layer_in.astype(jnp.float32)
    inv_scale = lax.rsqrt(lax.optimization_barrier(jnp.mean(inputs_f * inputs_f, axis=-1, keepdims=True)) + epsilon)
    normed = (inputs_f * inv_scale * gain_row).astype(jnp.bfloat16)
    gate_pre = block_apply(normed, gate_weight)
    values = block_apply(normed, value_weight).astype(jnp.bfloat16)
    r_blocks = r_section.astype(jnp.float32).reshape(N_SEQ, TOK_DEV, TOK_DEV)
    l_blocks = l_section.astype(jnp.float32).reshape(TOK_DEV, N_SEQ, N_SEQ)
    first_mix = jnp.einsum('ikj,ijd->ikd', r_blocks, values.astype(jnp.float32).reshape(N_SEQ, TOK_DEV, -1)).astype(jnp.bfloat16)
    seq_mixed = jnp.einsum('kpi,ikd->pkd', l_blocks, first_mix.astype(jnp.float32)).astype(jnp.bfloat16)
    seq_mixed = seq_mixed.reshape(N_SEQ * TOK_DEV, -1)
    inner_grad = block_back(out_grad, out_weight)
    gate_sigmoid = jax.nn.sigmoid(gate_pre)
    mixed_grad = (inner_grad * gate_pre * gate_sigmoid).astype(jnp.bfloat16)
    gate_grad = (inner_grad * seq_mixed.astype(jnp.float32) * gate_sigmoid * (1.0 + gate_pre * (1.0 - gate_sigmoid))).astype(jnp.bfloat16)
    folded = jnp.einsum('kpi,pkd->ikd', l_blocks, mixed_grad.astype(jnp.float32).reshape(N_SEQ, TOK_DEV, -1)).astype(jnp.bfloat16)
    value_grad = jnp.einsum('ikj,ikd->ijd', r_blocks, folded.astype(jnp.float32)).astype(jnp.bfloat16)
    value_grad = value_grad.reshape(N_SEQ * TOK_DEV, -1)
    norm_grad = (block_back(gate_grad, gate_weight) + block_back(value_grad, value_weight)) * gain_row
    result = out_grad.astype(jnp.float32) + inv_scale * norm_grad - inv_scale * inv_scale * inv_scale * inputs_f * lax.optimization_barrier(jnp.mean(norm_grad * inputs_f, axis=-1, keepdims=True))
    return result.astype(jnp.bfloat16)

def reference(saved_inputs, arrived_grad, loss_grad, norm_gain, w_gate, w_value, w_out, r_factor, l_factor):
    previous_sent = None
    per_tick = []
    for tick_index in range(TICKS):
        current = []
        for section_index in range(SECTIONS):
            if tick_index == 0:
                incoming = arrived_grad[section_index]
            elif section_index == SECTIONS - 1:
                incoming = loss_grad[tick_index - 1]
            else:
                incoming = previous_sent[section_index + 1]
            current.append(section_backward(saved_inputs[section_index, tick_index], incoming, norm_gain[section_index], w_gate[section_index], w_value[section_index], w_out[section_index], r_factor[section_index], l_factor[section_index]))
        previous_sent = current
        per_tick.append(jnp.stack(current))
    return jnp.stack(per_tick, axis=1)
```

```python
import functools

import jax
import jax.numpy as jnp
from jax import lax
from jax.experimental import pallas as pl
from jax.experimental.pallas import tpu as pltpu
from jax.sharding import PartitionSpec as P

TICKS = 2
EPSILON = 1e-05
F32 = jnp.float32
BF16 = jnp.bfloat16
PARAMS = pltpu.CompilerParams(
    dimension_semantics=("arbitrary",), vmem_limit_bytes=32 * 1024 * 1024
)


def dot(a, b, over=((1,), (0,))):
    return lax.dot_general(a, b, (over, ((), ())), preferred_element_type=F32)


def rows_of(slot, size):
    owner = lax.axis_index("seq") ^ slot
    return pl.ds(pl.multiple_of(owner * size, size), size)


def inverse_rms(x_ref):
    x = x_ref[...].astype(F32)
    return lax.rsqrt(jnp.mean(x * x, axis=-1, keepdims=True) + EPSILON)


def columns(j, width):
    return pl.ds(pl.multiple_of(j * width, 128), width)


def split(outs, wide_ref):
    for slot, out in enumerate(outs):
        out[...] = wide_ref[rows_of(slot, out.shape[0]), :].astype(BF16)


def first_kernel(count, x_ref, gain_ref, w_ref, r_ref, *refs):
    outs, (q_ref, wide_ref) = refs[:count], refs[count:]
    j = pl.program_id(0)

    @pl.when(j == 0)
    def _():
        q_ref[...] = inverse_rms(x_ref)

    x = x_ref[:, columns(j, w_ref.shape[1])].astype(F32)
    normed = (x * q_ref[...] * gain_ref[...]).astype(BF16)
    values = dot(normed, w_ref[...]).astype(BF16)
    wide_ref[...] = dot(r_ref[...], values)
    split(outs, wide_ref)


def pick_gradient(refs):
    if len(refs) == 1:
        return refs[0][...]
    last = lax.axis_index("pipe") == lax.axis_size("pipe") - 1
    return jnp.where(last, refs[1][...], refs[0][...])


def grad_kernel(count, sources, x_ref, gain_ref, w_gate_ref, w_out_ref, *refs):
    grads, refs = refs[:sources], refs[sources:]
    outs, (factor_ref, q_ref, wide_ref) = refs[:count], refs[count:]
    j = pl.program_id(0)

    @pl.when(j == 0)
    def _():
        q_ref[...] = inverse_rms(x_ref)

    x = x_ref[:, columns(j, w_gate_ref.shape[1])].astype(F32)
    normed = (x * q_ref[...] * gain_ref[...]).astype(BF16)
    gate = dot(normed, w_gate_ref[...])
    inner = dot(pick_gradient(grads), w_out_ref[...], ((1,), (1,)))
    sigmoid = jax.nn.sigmoid(gate)
    wide_ref[...] = inner * gate * sigmoid
    factor_ref[...] = inner * sigmoid * (1.0 + gate * (1.0 - sigmoid))
    split(outs, wide_ref)


def mix_matrix(l_ref, count, size):
    wide = count * size
    tall = jnp.broadcast_to(l_ref[...].astype(F32)[None], (count, size, count * count))
    p = lax.broadcasted_iota(jnp.int32, tall.shape, 0) * count
    r = lax.broadcasted_iota(jnp.int32, tall.shape, 2)
    tall = jnp.where((r >= p) & (r < p + count), tall, 0.0)
    tall = tall.reshape(wide, count * count).astype(BF16)
    r = lax.broadcasted_iota(jnp.int32, (count * count, wide), 0) & (count - 1)
    c = lax.broadcasted_iota(jnp.int32, (count * count, wide), 1) >> (size.bit_length() - 1)
    spread = dot(tall, jnp.where(r == c, 1.0, 0.0).astype(BF16))
    row = lax.broadcasted_iota(jnp.int32, (wide, wide), 0) & (size - 1)
    column = lax.broadcasted_iota(jnp.int32, (wide, wide), 1) & (size - 1)
    return jnp.where(row == column, spread, 0.0).astype(BF16)


def mix_kernel(count, transposed, l_ref, *refs):
    ins, outs, (m_ref, wide_ref) = refs[:count], refs[count : 2 * count], refs[2 * count :]
    size = ins[0].shape[0]

    @pl.when(pl.program_id(0) == 0)
    def _():
        m_ref[...] = mix_matrix(l_ref, count, size)

    for slot in range(count):
        wide_ref[rows_of(slot, size), :] = ins[slot][...].astype(F32)
    over = ((0,), (0,)) if transposed else ((1,), (0,))
    wide_ref[...] = dot(m_ref[...], wide_ref[...].astype(BF16), over)
    split(outs, wide_ref)


def result_kernel(
    count, sources, x_ref, gain_ref, w_gate_ref, w_value_ref, r_ref, factor_ref, *refs
):
    mixed, folded, refs = refs[:count], refs[count : 2 * count], refs[2 * count :]
    grads, refs = refs[:sources], refs[sources:]
    (outs, (wide_ref, e_ref, sum_ref)) = refs[:-3], refs[-3:]
    if sources > 1:
        outs = outs[1:]
    j = pl.program_id(0)
    width = w_gate_ref.shape[1]
    size = mixed[0].shape[0]
    at = columns(j, width)
    for slot in range(count):
        wide_ref[rows_of(slot, size), :] = mixed[slot][...].astype(F32)
    gate_grad = (factor_ref[...] * wide_ref[...]).astype(BF16)
    for slot in range(count):
        wide_ref[rows_of(slot, size), :] = folded[slot][...].astype(F32)
    value_grad = dot(r_ref[...], wide_ref[...].astype(BF16), ((0,), (0,))).astype(BF16)
    e = dot(gate_grad, w_gate_ref[...], ((1,), (1,))) + dot(
        value_grad, w_value_ref[...], ((1,), (1,))
    )
    e = e * gain_ref[...]
    e_ref[:, at] = e
    part = jnp.sum(e * x_ref[:, at].astype(F32), axis=-1, keepdims=True)

    @pl.when(j == 0)
    def _():
        sum_ref[...] = part

    @pl.when(j > 0)
    def _():
        sum_ref[...] += part

    @pl.when(j == pl.num_programs(0) - 1)
    def _():
        x = x_ref[...].astype(F32)
        q = inverse_rms(x_ref)
        mean = sum_ref[...] / x.shape[1]
        result = pick_gradient(grads).astype(F32) + q * e_ref[...] - q * q * q * x * mean
        for out in outs:
            out[...] = result.astype(BF16)


def row_cut(row, j):
    return (row, 0, j)


def row_whole(row, j):
    return (row, 0, 0)


def exchange(parts):
    count = len(parts)
    return [parts[0]] + [
        lax.ppermute(parts[slot], "seq", [(i, i ^ slot) for i in range(count)])
        for slot in range(1, count)
    ]


def local(
    saved_inputs, arrived_grad, loss_grad, norm_gain, w_gate, w_value, w_out, r_factor, l_factor
):
    count = lax.axis_size("seq")
    pipe = lax.axis_size("pipe")
    _, _, rows, width = saved_inputs.shape
    block = w_gate.shape[1]
    size = rows // count
    grid = (width // block,)

    whole = pl.BlockSpec((rows, width), lambda j: (0, 0))
    whole3 = pl.BlockSpec((None, rows, width), lambda j: (0, 0, 0))
    cut = pl.BlockSpec((rows, block), lambda j: (0, j))
    cut3 = pl.BlockSpec((None, rows, block), lambda j: (0, 0, j))
    weight = pl.BlockSpec((None, block, block), lambda j: (0, 0, j))
    gain = pl.BlockSpec((1, block), lambda j: (0, j))
    square = pl.BlockSpec((None, rows, rows), lambda j: (0, 0, 0))
    small = pl.BlockSpec((None, size, count * count), lambda j: (0, 0, 0))
    slots = [pl.BlockSpec((size, block), lambda j: (0, j))] * count
    slot_shapes = [jax.ShapeDtypeStruct((size, width), BF16)] * count

    def x_of(tick):
        return pl.BlockSpec((None, None, rows, width), lambda j: (0, tick, 0, 0))

    column = pltpu.VMEM((rows, 1), F32)
    wide = pltpu.VMEM((rows, block), F32)
    product = 2 * rows * width * block

    def cost(products, arrays):
        return pl.CostEstimate(
            flops=products * product, bytes_accessed=arrays * rows * width * 2, transcendentals=0
        )

    def first(tick):
        return pl.pallas_call(
            functools.partial(first_kernel, count),
            grid=grid,
            in_specs=[x_of(tick), gain, weight, square],
            out_specs=slots,
            out_shape=slot_shapes,
            scratch_shapes=[column, wide],
            compiler_params=PARAMS,
            cost_estimate=cost(2, 4),
            name=f"first_{tick}",
        )(saved_inputs, norm_gain, w_value, r_factor)

    def grads(tick, incoming, specs):
        out = pl.pallas_call(
            functools.partial(grad_kernel, count, len(specs)),
            grid=grid,
            in_specs=[x_of(tick), gain, weight, weight, *specs],
            out_specs=[*slots, cut],
            out_shape=[*slot_shapes, jax.ShapeDtypeStruct((rows, width), F32)],
            scratch_shapes=[column, wide],
            compiler_params=PARAMS,
            cost_estimate=cost(2, 8),
            name=f"grads_{tick}",
        )(saved_inputs, norm_gain, w_gate, w_out, *incoming)
        return out[:count], out[count]

    def mix(parts, transposed, name):
        return pl.pallas_call(
            functools.partial(mix_kernel, count, transposed),
            grid=grid,
            in_specs=[small, *slots],
            out_specs=slots,
            out_shape=slot_shapes,
            scratch_shapes=[pltpu.VMEM((rows, rows), BF16), wide],
            compiler_params=PARAMS,
            cost_estimate=cost(1, 2),
            name=name,
        )(l_factor, *parts)

    def result(tick, mixed, folded, factor, incoming, specs, before):
        last = tick == TICKS - 1
        in_specs = [x_of(tick), gain, weight, weight, square, cut, *slots, *slots, *specs]
        operands = [saved_inputs, norm_gain, w_gate, w_value, r_factor, factor]
        operands += [*mixed, *folded, *incoming]
        stacked = pl.BlockSpec((None, None, rows, width), lambda j: (0, tick, 0, 0))
        out_specs = [stacked]
        out_shape = [jax.ShapeDtypeStruct(saved_inputs.shape, BF16)]
        aliases = {}
        if before is not None:
            aliases = {len(operands): 0}
            in_specs.append(pl.BlockSpec(memory_space=pl.ANY))
            operands.append(before)
        if not last:
            out_specs.append(whole)
            out_shape.append(jax.ShapeDtypeStruct((rows, width), BF16))
        return pl.pallas_call(
            functools.partial(result_kernel, count, len(specs)),
            grid=grid,
            in_specs=in_specs,
            out_specs=out_specs,
            out_shape=out_shape,
            scratch_shapes=[wide, pltpu.VMEM((rows, width), F32), column],
            input_output_aliases=aliases,
            compiler_params=PARAMS,
            cost_estimate=cost(3, 8),
            name=f"result_{tick}",
        )(*operands)

    incoming, cuts, wholes = (arrived_grad,), (cut3,), (whole3,)
    stacked = None
    first_there = []
    for tick in range(TICKS):
        grad_parts, factor = grads(tick, incoming, cuts)
        grad_there = exchange(grad_parts)
        if tick == 0:
            first_there = [exchange(first(later)) for later in range(TICKS)]
        folded = exchange(mix(grad_there, True, f"fold_{tick}"))
        mixed = exchange(mix(first_there[tick], False, f"mix_{tick}"))
        outs = result(tick, mixed, folded, factor, incoming, wholes, stacked)
        stacked = outs[0]
        if tick + 1 < TICKS:
            passed = lax.ppermute(outs[1], "pipe", [(s, s - 1) for s in range(1, pipe)])
            incoming = (passed, loss_grad)
            cuts = (cut, pl.BlockSpec((None, rows, block), functools.partial(row_cut, tick)))
            wholes = (whole, pl.BlockSpec((None, rows, width), functools.partial(row_whole, tick)))
    return stacked


def solution(mesh):
    placed = (
        P("pipe", None, "seq", None),
        P("pipe", "seq", None),
        P(None, "seq", None),
        P("pipe", None),
        P("pipe", None, None),
        P("pipe", None, None),
        P("pipe", None, None),
        P("pipe", "seq", None),
        P("pipe", "seq", None),
    )
    return jax.shard_map(
        local, mesh=mesh, in_specs=placed, out_specs=P("pipe", None, "seq", None), check_vma=False
    )
```

```python
import functools

import jax
import jax.numpy as jnp
from jax import lax
from jax.experimental import pallas as pl
from jax.experimental.pallas import tpu as pltpu
from jax.sharding import PartitionSpec as P

TICKS = 2
EPSILON = 1e-05
F32 = jnp.float32
BF16 = jnp.bfloat16
WINDOW = 5


def params(mebibytes=32):
    return pltpu.CompilerParams(
        dimension_semantics=("arbitrary",), vmem_limit_bytes=mebibytes * 1024 * 1024
    )


def dot(a, b, over=((1,), (0,))):
    return lax.dot_general(a, b, (over, ((), ())), preferred_element_type=F32)


def rows_of(slot, size):
    owner = lax.axis_index("seq") ^ slot
    return pl.ds(pl.multiple_of(owner * size, size), size)


def inverse_rms(x_ref):
    x = x_ref[...].astype(F32)
    return lax.rsqrt(jnp.mean(x * x, axis=-1, keepdims=True) + EPSILON)


def columns(j, width):
    return pl.ds(pl.multiple_of(j * width, 128), width)


def split(outs, wide_ref):
    for slot, out in enumerate(outs):
        out[...] = wide_ref[rows_of(slot, out.shape[0]), :].astype(BF16)


def first_kernel(count, x_ref, gain_ref, w_ref, r_ref, *refs):
    outs, (q_ref, wide_ref) = refs[:count], refs[count:]
    j = pl.program_id(0)

    @pl.when(j == 0)
    def _():
        q_ref[...] = inverse_rms(x_ref)

    x = x_ref[:, columns(j, w_ref.shape[1])].astype(F32)
    normed = (x * q_ref[...] * gain_ref[...]).astype(BF16)
    values = dot(normed, w_ref[...]).astype(BF16)
    wide_ref[...] = dot(r_ref[...], values)
    split(outs, wide_ref)


def pick_gradient(refs):
    if len(refs) == 1:
        return refs[0][...]
    last = lax.axis_index("pipe") == lax.axis_size("pipe") - 1
    return jnp.where(last, refs[1][...], refs[0][...])


def grad_kernel(count, sources, x_ref, gain_ref, w_gate_ref, w_out_ref, *refs):
    grads, refs = refs[:sources], refs[sources:]
    outs, (factor_ref, q_ref, wide_ref) = refs[:count], refs[count:]
    j = pl.program_id(0)

    @pl.when(j == 0)
    def _():
        q_ref[...] = inverse_rms(x_ref)

    x = x_ref[:, columns(j, w_gate_ref.shape[1])].astype(F32)
    normed = (x * q_ref[...] * gain_ref[...]).astype(BF16)
    gate = dot(normed, w_gate_ref[...])
    inner = dot(pick_gradient(grads), w_out_ref[...], ((1,), (1,)))
    sigmoid = jax.nn.sigmoid(gate)
    wide_ref[...] = inner * gate * sigmoid
    factor_ref[...] = inner * sigmoid * (1.0 + gate * (1.0 - sigmoid))
    split(outs, wide_ref)


def mix_matrix(l_ref, count, size):
    wide = count * size
    tall = jnp.broadcast_to(l_ref[...].astype(F32)[None], (count, size, count * count))
    p = lax.broadcasted_iota(jnp.int32, tall.shape, 0) * count
    r = lax.broadcasted_iota(jnp.int32, tall.shape, 2)
    tall = jnp.where((r >= p) & (r < p + count), tall, 0.0)
    tall = tall.reshape(wide, count * count).astype(BF16)
    r = lax.broadcasted_iota(jnp.int32, (count * count, wide), 0) & (count - 1)
    c = lax.broadcasted_iota(jnp.int32, (count * count, wide), 1) >> (size.bit_length() - 1)
    spread = dot(tall, jnp.where(r == c, 1.0, 0.0).astype(BF16))
    row = lax.broadcasted_iota(jnp.int32, (wide, wide), 0) & (size - 1)
    column = lax.broadcasted_iota(jnp.int32, (wide, wide), 1) & (size - 1)
    return jnp.where(row == column, spread, 0.0).astype(BF16)


def mix_kernel(count, transposed, l_ref, *refs):
    ins, outs, (m_ref, wide_ref) = refs[:count], refs[count : 2 * count], refs[2 * count :]
    size = ins[0].shape[0]

    @pl.when(pl.program_id(0) == 0)
    def _():
        m_ref[...] = mix_matrix(l_ref, count, size)

    for slot in range(count):
        wide_ref[rows_of(slot, size), :] = ins[slot][...].astype(F32)
    over = ((0,), (0,)) if transposed else ((1,), (0,))
    wide_ref[...] = dot(m_ref[...], wide_ref[...].astype(BF16), over)
    split(outs, wide_ref)


def gate_back_kernel(count, w_gate_ref, factor_ref, *refs):
    mixed, (out_ref, wide_ref) = refs[:count], refs[count:]
    size = mixed[0].shape[0]
    for slot in range(count):
        wide_ref[rows_of(slot, size), :] = mixed[slot][...].astype(F32)
    gate_grad = (factor_ref[...] * wide_ref[...]).astype(BF16)
    out_ref[...] = dot(gate_grad, w_gate_ref[...], ((1,), (1,)))


def result_kernel(count, sources, x_ref, gain_ref, w_value_ref, r_ref, gate_back_ref, *refs):
    folded, refs = refs[:count], refs[count:]
    grads, refs = refs[:sources], refs[sources:]
    (outs, (wide_ref, e_ref, sum_ref)) = refs[:-3], refs[-3:]
    if sources > 1:
        outs = outs[1:]
    j = pl.program_id(0)
    size = folded[0].shape[0]
    at = columns(j, w_value_ref.shape[1])
    for slot in range(count):
        wide_ref[rows_of(slot, size), :] = folded[slot][...].astype(F32)
    value_grad = dot(r_ref[...], wide_ref[...].astype(BF16), ((0,), (0,))).astype(BF16)
    e = gate_back_ref[...] + dot(value_grad, w_value_ref[...], ((1,), (1,)))
    e = e * gain_ref[...]
    e_ref[:, at] = e
    part = jnp.sum(e * x_ref[:, at].astype(F32), axis=-1, keepdims=True)

    @pl.when(j == 0)
    def _():
        sum_ref[...] = part

    @pl.when(j > 0)
    def _():
        sum_ref[...] += part

    @pl.when(j == pl.num_programs(0) - 1)
    def _():
        x = x_ref[...].astype(F32)
        q = inverse_rms(x_ref)
        mean = sum_ref[...] / x.shape[1]
        result = pick_gradient(grads).astype(F32) + q * e_ref[...] - q * q * q * x * mean
        for out in outs:
            out[...] = result.astype(BF16)


class Lane:
    def __init__(self):
        self.done = []

    def send(self, part, axis, pairs, after=()):
        boxes = [*self.done[-WINDOW:][:1], *after] if len(self.done) >= WINDOW else [*after]
        if boxes:
            part, *ended = lax.optimization_barrier((part, *(box[0] for box in boxes)))
            for box, value in zip(boxes, ended):
                box[0] = value
        box = [lax.ppermute(part, axis, pairs)]
        self.done.append(box)
        return box

    def send_slots(self, parts, slots):
        count = len(parts)
        return {
            slot: self.send(parts[slot], "seq", [(i, i ^ slot) for i in range(count)])
            for slot in slots
        }


def gathered(parts, *boxes):
    boxes = {slot: box for some in boxes for slot, box in some.items()}
    return [parts[0]] + [boxes[slot][0] for slot in range(1, len(parts))]


def slot_order(count):
    far = list(range(count // 2, count))
    near = list(range(1, count // 2)) + [None]
    return [slot for pair in zip(far, near) for slot in pair if slot is not None]


def local(
    saved_inputs, arrived_grad, loss_grad, norm_gain, w_gate, w_value, w_out, r_factor, l_factor
):
    count = lax.axis_size("seq")
    pipe = lax.axis_size("pipe")
    _, _, rows, width = saved_inputs.shape
    block = w_gate.shape[1]
    size = rows // count
    grid = (width // block,)

    whole = pl.BlockSpec((rows, width), lambda j: (0, 0))
    whole3 = pl.BlockSpec((None, rows, width), lambda j: (0, 0, 0))
    cut = pl.BlockSpec((rows, block), lambda j: (0, j))
    cut3 = pl.BlockSpec((None, rows, block), lambda j: (0, 0, j))
    weight = pl.BlockSpec((None, block, block), lambda j: (0, 0, j))
    gain = pl.BlockSpec((1, block), lambda j: (0, j))
    square = pl.BlockSpec((None, rows, rows), lambda j: (0, 0, 0))
    small = pl.BlockSpec((None, size, count * count), lambda j: (0, 0, 0))
    slots = [pl.BlockSpec((size, block), lambda j: (0, j))] * count
    slot_shapes = [jax.ShapeDtypeStruct((size, width), BF16)] * count

    def x_of(tick):
        return pl.BlockSpec((None, None, rows, width), lambda j: (0, tick, 0, 0))

    column = pltpu.VMEM((rows, 1), F32)
    wide = pltpu.VMEM((rows, block), F32)
    product = 2 * rows * width * block

    def cost(products, arrays):
        return pl.CostEstimate(
            flops=products * product, bytes_accessed=arrays * rows * width * 2, transcendentals=0
        )

    def first(tick, mebibytes=32):
        return pl.pallas_call(
            functools.partial(first_kernel, count),
            grid=grid,
            in_specs=[x_of(tick), gain, weight, square],
            out_specs=slots,
            out_shape=slot_shapes,
            scratch_shapes=[column, wide],
            compiler_params=params(mebibytes),
            cost_estimate=cost(2, 4),
            name=f"first_{tick}",
        )(saved_inputs, norm_gain, w_value, r_factor)

    def grads(tick, incoming, specs):
        out = pl.pallas_call(
            functools.partial(grad_kernel, count, len(specs)),
            grid=grid,
            in_specs=[x_of(tick), gain, weight, weight, *specs],
            out_specs=[*slots, cut],
            out_shape=[*slot_shapes, jax.ShapeDtypeStruct((rows, width), F32)],
            scratch_shapes=[column, wide],
            compiler_params=params(),
            cost_estimate=cost(2, 8),
            name=f"grads_{tick}",
        )(saved_inputs, norm_gain, w_gate, w_out, *incoming)
        return out[:count], out[count]

    def mix(parts, transposed, name):
        return pl.pallas_call(
            functools.partial(mix_kernel, count, transposed),
            grid=grid,
            in_specs=[small, *slots],
            out_specs=slots,
            out_shape=slot_shapes,
            scratch_shapes=[pltpu.VMEM((rows, rows), BF16), wide],
            compiler_params=params(),
            cost_estimate=cost(1, 2),
            name=name,
        )(l_factor, *parts)

    def gate_back(tick, mixed, factor):
        return pl.pallas_call(
            functools.partial(gate_back_kernel, count),
            grid=grid,
            in_specs=[weight, cut, *slots],
            out_specs=cut,
            out_shape=jax.ShapeDtypeStruct((rows, width), F32),
            scratch_shapes=[wide],
            compiler_params=params(),
            cost_estimate=cost(1, 6),
            name=f"gate_back_{tick}",
        )(w_gate, factor, *mixed)

    def result(tick, gate_part, folded, incoming, specs, before):
        last = tick == TICKS - 1
        in_specs = [x_of(tick), gain, weight, square, cut, *slots, *specs]
        operands = [saved_inputs, norm_gain, w_value, r_factor, gate_part, *folded, *incoming]
        stacked = pl.BlockSpec((None, None, rows, width), lambda j: (0, tick, 0, 0))
        out_specs = [stacked]
        out_shape = [jax.ShapeDtypeStruct(saved_inputs.shape, BF16)]
        aliases = {}
        if before is not None:
            aliases = {len(operands): 0}
            in_specs.append(pl.BlockSpec(memory_space=pl.ANY))
            operands.append(before)
        if not last:
            out_specs.append(whole)
            out_shape.append(jax.ShapeDtypeStruct((rows, width), BF16))
        return pl.pallas_call(
            functools.partial(result_kernel, count, len(specs)),
            grid=grid,
            in_specs=in_specs,
            out_specs=out_specs,
            out_shape=out_shape,
            scratch_shapes=[wide, pltpu.VMEM((rows, width), F32), column],
            input_output_aliases=aliases,
            compiler_params=params(),
            cost_estimate=cost(3, 8),
            name=f"result_{tick}",
        )(*operands)

    lane = Lane()
    order = slot_order(count)
    some, rest = order[: count // 2 - 1], order[count // 2 - 1 :]
    later_grad = (cut, pl.BlockSpec((None, rows, block), lambda j: (0, 0, j)))
    later_whole = (whole, pl.BlockSpec((None, rows, width), lambda j: (0, 0, 0)))

    first_0 = first(0, 60)
    first_0_there = lane.send_slots(first_0, order)
    grad_0, factor_0 = grads(0, (arrived_grad,), (cut3,))
    grad_0_there = lane.send_slots(grad_0, order)
    mix_0 = mix(gathered(first_0, first_0_there), False, "mix_0")
    mix_0_there = lane.send_slots(mix_0, order)
    fold_0 = mix(gathered(grad_0, grad_0_there), True, "fold_0")
    fold_0_there = lane.send_slots(fold_0, order)
    first_1 = first(1)
    first_1_there = lane.send_slots(first_1, order)
    gate_0 = gate_back(0, gathered(mix_0, mix_0_there), factor_0)
    stacked, passed = result(
        0, gate_0, gathered(fold_0, fold_0_there), (arrived_grad,), (whole3,), None
    )
    ahead = [first_1_there[slot] for slot in some]
    lane.done, recent = [], lane.done
    passed = lane.send(passed, "pipe", [(s, s - 1) for s in range(1, pipe)], ahead)
    lane.done = recent + lane.done
    mix_1 = mix(gathered(first_1, first_1_there), False, "mix_1")
    mix_1_some = lane.send_slots(mix_1, some)
    grad_1, factor_1 = grads(1, (passed[0], loss_grad), later_grad)
    grad_1_there = lane.send_slots(grad_1, order)
    mix_1_rest = lane.send_slots(mix_1, rest)
    fold_1 = mix(gathered(grad_1, grad_1_there), True, "fold_1")
    fold_1_there = lane.send_slots(fold_1, order)
    gate_1 = gate_back(1, gathered(mix_1, mix_1_some, mix_1_rest), factor_1)
    return result(
        1, gate_1, gathered(fold_1, fold_1_there), (passed[0], loss_grad), later_whole, stacked
    )[0]


def solution(mesh):
    placed = (
        P("pipe", None, "seq", None),
        P("pipe", "seq", None),
        P(None, "seq", None),
        P("pipe", None),
        P("pipe", None, None),
        P("pipe", None, None),
        P("pipe", None, None),
        P("pipe", "seq", None),
        P("pipe", "seq", None),
    )
    return jax.shard_map(
        local, mesh=mesh, in_specs=placed, out_specs=P("pipe", None, "seq", None), check_vma=False
    )
```

```python
import functools

import jax
import jax.numpy as jnp
from jax import lax
from jax.experimental import pallas as pl
from jax.experimental.pallas import tpu as pltpu
from jax.sharding import PartitionSpec as P

TICKS = 2
EPSILON = 1e-05
F32 = jnp.float32
BF16 = jnp.bfloat16
def params(mebibytes=32):
    return pltpu.CompilerParams(
        dimension_semantics=("arbitrary",), vmem_limit_bytes=mebibytes * 1024 * 1024
    )


def dot(a, b, over=((1,), (0,))):
    return lax.dot_general(a, b, (over, ((), ())), preferred_element_type=F32)


def rows_of(slot, size):
    owner = lax.axis_index("seq") ^ slot
    return pl.ds(pl.multiple_of(owner * size, size), size)


def inverse_rms(x_ref):
    x = x_ref[...].astype(F32)
    return lax.rsqrt(jnp.mean(x * x, axis=-1, keepdims=True) + EPSILON)


def columns(j, width):
    return pl.ds(pl.multiple_of(j * width, 128), width)


def split(outs, wide_ref):
    for slot, out in enumerate(outs):
        out[...] = wide_ref[rows_of(slot, out.shape[0]), :].astype(BF16)


def normed_block(j, x_ref, gain_ref, q_ref, width):
    @pl.when(j == 0)
    def _():
        q_ref[...] = inverse_rms(x_ref)

    x = x_ref[:, columns(j, width)].astype(F32)
    return (x * q_ref[...] * gain_ref[...]).astype(BF16)


def first_of(normed, w_ref, r_ref):
    return dot(r_ref[...], dot(normed, w_ref[...]).astype(BF16))


def grads_of(normed, grad, w_gate_ref, w_out_ref, factor_ref):
    gate = dot(normed, w_gate_ref[...])
    inner = dot(grad, w_out_ref[...], ((1,), (1,)))
    sigmoid = jax.nn.sigmoid(gate)
    factor_ref[...] = inner * sigmoid * (1.0 + gate * (1.0 - sigmoid))
    return inner * gate * sigmoid


def first_kernel(x_ref, gain_ref, w_ref, r_ref, out_ref, q_ref):
    normed = normed_block(pl.program_id(0), x_ref, gain_ref, q_ref, w_ref.shape[1])
    out_ref[...] = first_of(normed, w_ref, r_ref).astype(BF16)


def both_kernel(
    count, x_ref, gain_ref, w_value_ref, r_ref, w_gate_ref, w_out_ref, grad_ref, *refs
):
    outs, (factor_ref, q_ref, wide_ref) = refs[:count], refs[count:]
    normed = normed_block(pl.program_id(0), x_ref, gain_ref, q_ref, w_gate_ref.shape[1])
    wide_ref[...] = grads_of(normed, grad_ref[...], w_gate_ref, w_out_ref, factor_ref)
    split([out.at[1] for out in outs], wide_ref)
    wide_ref[...] = first_of(normed, w_value_ref, r_ref)
    split([out.at[0] for out in outs], wide_ref)


def pick_gradient(refs):
    if len(refs) == 1:
        return refs[0][...]
    last = lax.axis_index("pipe") == lax.axis_size("pipe") - 1
    return jnp.where(last, refs[1][...], refs[0][...])


def grad_kernel(count, sources, x_ref, gain_ref, w_gate_ref, w_out_ref, *refs):
    grads, refs = refs[:sources], refs[sources:]
    outs, (factor_ref, q_ref, wide_ref) = refs[:count], refs[count:]
    normed = normed_block(pl.program_id(0), x_ref, gain_ref, q_ref, w_gate_ref.shape[1])
    wide_ref[...] = grads_of(normed, pick_gradient(grads), w_gate_ref, w_out_ref, factor_ref)
    split(outs, wide_ref)


def mix_matrix(l_ref, count, size):
    wide = count * size
    tall = jnp.broadcast_to(l_ref[...].astype(F32)[None], (count, size, count * count))
    p = lax.broadcasted_iota(jnp.int32, tall.shape, 0) * count
    r = lax.broadcasted_iota(jnp.int32, tall.shape, 2)
    tall = jnp.where((r >= p) & (r < p + count), tall, 0.0)
    tall = tall.reshape(wide, count * count).astype(BF16)
    r = lax.broadcasted_iota(jnp.int32, (count * count, wide), 0) & (count - 1)
    c = lax.broadcasted_iota(jnp.int32, (count * count, wide), 1) >> (size.bit_length() - 1)
    spread = dot(tall, jnp.where(r == c, 1.0, 0.0).astype(BF16))
    row = lax.broadcasted_iota(jnp.int32, (wide, wide), 0) & (size - 1)
    column = lax.broadcasted_iota(jnp.int32, (wide, wide), 1) & (size - 1)
    return jnp.where(row == column, spread, 0.0).astype(BF16)


def joined(ins, wide_ref):
    for slot, part in enumerate(ins):
        wide_ref[rows_of(slot, part.shape[0]), :] = part[...].astype(F32)
    return wide_ref[...]


def make_matrix(l_ref, m_ref, count):
    @pl.when(pl.program_id(0) == 0)
    def _():
        m_ref[...] = mix_matrix(l_ref, count, l_ref.shape[0])


def mix_kernel(count, l_ref, in_ref, out_ref, m_ref):
    make_matrix(l_ref, m_ref, count)
    out_ref[...] = dot(m_ref[...], in_ref[...]).astype(BF16)


def fold_kernel(count, l_ref, *refs):
    ins, outs, (m_ref, wide_ref) = refs[:count], refs[count : 2 * count], refs[2 * count :]
    make_matrix(l_ref, m_ref, count)
    wide_ref[...] = dot(m_ref[...], joined(ins, wide_ref).astype(BF16), ((0,), (0,)))
    split(outs, wide_ref)


def mix_fold_kernel(count, l_ref, *refs):
    ins, outs, (m_ref, wide_ref) = refs[:count], refs[count : 2 * count], refs[2 * count :]
    make_matrix(l_ref, m_ref, count)
    for half, over in ((0, ((1,), (0,))), (1, ((0,), (0,)))):
        value = joined([part.at[half] for part in ins], wide_ref).astype(BF16)
        wide_ref[...] = dot(m_ref[...], value, over)
        split([out.at[half] for out in outs], wide_ref)


def gate_back_kernel(w_gate_ref, factor_ref, mixed_ref, out_ref):
    gate_grad = (factor_ref[...] * mixed_ref[...].astype(F32)).astype(BF16)
    out_ref[...] = dot(gate_grad, w_gate_ref[...], ((1,), (1,)))


def finish(j, back, folded, grads, outs, x_ref, gain_ref, w_value_ref, r_ref, e_ref, sum_ref):
    at = columns(j, w_value_ref.shape[1])
    value_grad = dot(r_ref[...], folded.astype(BF16), ((0,), (0,))).astype(BF16)
    e = (back + dot(value_grad, w_value_ref[...], ((1,), (1,)))) * gain_ref[...]
    e_ref[:, at] = e
    part = jnp.sum(e * x_ref[:, at].astype(F32), axis=-1, keepdims=True)

    @pl.when(j == 0)
    def _():
        sum_ref[...] = part

    @pl.when(j > 0)
    def _():
        sum_ref[...] += part

    @pl.when(j == pl.num_programs(0) - 1)
    def _():
        x = x_ref[...].astype(F32)
        q = inverse_rms(x_ref)
        mean = sum_ref[...] / x.shape[1]
        result = pick_gradient(grads).astype(F32) + q * e_ref[...] - q * q * q * x * mean
        for out in outs:
            out[...] = result.astype(BF16)


def result_both_kernel(
    count, x_ref, gain_ref, w_value_ref, r_ref, w_gate_ref, factor_ref, grad_ref, *refs
):
    ins, (stacked_ref, out_ref, wide_ref, e_ref, sum_ref) = refs[:count], refs[count:]
    mixed = joined([part.at[0] for part in ins], wide_ref)
    gate_grad = (factor_ref[...] * mixed).astype(BF16)
    back = dot(gate_grad, w_gate_ref[...], ((1,), (1,)))
    folded = joined([part.at[1] for part in ins], wide_ref)
    finish(
        pl.program_id(0), back, folded, (grad_ref,), (stacked_ref, out_ref),
        x_ref, gain_ref, w_value_ref, r_ref, e_ref, sum_ref,
    )


def result_kernel(count, sources, x_ref, gain_ref, w_value_ref, r_ref, back_ref, *refs):
    folded, refs = refs[:count], refs[count:]
    grads, (_, out_ref, wide_ref, e_ref, sum_ref) = refs[:sources], refs[sources:]
    finish(
        pl.program_id(0), back_ref[...], joined(folded, wide_ref), grads, (out_ref,),
        x_ref, gain_ref, w_value_ref, r_ref, e_ref, sum_ref,
    )


def exchange(parts):
    count = len(parts)
    return [parts[0]] + [
        lax.ppermute(parts[slot], "seq", [(i, i ^ slot) for i in range(count)])
        for slot in range(1, count)
    ]


def exchange_whole(value, count):
    rows, width = value.shape
    value = value.reshape(count, rows // count, width)
    return lax.all_to_all(value, "seq", 0, 0, tiled=True).reshape(rows, width)


def local(
    saved_inputs, arrived_grad, loss_grad, norm_gain, w_gate, w_value, w_out, r_factor, l_factor
):
    count = lax.axis_size("seq")
    pipe = lax.axis_size("pipe")
    _, _, rows, width = saved_inputs.shape
    block = w_gate.shape[1]
    size = rows // count

    whole = pl.BlockSpec((rows, width), lambda j: (0, 0))
    whole3 = pl.BlockSpec((None, rows, width), lambda j: (0, 0, 0))
    cut = pl.BlockSpec((rows, block), lambda j: (0, j))
    cut3 = pl.BlockSpec((None, rows, block), lambda j: (0, 0, j))
    weight = pl.BlockSpec((None, block, block), lambda j: (0, 0, j))
    gain = pl.BlockSpec((1, block), lambda j: (0, j))
    square = pl.BlockSpec((None, rows, rows), lambda j: (0, 0, 0))
    small = pl.BlockSpec((None, size, count * count), lambda j: (0, 0, 0))
    slots = [pl.BlockSpec((size, block), lambda j: (0, j))] * count
    pairs = [pl.BlockSpec((2, size, block), lambda j: (0, 0, j))] * count
    anywhere = pl.BlockSpec(memory_space=pl.ANY)
    x_0 = pl.BlockSpec((None, None, rows, width), lambda j: (0, 0, 0, 0))
    x_1 = pl.BlockSpec((None, None, rows, width), lambda j: (0, 1, 0, 0))

    slot_shapes = [jax.ShapeDtypeStruct((size, width), BF16)] * count
    pair_shapes = [jax.ShapeDtypeStruct((2, size, width), BF16)] * count
    plain = jax.ShapeDtypeStruct((rows, width), BF16)
    exact = jax.ShapeDtypeStruct((rows, width), F32)
    output = jax.ShapeDtypeStruct(saved_inputs.shape, BF16)

    column = pltpu.VMEM((rows, 1), F32)
    wide = pltpu.VMEM((rows, block), F32)
    full = pltpu.VMEM((rows, width), F32)
    matrix = pltpu.VMEM((rows, rows), BF16)
    product = 2 * rows * width * block

    def call(name, kernel, cost, ins, outs, scratch, mebibytes=32, aliases=None):
        return pl.pallas_call(
            kernel,
            grid=(width // block,),
            in_specs=[spec for spec, _ in ins],
            out_specs=[spec for spec, _ in outs],
            out_shape=[shape for _, shape in outs],
            scratch_shapes=scratch,
            input_output_aliases=aliases or {},
            compiler_params=params(mebibytes),
            cost_estimate=pl.CostEstimate(
                flops=cost[0] * product,
                bytes_accessed=cost[1] * rows * width * 2,
                transcendentals=0,
            ),
            name=name,
        )(*(value for _, value in ins))

    gains = (gain, norm_gain)
    value_in, gate_in, out_in = (weight, w_value), (weight, w_gate), (weight, w_out)
    r_in, l_in = (square, r_factor), (small, l_factor)

    *parts, factor_0 = call(
        "both_0",
        functools.partial(both_kernel, count),
        (4, 10),
        [(x_0, saved_inputs), gains, value_in, r_in, gate_in, out_in, (cut3, arrived_grad)],
        [*zip(pairs, pair_shapes), (cut, exact)],
        [column, wide],
        60,
    )
    parts = exchange(parts)
    (first_1,) = call(
        "first_1",
        first_kernel,
        (2, 4),
        [(x_1, saved_inputs), gains, value_in, r_in],
        [(cut, plain)],
        [column],
    )
    first_1, parts = lax.optimization_barrier((first_1, parts))
    first_1 = exchange_whole(first_1, count)
    parts = call(
        "mixfold_0",
        functools.partial(mix_fold_kernel, count),
        (2, 4),
        [l_in, *zip(pairs, parts)],
        [*zip(pairs, pair_shapes)],
        [matrix, wide],
    )
    parts = exchange(parts)
    (mix_1,) = call(
        "mix_1",
        functools.partial(mix_kernel, count),
        (1, 2),
        [l_in, (cut, first_1)],
        [(cut, plain)],
        [matrix],
    )
    mix_1, parts = lax.optimization_barrier((mix_1, parts))
    mix_1 = exchange_whole(mix_1, count)
    stacked, result_0 = call(
        "result_0",
        functools.partial(result_both_kernel, count),
        (4, 10),
        [
            (x_0, saved_inputs), gains, value_in, r_in, gate_in, (cut, factor_0),
            (whole3, arrived_grad), *zip(pairs, parts),
        ],
        [(x_0, output), (whole, plain)],
        [wide, full, column],
    )
    passed = lax.ppermute(result_0, "pipe", [(s, s - 1) for s in range(1, pipe)])
    *parts, factor_1 = call(
        "grads_1",
        functools.partial(grad_kernel, count, 2),
        (2, 8),
        [(x_1, saved_inputs), gains, gate_in, out_in, (cut, passed), (cut3, loss_grad)],
        [*zip(slots, slot_shapes), (cut, exact)],
        [column, wide],
    )
    parts = exchange(parts)
    parts = call(
        "fold_1",
        functools.partial(fold_kernel, count),
        (1, 2),
        [l_in, *zip(slots, parts)],
        [*zip(slots, slot_shapes)],
        [matrix, wide],
    )
    parts = exchange(parts)
    (back_1,) = call(
        "back_1",
        gate_back_kernel,
        (1, 6),
        [gate_in, (cut, factor_1), (cut, mix_1)],
        [(cut, exact)],
        [],
    )
    ins = [
        (x_1, saved_inputs), gains, value_in, r_in, (cut, back_1), *zip(slots, parts),
        (whole, passed), (whole3, loss_grad), (anywhere, stacked),
    ]
    (out,) = call(
        "result_1",
        functools.partial(result_kernel, count, 2),
        (3, 8),
        ins,
        [(x_1, output)],
        [wide, full, column],
        aliases={len(ins) - 1: 0},
    )
    return out


def solution(mesh):
    placed = (
        P("pipe", None, "seq", None),
        P("pipe", "seq", None),
        P(None, "seq", None),
        P("pipe", None),
        P("pipe", None, None),
        P("pipe", None, None),
        P("pipe", None, None),
        P("pipe", "seq", None),
        P("pipe", "seq", None),
    )
    return jax.shard_map(
        local, mesh=mesh, in_specs=placed, out_specs=P("pipe", None, "seq", None), check_vma=False
    )
```

```python
import functools

import jax
import jax.numpy as jnp
from jax import lax
from jax.experimental import pallas as pl
from jax.experimental.pallas import tpu as pltpu
from jax.sharding import PartitionSpec as P

TICKS = 2
EPSILON = 1e-05
F32 = jnp.float32
BF16 = jnp.bfloat16
def params(mebibytes=32):
    return pltpu.CompilerParams(
        dimension_semantics=("arbitrary",), vmem_limit_bytes=mebibytes * 1024 * 1024
    )


def dot(a, b, over=((1,), (0,))):
    return lax.dot_general(a, b, (over, ((), ())), preferred_element_type=F32)


def place():
    me = lax.axis_index("seq")
    return me >> 1, me & 1


def rows_of(slot, size):
    return pl.ds(pl.multiple_of((place()[0] ^ slot) * size, size), size)


def inverse_rms(x_ref):
    x = x_ref[...].astype(F32)
    return lax.rsqrt(jnp.mean(x * x, axis=-1, keepdims=True) + EPSILON)


def columns(j, width):
    return pl.ds(pl.multiple_of(j * width, 128), width)


def split(outs, wide_ref):
    for slot, out in enumerate(outs):
        out[...] = wide_ref[rows_of(slot, out.shape[0]), :].astype(BF16)


def normed_block(j, x_ref, gain_ref, q_ref, width):
    @pl.when(j == 0)
    def _():
        q_ref[...] = inverse_rms(x_ref)

    x = x_ref[:, columns(j, width)].astype(F32)
    return (x * q_ref[...] * gain_ref[...]).astype(BF16)


def first_of(normed, w_ref, r_ref):
    return dot(r_ref[...], dot(normed, w_ref[...]).astype(BF16))


def grads_of(normed, grad, w_gate_ref, w_out_ref, factor_ref):
    gate = dot(normed, w_gate_ref[...])
    inner = dot(grad, w_out_ref[...], ((1,), (1,)))
    sigmoid = jax.nn.sigmoid(gate)
    factor_ref[...] = inner * sigmoid * (1.0 + gate * (1.0 - sigmoid))
    return inner * gate * sigmoid


def first_kernel(count, x_ref, gain_ref, w_ref, r_ref, *refs):
    outs, (q_ref, wide_ref) = refs[:count], refs[count:]
    normed = normed_block(pl.program_id(0), x_ref, gain_ref, q_ref, w_ref.shape[1])
    wide_ref[...] = first_of(normed, w_ref, r_ref)
    split(outs, wide_ref)


def pick_gradient(refs):
    if len(refs) == 1:
        return refs[0][...]
    last = lax.axis_index("pipe") == lax.axis_size("pipe") - 1
    return jnp.where(last, refs[1][...], refs[0][...])


def grad_kernel(count, sources, x_ref, gain_ref, w_gate_ref, w_out_ref, *refs):
    grads, refs = refs[:sources], refs[sources:]
    outs, (factor_ref, q_ref, wide_ref) = refs[:count], refs[count:]
    normed = normed_block(pl.program_id(0), x_ref, gain_ref, q_ref, w_gate_ref.shape[1])
    wide_ref[...] = grads_of(normed, pick_gradient(grads), w_gate_ref, w_out_ref, factor_ref)
    split(outs, wide_ref)


def sum_matrix(l, count, transposed, same_side):
    size = l.shape[0]
    pairs = count // 2
    wide = pairs * size
    bits = count.bit_length() - 1
    hi, lo = place()
    iota = functools.partial(lax.broadcasted_iota, jnp.int32)

    shape = (pairs, size, count * count)
    to = 2 * (iota(shape, 0) ^ hi) + (lo if same_side else 1 - lo)
    at = iota(shape, 2)
    at = at & (count - 1) if transposed else at >> bits
    tall = jnp.where(at == to, jnp.broadcast_to(l[None], shape), 0.0)
    tall = tall.reshape(wide, count * count).astype(BF16)

    shape = (count * count, wide)
    source = 2 * ((iota(shape, 1) >> (size.bit_length() - 1)) ^ hi) + lo
    at = iota(shape, 0)
    at = at >> bits if transposed else at & (count - 1)
    spread = dot(tall, jnp.where(at == source, 1.0, 0.0).astype(BF16))

    row, column = iota((wide, wide), 0) & (size - 1), iota((wide, wide), 1) & (size - 1)
    return jnp.where(row == column, spread, 0.0).astype(BF16)


def matrices_kernel(count, mine_ref, other_ref, mix_ref, fold_ref, l_ref):
    size = mine_ref.shape[0]
    _, lo = place()
    l_ref[pl.ds(pl.multiple_of(lo * size, size), size), :] = mine_ref[...].astype(F32)
    l_ref[pl.ds(pl.multiple_of((1 - lo) * size, size), size), :] = other_ref[...].astype(F32)
    for out_ref, transposed in ((mix_ref, False), (fold_ref, True)):
        for side in range(2):
            out_ref[side] = sum_matrix(l_ref[...], count, transposed, side == 0)


def part_kernel(count, m_ref, *refs):
    ins, (keep_ref, send_ref) = refs[:count], refs[count:]
    value = jnp.concatenate([part[...] for part in ins], axis=0)
    keep_ref[...] = dot(m_ref[0], value)
    send_ref[...] = dot(m_ref[1], value).astype(BF16)


def total_kernel(keep_ref, other_ref, *outs):
    size = outs[0].shape[0]
    for slot, out in enumerate(outs):
        at = slice(slot * size, (slot + 1) * size)
        out[...] = (keep_ref[at, :] + other_ref[at, :].astype(F32)).astype(BF16)


def joined(ins, wide_ref):
    for slot, part in enumerate(ins):
        wide_ref[rows_of(slot, part.shape[0]), :] = part[...].astype(F32)
    return wide_ref[...]


def back_kernel(count, w_gate_ref, factor_ref, *refs):
    mixed, (out_ref, wide_ref) = refs[:count], refs[count:]
    gate_grad = (factor_ref[...] * joined(mixed, wide_ref)).astype(BF16)
    out_ref[...] = dot(gate_grad, w_gate_ref[...], ((1,), (1,)))


def finish(j, back, folded, grads, outs, x_ref, gain_ref, w_value_ref, r_ref, e_ref, sum_ref):
    at = columns(j, w_value_ref.shape[1])
    value_grad = dot(r_ref[...], folded.astype(BF16), ((0,), (0,))).astype(BF16)
    e = (back + dot(value_grad, w_value_ref[...], ((1,), (1,)))) * gain_ref[...]
    e_ref[:, at] = e
    part = jnp.sum(e * x_ref[:, at].astype(F32), axis=-1, keepdims=True)

    @pl.when(j == 0)
    def _():
        sum_ref[...] = part

    @pl.when(j > 0)
    def _():
        sum_ref[...] += part

    @pl.when(j == pl.num_programs(0) - 1)
    def _():
        x = x_ref[...].astype(F32)
        q = inverse_rms(x_ref)
        mean = sum_ref[...] / x.shape[1]
        result = pick_gradient(grads).astype(F32) + q * e_ref[...] - q * q * q * x * mean
        for out in outs:
            out[...] = result.astype(BF16)


def result_kernel(count, sources, x_ref, gain_ref, w_value_ref, r_ref, back_ref, *refs):
    folded, refs = refs[:count], refs[count:]
    grads, refs = refs[:sources], refs[sources:]
    outs, (wide_ref, e_ref, sum_ref) = refs[sources - 1 : -3], refs[-3:]
    finish(
        pl.program_id(0), back_ref[...], joined(folded, wide_ref), grads, outs,
        x_ref, gain_ref, w_value_ref, r_ref, e_ref, sum_ref,
    )


def exchange(parts):
    return [parts[0]] + [
        lax.ppermute(parts[slot], "seq", [(i, i ^ (2 * slot)) for i in range(2 * len(parts))])
        for slot in range(1, len(parts))
    ]


def swap(value):
    return lax.ppermute(value, "seq", [(i, i ^ 1) for i in range(lax.axis_size("seq"))])


def local(
    saved_inputs, arrived_grad, loss_grad, norm_gain, w_gate, w_value, w_out, r_factor, l_factor
):
    count = lax.axis_size("seq")
    pipe = lax.axis_size("pipe")
    _, _, rows, width = saved_inputs.shape
    block = w_gate.shape[1]
    pairs = count // 2
    size = rows // pairs

    whole = pl.BlockSpec((rows, width), lambda j: (0, 0))
    whole3 = pl.BlockSpec((None, rows, width), lambda j: (0, 0, 0))
    cut = pl.BlockSpec((rows, block), lambda j: (0, j))
    cut3 = pl.BlockSpec((None, rows, block), lambda j: (0, 0, j))
    weight = pl.BlockSpec((None, block, block), lambda j: (0, 0, j))
    gain = pl.BlockSpec((1, block), lambda j: (0, j))
    square = pl.BlockSpec((None, rows, rows), lambda j: (0, 0, 0))
    small = pl.BlockSpec((None, size // 2, count * count), lambda j: (0, 0, 0))
    both = pl.BlockSpec((2, rows, rows), lambda j: (0, 0, 0))
    slots = [pl.BlockSpec((size, block), lambda j: (0, j))] * pairs
    anywhere = pl.BlockSpec(memory_space=pl.ANY)
    x_at = [
        pl.BlockSpec((None, None, rows, width), functools.partial(tick_index, tick))
        for tick in range(TICKS)
    ]

    slot_shapes = [jax.ShapeDtypeStruct((size, width), BF16)] * pairs
    plain = jax.ShapeDtypeStruct((rows, width), BF16)
    exact = jax.ShapeDtypeStruct((rows, width), F32)
    output = jax.ShapeDtypeStruct(saved_inputs.shape, BF16)
    two = jax.ShapeDtypeStruct((2, rows, rows), BF16)

    column = pltpu.VMEM((rows, 1), F32)
    wide = pltpu.VMEM((rows, block), F32)
    full = pltpu.VMEM((rows, width), F32)
    product = 2 * rows * width * block

    def call(name, kernel, cost, ins, outs, scratch, mebibytes=32, aliases=None, steps=None):
        return pl.pallas_call(
            kernel,
            grid=(steps or width // block,),
            in_specs=[spec for spec, _ in ins],
            out_specs=[spec for spec, _ in outs],
            out_shape=[shape for _, shape in outs],
            scratch_shapes=scratch,
            input_output_aliases=aliases or {},
            compiler_params=params(mebibytes),
            cost_estimate=pl.CostEstimate(
                flops=int(cost[0] * product),
                bytes_accessed=int(cost[1] * rows * width * 2),
                transcendentals=0,
            ),
            name=name,
        )(*(value for _, value in ins))

    gains = (gain, norm_gain)
    value_in, gate_in, out_in = (weight, w_value), (weight, w_gate), (weight, w_out)
    r_in = (square, r_factor)

    def first(tick):
        return call(
            f"first_{tick}",
            functools.partial(first_kernel, pairs),
            (2, 4),
            [(x_at[tick], saved_inputs), gains, value_in, r_in],
            [*zip(slots, slot_shapes)],
            [column, wide],
            60 if tick == 0 else 32,
        )

    def grads(tick, incoming):
        *parts, factor = call(
            f"grads_{tick}",
            functools.partial(grad_kernel, pairs, len(incoming)),
            (2, 8),
            [(x_at[tick], saved_inputs), gains, gate_in, out_in, *incoming],
            [*zip(slots, slot_shapes), (cut, exact)],
            [column, wide],
        )
        return parts, factor

    def part(name, matrix, parts):
        return call(
            name,
            functools.partial(part_kernel, pairs),
            (1.4, 4),
            [(both, matrix), *zip(slots, parts)],
            [(cut, exact), (cut, plain)],
            [],
        )

    def total(name, keep, other):
        return call(
            name,
            total_kernel,
            (0.1, 4),
            [(cut, keep), (cut, other)],
            [*zip(slots, slot_shapes)],
            [],
        )

    def back(tick, mixed, factor):
        return call(
            f"back_{tick}",
            functools.partial(back_kernel, pairs),
            (1, 6),
            [gate_in, (cut, factor), *zip(slots, mixed)],
            [(cut, exact)],
            [wide],
        )[0]

    def result(tick, gate_part, folded, incoming, stacked):
        ins = [(x_at[tick], saved_inputs), gains, value_in, r_in, (cut, gate_part)]
        ins += [*zip(slots, folded), *incoming]
        outs = [(x_at[tick], output)]
        aliases = {}
        if stacked is None:
            outs.append((whole, plain))
        else:
            ins.append((anywhere, stacked))
            aliases = {len(ins) - 1: 0}
        return call(
            f"result_{tick}",
            functools.partial(result_kernel, pairs, len(incoming)),
            (3, 8),
            ins,
            outs,
            [wide, full, column],
            aliases=aliases,
        )

    l_other = swap(l_factor)
    first_0 = exchange(first(0))
    mixing, folding = call(
        "matrices",
        functools.partial(matrices_kernel, count),
        (0.3, 1),
        [(small, l_factor), (small, l_other)],
        [(both, two), (both, two)],
        [pltpu.VMEM((size, count * count), F32)],
        steps=1,
    )
    grad_0, factor_0 = grads(0, [(cut3, arrived_grad)])
    grad_0 = exchange(grad_0)
    keep_mix, send_mix = part("part_mix_0", mixing, first_0)
    other_mix = swap(send_mix)
    keep_fold, send_fold = part("part_fold_0", folding, grad_0)
    mix_0 = exchange(total("total_mix_0", keep_mix, other_mix))
    fold_0 = exchange(total("total_fold_0", keep_fold, swap(send_fold)))
    gate_0 = back(0, mix_0, factor_0)
    first_1 = first(1)
    gate_0, first_1 = lax.optimization_barrier((gate_0, first_1))
    first_1 = exchange(first_1)
    stacked, result_0 = result(0, gate_0, fold_0, [(whole3, arrived_grad)], None)
    passed = lax.ppermute(result_0, "pipe", [(s, s - 1) for s in range(1, pipe)])

    keep_mix, send_mix = part("part_mix_1", mixing, first_1)
    other_mix = swap(send_mix)
    grad_1, factor_1 = grads(1, [(cut, passed), (cut3, loss_grad)])
    grad_1 = exchange(grad_1)
    mix_1 = exchange(total("total_mix_1", keep_mix, other_mix))
    keep_fold, send_fold = part("part_fold_1", folding, grad_1)
    fold_1 = exchange(total("total_fold_1", keep_fold, swap(send_fold)))
    gate_1 = back(1, mix_1, factor_1)
    return result(1, gate_1, fold_1, [(whole, passed), (whole3, loss_grad)], stacked)[0]


def tick_index(tick, j):
    return (0, tick, 0, 0)


def solution(mesh):
    placed = (
        P("pipe", None, "seq", None),
        P("pipe", "seq", None),
        P(None, "seq", None),
        P("pipe", None),
        P("pipe", None, None),
        P("pipe", None, None),
        P("pipe", None, None),
        P("pipe", "seq", None),
        P("pipe", "seq", None),
    )
    return jax.shard_map(
        local, mesh=mesh, in_specs=placed, out_specs=P("pipe", None, "seq", None), check_vma=False
    )
```

```python
import functools

import jax
import jax.numpy as jnp
from jax import lax
from jax.experimental import pallas as pl
from jax.experimental.pallas import tpu as pltpu
from jax.sharding import PartitionSpec as P

TICKS = 2
EPSILON = 1e-05
F32 = jnp.float32
BF16 = jnp.bfloat16
def params(mebibytes=32):
    return pltpu.CompilerParams(
        dimension_semantics=("arbitrary",), vmem_limit_bytes=mebibytes * 1024 * 1024
    )


def dot(a, b, over=((1,), (0,))):
    return lax.dot_general(a, b, (over, ((), ())), preferred_element_type=F32)


def rows_of(slot, size):
    owner = lax.axis_index("seq") ^ slot
    return pl.ds(pl.multiple_of(owner * size, size), size)


def inverse_rms(x_ref):
    x = x_ref[...].astype(F32)
    return lax.rsqrt(jnp.mean(x * x, axis=-1, keepdims=True) + EPSILON)


def columns(j, width):
    return pl.ds(pl.multiple_of(j * width, 128), width)


def split(outs, wide_ref):
    for slot, out in enumerate(outs):
        out[...] = wide_ref[rows_of(slot, out.shape[0]), :].astype(BF16)


def normed_block(j, x_ref, gain_ref, q_ref, width):
    @pl.when(j == 0)
    def _():
        q_ref[...] = inverse_rms(x_ref)

    x = x_ref[:, columns(j, width)].astype(F32)
    return (x * q_ref[...] * gain_ref[...]).astype(BF16)


def first_of(normed, w_ref, r_ref):
    return dot(r_ref[...], dot(normed, w_ref[...]).astype(BF16))


def grads_of(normed, grad, w_gate_ref, w_out_ref, factor_ref):
    gate = dot(normed, w_gate_ref[...])
    inner = dot(grad, w_out_ref[...], ((1,), (1,)))
    sigmoid = jax.nn.sigmoid(gate)
    factor_ref[...] = inner * sigmoid * (1.0 + gate * (1.0 - sigmoid))
    return inner * gate * sigmoid


def first_kernel(count, x_ref, gain_ref, w_ref, r_ref, *refs):
    outs, (q_ref, wide_ref) = refs[:count], refs[count:]
    normed = normed_block(pl.program_id(0), x_ref, gain_ref, q_ref, w_ref.shape[1])
    wide_ref[...] = first_of(normed, w_ref, r_ref)
    split(outs, wide_ref)


def both_kernel(
    count, x_ref, gain_ref, w_value_ref, r_ref, w_gate_ref, w_out_ref, grad_ref, *refs
):
    outs, (factor_ref, q_ref, wide_ref) = refs[:count], refs[count:]
    normed = normed_block(pl.program_id(0), x_ref, gain_ref, q_ref, w_gate_ref.shape[1])
    wide_ref[...] = grads_of(normed, grad_ref[...], w_gate_ref, w_out_ref, factor_ref)
    split([out.at[1] for out in outs], wide_ref)
    wide_ref[...] = first_of(normed, w_value_ref, r_ref)
    split([out.at[0] for out in outs], wide_ref)


def pick_gradient(refs):
    if len(refs) == 1:
        return refs[0][...]
    last = lax.axis_index("pipe") == lax.axis_size("pipe") - 1
    return jnp.where(last, refs[1][...], refs[0][...])


def grad_kernel(count, sources, x_ref, gain_ref, w_gate_ref, w_out_ref, *refs):
    grads, refs = refs[:sources], refs[sources:]
    outs, (factor_ref, q_ref, wide_ref) = refs[:count], refs[count:]
    normed = normed_block(pl.program_id(0), x_ref, gain_ref, q_ref, w_gate_ref.shape[1])
    wide_ref[...] = grads_of(normed, pick_gradient(grads), w_gate_ref, w_out_ref, factor_ref)
    split(outs, wide_ref)


def matrix_kernel(count, l_ref, out_ref):
    size = l_ref.shape[0]
    wide = count * size
    bits = count.bit_length() - 1
    me = lax.axis_index("seq")
    iota = functools.partial(lax.broadcasted_iota, jnp.int32)

    shape = (count, size, count * count)
    tall = jnp.broadcast_to(l_ref[...].astype(F32)[None], shape)
    tall = jnp.where(iota(shape, 2) >> bits == iota(shape, 0) ^ me, tall, 0.0)
    tall = tall.reshape(wide, count * count).astype(BF16)

    shape = (count * count, wide)
    source = (iota(shape, 1) >> (size.bit_length() - 1)) ^ me
    spread = dot(tall, jnp.where(iota(shape, 0) & (count - 1) == source, 1.0, 0.0).astype(BF16))

    row, column = iota((wide, wide), 0) & (size - 1), iota((wide, wide), 1) & (size - 1)
    out_ref[...] = jnp.where(row == column, spread, 0.0).astype(BF16)


def turned(parts):
    half = len(parts) // 2
    return [*parts[half:], *parts[:half]]


def stacked_slots(ins):
    if ins[0].shape[0] % 16 == 0:
        return jnp.concatenate([part[...] for part in ins], axis=0)
    return jnp.concatenate([part[...].astype(F32) for part in ins], axis=0).astype(BF16)


def spread_slots(outs, value):
    size = outs[0].shape[0]
    for slot, out in enumerate(outs):
        out[...] = value[slot * size : (slot + 1) * size].astype(BF16)


def joined(ins, wide_ref):
    for slot, part in enumerate(ins):
        wide_ref[rows_of(slot, part.shape[0]), :] = part[...].astype(wide_ref.dtype)
    return wide_ref[...]


def mix_kernel(count, transposed, m_ref, *refs):
    ins, outs = turned(refs[:count]), refs[count:]
    over = ((0,), (0,)) if transposed else ((1,), (0,))
    spread_slots(outs, dot(m_ref[...], stacked_slots(ins), over))


def mix_fold_kernel(count, m_ref, *refs):
    ins, outs = turned(refs[:count]), refs[count:]
    for half, over in ((0, ((1,), (0,))), (1, ((0,), (0,)))):
        value = stacked_slots([part.at[half] for part in ins])
        spread_slots([out.at[half] for out in outs], dot(m_ref[...], value, over))


def back_of(w_gate_ref, factor_ref, mixed):
    gate_grad = (factor_ref[...] * mixed.astype(F32)).astype(BF16)
    return dot(gate_grad, w_gate_ref[...], ((1,), (1,)))


def back_kernel(count, w_gate_ref, factor_ref, *refs):
    mixed, (out_ref, wide_ref) = turned(refs[:count]), refs[count:]
    out_ref[...] = back_of(w_gate_ref, factor_ref, joined(mixed, wide_ref))


def finish(j, back, folded, grads, outs, x_ref, gain_ref, w_value_ref, r_ref, e_ref, sum_ref):
    at = columns(j, w_value_ref.shape[1])
    value_grad = dot(r_ref[...], folded.astype(BF16), ((0,), (0,))).astype(BF16)
    e = (back + dot(value_grad, w_value_ref[...], ((1,), (1,)))) * gain_ref[...]
    e_ref[:, at] = e
    part = jnp.sum(e * x_ref[:, at].astype(F32), axis=-1, keepdims=True)

    @pl.when(j == 0)
    def _():
        sum_ref[...] = part

    @pl.when(j > 0)
    def _():
        sum_ref[...] += part

    @pl.when(j == pl.num_programs(0) - 1)
    def _():
        x = x_ref[...].astype(F32)
        q = inverse_rms(x_ref)
        mean = sum_ref[...] / x.shape[1]
        result = pick_gradient(grads).astype(F32) + q * e_ref[...] - q * q * q * x * mean
        for out in outs:
            out[...] = result.astype(BF16)


def result_both_kernel(
    count, x_ref, gain_ref, w_value_ref, r_ref, w_gate_ref, factor_ref, grad_ref, *refs
):
    ins, (stacked_ref, out_ref, wide_ref, e_ref, sum_ref) = turned(refs[:count]), refs[count:]
    back = back_of(w_gate_ref, factor_ref, joined([part.at[0] for part in ins], wide_ref))
    folded = joined([part.at[1] for part in ins], wide_ref)
    finish(
        pl.program_id(0), back, folded, (grad_ref,), (stacked_ref, out_ref),
        x_ref, gain_ref, w_value_ref, r_ref, e_ref, sum_ref,
    )


def result_kernel(count, sources, x_ref, gain_ref, w_value_ref, r_ref, back_ref, *refs):
    folded, refs = turned(refs[:count]), refs[count:]
    grads, (_, out_ref, wide_ref, e_ref, sum_ref) = refs[:sources], refs[sources:]
    finish(
        pl.program_id(0), back_ref[...], joined(folded, wide_ref), grads, (out_ref,),
        x_ref, gain_ref, w_value_ref, r_ref, e_ref, sum_ref,
    )


class Exchange:
    def __init__(self, parts):
        self.parts = list(parts)
        self.got = {0: parts[0]}

    def send(self, slots, after=()):
        for slot in slots:
            pairs = [(i, i ^ slot) for i in range(len(self.parts))]
            self.got[slot] = lax.ppermute(tied(self.parts[slot], after), "seq", pairs)
        return self

    def all(self):
        return [self.got[slot] for slot in range(len(self.parts))]


def gate_by(exchange, other, slots):
    half = len(exchange.parts) // 2
    cut = (len(slots) + 1) // 2
    for slot in [*range(half, 2 * half), *range(1, half)]:
        after = slots[:cut] if slot == 2 * half - 1 else slots[cut:] if slot == half - 1 else []
        exchange.send([slot], [(other, at) for at in after])


def tied(value, after):
    if not after:
        return value
    value, *ended = lax.optimization_barrier((value, *(where.got[slot] for where, slot in after)))
    for (where, slot), got in zip(after, ended):
        where.got[slot] = got
    return value


def local(
    saved_inputs, arrived_grad, loss_grad, norm_gain, w_gate, w_value, w_out, r_factor, l_factor
):
    count = lax.axis_size("seq")
    pipe = lax.axis_size("pipe")
    _, _, rows, width = saved_inputs.shape
    block = w_gate.shape[1]
    size = rows // count

    whole = pl.BlockSpec((rows, width), lambda j: (0, 0))
    whole3 = pl.BlockSpec((None, rows, width), lambda j: (0, 0, 0))
    cut = pl.BlockSpec((rows, block), lambda j: (0, j))
    cut3 = pl.BlockSpec((None, rows, block), lambda j: (0, 0, j))
    weight = pl.BlockSpec((None, block, block), lambda j: (0, 0, j))
    gain = pl.BlockSpec((1, block), lambda j: (0, j))
    square = pl.BlockSpec((None, rows, rows), lambda j: (0, 0, 0))
    small = pl.BlockSpec((None, size, count * count), lambda j: (0, 0, 0))
    slots = [pl.BlockSpec((size, block), lambda j: (0, j))] * count
    pairs = [pl.BlockSpec((2, size, block), lambda j: (0, 0, j))] * count
    anywhere = pl.BlockSpec(memory_space=pl.ANY)
    x_0 = pl.BlockSpec((None, None, rows, width), lambda j: (0, 0, 0, 0))
    x_1 = pl.BlockSpec((None, None, rows, width), lambda j: (0, 1, 0, 0))

    slot_shapes = [jax.ShapeDtypeStruct((size, width), BF16)] * count
    pair_shapes = [jax.ShapeDtypeStruct((2, size, width), BF16)] * count
    plain = jax.ShapeDtypeStruct((rows, width), BF16)
    exact = jax.ShapeDtypeStruct((rows, width), F32)
    output = jax.ShapeDtypeStruct(saved_inputs.shape, BF16)

    column = pltpu.VMEM((rows, 1), F32)
    wide = pltpu.VMEM((rows, block), F32)
    full = pltpu.VMEM((rows, width), F32)
    square_plain = pl.BlockSpec((rows, rows), lambda j: (0, 0))
    joining = pltpu.VMEM((rows, block), BF16 if size % 16 == 0 else F32)
    product = 2 * rows * width * block

    def call(name, kernel, cost, ins, outs, scratch, mebibytes=32, aliases=None, steps=None):
        return pl.pallas_call(
            kernel,
            grid=(steps or width // block,),
            in_specs=[spec for spec, _ in ins],
            out_specs=[spec for spec, _ in outs],
            out_shape=[shape for _, shape in outs],
            scratch_shapes=scratch,
            input_output_aliases=aliases or {},
            compiler_params=params(mebibytes),
            cost_estimate=pl.CostEstimate(
                flops=int(cost[0] * product),
                bytes_accessed=cost[1] * rows * width * 2,
                transcendentals=0,
            ),
            name=name,
        )(*(value for _, value in ins))

    gains = (gain, norm_gain)
    value_in, gate_in, out_in = (weight, w_value), (weight, w_gate), (weight, w_out)
    r_in = (square, r_factor)
    slots_out, pairs_out = [*zip(slots, slot_shapes)], [*zip(pairs, pair_shapes)]
    half = count // 2
    far, near = range(half, count), range(1, half)
    early, late = far[: half // 2], far[half // 2 :]

    *parts, factor_0 = call(
        "both_0",
        functools.partial(both_kernel, count),
        (4, 10),
        [(x_0, saved_inputs), gains, value_in, r_in, gate_in, out_in, (cut3, arrived_grad)],
        [*pairs_out, (cut, exact)],
        [column, wide],
        60,
    )
    out_0 = Exchange(parts).send(far).send(near)
    (matrix,) = call(
        "matrix",
        functools.partial(matrix_kernel, count),
        (0.3, 1),
        [(small, l_factor)],
        [(square_plain, jax.ShapeDtypeStruct((rows, rows), BF16))],
        [],
        steps=1,
    )
    m_in = (square_plain, matrix)
    parts = call(
        "first_1",
        functools.partial(first_kernel, count),
        (2, 4),
        [(x_1, saved_inputs), gains, value_in, r_in],
        slots_out,
        [column, wide],
    )
    first_1 = Exchange(parts).send(early).send(near).send(late)
    ins = out_0.all()
    ins[0], first_1.parts[0] = lax.optimization_barrier((ins[0], first_1.parts[0]))
    parts = call(
        "mixfold_0",
        functools.partial(mix_fold_kernel, count),
        (2, 4),
        [m_in, *zip(pairs, turned(ins))],
        pairs_out,
        [],
    )
    back_0 = Exchange(parts)
    gate_by(back_0, first_1, early)
    stacked, result_0 = call(
        "result_0",
        functools.partial(result_both_kernel, count),
        (4, 10),
        [
            (x_0, saved_inputs), gains, value_in, r_in, gate_in, (cut, factor_0),
            (whole3, arrived_grad), *zip(pairs, turned(back_0.all())),
        ],
        [(x_0, output), (whole, plain)],
        [joining, full, column],
    )
    result_0 = tied(result_0, [(first_1, slot) for slot in [*late[:2], *near[:3]]])
    passed = lax.ppermute(result_0, "pipe", [(s, s - 1) for s in range(1, pipe)])
    parts = call(
        "mix_1",
        functools.partial(mix_kernel, count, False),
        (1, 2),
        [m_in, *zip(slots, turned(first_1.all()))],
        slots_out,
        [],
    )
    mix_1 = Exchange(parts).send(early).send(late).send(near)
    passed, mix_1.parts[0] = lax.optimization_barrier((passed, mix_1.parts[0]))
    *parts, factor_1 = call(
        "grads_1",
        functools.partial(grad_kernel, count, 2),
        (2, 8),
        [(x_1, saved_inputs), gains, gate_in, out_in, (cut, passed), (cut3, loss_grad)],
        [*slots_out, (cut, exact)],
        [column, wide],
    )
    grad_1 = Exchange(parts)
    gate_by(grad_1, mix_1, early)
    parts = call(
        "fold_1",
        functools.partial(mix_kernel, count, True),
        (1, 2),
        [m_in, *zip(slots, turned(grad_1.all()))],
        slots_out,
        [],
    )
    fold_1 = Exchange(parts)
    gate_by(fold_1, mix_1, late)
    (gate_1,) = call(
        "back_1",
        functools.partial(back_kernel, count),
        (1, 6),
        [gate_in, (cut, factor_1), *zip(slots, turned(mix_1.all()))],
        [(cut, exact)],
        [joining],
    )
    ins = [
        (x_1, saved_inputs), gains, value_in, r_in, (cut, gate_1), *zip(slots, turned(fold_1.all())),
        (whole, passed), (whole3, loss_grad), (anywhere, stacked),
    ]
    (out,) = call(
        "result_1",
        functools.partial(result_kernel, count, 2),
        (3, 8),
        ins,
        [(x_1, output)],
        [joining, full, column],
        aliases={len(ins) - 1: 0},
    )
    return out


def solution(mesh):
    placed = (
        P("pipe", None, "seq", None),
        P("pipe", "seq", None),
        P(None, "seq", None),
        P("pipe", None),
        P("pipe", None, None),
        P("pipe", None, None),
        P("pipe", None, None),
        P("pipe", "seq", None),
        P("pipe", "seq", None),
    )
    return jax.shard_map(
        local, mesh=mesh, in_specs=placed, out_specs=P("pipe", None, "seq", None), check_vma=False
    )
```

```python
import functools

import jax
import jax.numpy as jnp
from jax import lax
from jax.experimental import pallas as pl
from jax.experimental.pallas import tpu as pltpu
from jax.sharding import PartitionSpec as P

TICKS = 2
EPSILON = 1e-05
F32 = jnp.float32
BF16 = jnp.bfloat16
def params(mebibytes=32):
    return pltpu.CompilerParams(
        dimension_semantics=("arbitrary",), vmem_limit_bytes=mebibytes * 1024 * 1024
    )


def dot(a, b, over=((1,), (0,))):
    return lax.dot_general(a, b, (over, ((), ())), preferred_element_type=F32)


def rows_of(slot, size):
    owner = lax.axis_index("seq") ^ slot
    return pl.ds(pl.multiple_of(owner * size, size), size)


def inverse_rms(x_ref):
    x = x_ref[...].astype(F32)
    return lax.rsqrt(jnp.mean(x * x, axis=-1, keepdims=True) + EPSILON)


def columns(j, width):
    return pl.ds(pl.multiple_of(j * width, 128), width)


def split(outs, wide_ref):
    for slot, out in enumerate(outs):
        out[...] = wide_ref[rows_of(slot, out.shape[0]), :].astype(BF16)


def normed_block(j, x_ref, gain_ref, q_ref, width):
    @pl.when(j == 0)
    def _():
        q_ref[...] = inverse_rms(x_ref)

    x = x_ref[:, columns(j, width)].astype(F32)
    return (x * q_ref[...] * gain_ref[...]).astype(BF16)


def first_of(normed, w_ref, r_ref):
    return dot(r_ref[...], dot(normed, w_ref[...]).astype(BF16))


def grads_of(normed, grad, w_gate_ref, w_out_ref, factor_ref):
    gate = dot(normed, w_gate_ref[...])
    inner = dot(grad, w_out_ref[...], ((1,), (1,)))
    sigmoid = jax.nn.sigmoid(gate)
    factor_ref[...] = inner * sigmoid * (1.0 + gate * (1.0 - sigmoid))
    return inner * gate * sigmoid


def first_kernel(count, x_ref, gain_ref, w_ref, r_ref, *refs):
    outs, (q_ref, wide_ref) = refs[:count], refs[count:]
    normed = normed_block(pl.program_id(0), x_ref, gain_ref, q_ref, w_ref.shape[1])
    wide_ref[...] = first_of(normed, w_ref, r_ref)
    split(outs, wide_ref)


def pick_gradient(refs):
    if len(refs) == 1:
        return refs[0][...]
    last = lax.axis_index("pipe") == lax.axis_size("pipe") - 1
    return jnp.where(last, refs[1][...], refs[0][...])


def grad_kernel(count, sources, x_ref, gain_ref, w_gate_ref, w_out_ref, *refs):
    grads, refs = refs[:sources], refs[sources:]
    outs, (factor_ref, q_ref, wide_ref) = refs[:count], refs[count:]
    normed = normed_block(pl.program_id(0), x_ref, gain_ref, q_ref, w_gate_ref.shape[1])
    wide_ref[...] = grads_of(normed, pick_gradient(grads), w_gate_ref, w_out_ref, factor_ref)
    split(outs, wide_ref)


def matrix_kernel(count, l_ref, out_ref):
    size = l_ref.shape[0]
    wide = count * size
    bits = count.bit_length() - 1
    me = lax.axis_index("seq")
    iota = functools.partial(lax.broadcasted_iota, jnp.int32)

    shape = (count, size, count * count)
    tall = jnp.broadcast_to(l_ref[...].astype(F32)[None], shape)
    tall = jnp.where(iota(shape, 2) >> bits == iota(shape, 0) ^ me, tall, 0.0)
    tall = tall.reshape(wide, count * count).astype(BF16)

    shape = (count * count, wide)
    source = (iota(shape, 1) >> (size.bit_length() - 1)) ^ me
    spread = dot(tall, jnp.where(iota(shape, 0) & (count - 1) == source, 1.0, 0.0).astype(BF16))

    row, column = iota((wide, wide), 0) & (size - 1), iota((wide, wide), 1) & (size - 1)
    out_ref[...] = jnp.where(row == column, spread, 0.0).astype(BF16)


def stacked_slots(ins):
    if ins[0].shape[0] % 16 == 0:
        return jnp.concatenate([part[...] for part in ins], axis=0)
    return jnp.concatenate([part[...].astype(F32) for part in ins], axis=0).astype(BF16)


def spread_slots(outs, value):
    size = outs[0].shape[0]
    for slot, out in enumerate(outs):
        out[...] = value[slot * size : (slot + 1) * size].astype(BF16)


def joined(ins, wide_ref):
    for slot, part in enumerate(ins):
        wide_ref[rows_of(slot, part.shape[0]), :] = part[...].astype(wide_ref.dtype)
    return wide_ref[...]


def mix_kernel(count, transposed, m_ref, *refs):
    ins, outs = refs[:count], refs[count:]
    over = ((0,), (0,)) if transposed else ((1,), (0,))
    spread_slots(outs, dot(m_ref[...], stacked_slots(ins), over))


def back_kernel(count, w_gate_ref, factor_ref, *refs):
    mixed, (out_ref, wide_ref) = refs[:count], refs[count:]
    gate_grad = (factor_ref[...] * joined(mixed, wide_ref).astype(F32)).astype(BF16)
    out_ref[...] = dot(gate_grad, w_gate_ref[...], ((1,), (1,)))


def finish(j, back, folded, grads, outs, x_ref, gain_ref, w_value_ref, r_ref, e_ref, sum_ref):
    at = columns(j, w_value_ref.shape[1])
    value_grad = dot(r_ref[...], folded.astype(BF16), ((0,), (0,))).astype(BF16)
    e = (back + dot(value_grad, w_value_ref[...], ((1,), (1,)))) * gain_ref[...]
    e_ref[:, at] = e
    part = jnp.sum(e * x_ref[:, at].astype(F32), axis=-1, keepdims=True)

    @pl.when(j == 0)
    def _():
        sum_ref[...] = part

    @pl.when(j > 0)
    def _():
        sum_ref[...] += part

    @pl.when(j == pl.num_programs(0) - 1)
    def _():
        x = x_ref[...].astype(F32)
        q = inverse_rms(x_ref)
        mean = sum_ref[...] / x.shape[1]
        result = pick_gradient(grads).astype(F32) + q * e_ref[...] - q * q * q * x * mean
        for out in outs:
            out[...] = result.astype(BF16)


def result_kernel(count, sources, x_ref, gain_ref, w_value_ref, r_ref, back_ref, *refs):
    folded, refs = refs[:count], refs[count:]
    grads, refs = refs[:sources], refs[sources:]
    outs, (wide_ref, e_ref, sum_ref) = refs[sources - 1 : -3], refs[-3:]
    finish(
        pl.program_id(0), back_ref[...], joined(folded, wide_ref), grads, outs,
        x_ref, gain_ref, w_value_ref, r_ref, e_ref, sum_ref,
    )


class Exchange:
    def __init__(self, parts):
        self.parts = list(parts)
        self.got = {0: parts[0]}

    def send(self, slots, after=()):
        for slot in slots:
            pairs = [(i, i ^ slot) for i in range(len(self.parts))]
            self.got[slot] = lax.ppermute(tied(self.parts[slot], after), "seq", pairs)
        return self

    def all(self):
        return [self.got[slot] for slot in range(len(self.parts))]


def tied(value, after):
    if not after:
        return value
    value, *ended = lax.optimization_barrier((value, *(where.got[slot] for where, slot in after)))
    for (where, slot), got in zip(after, ended):
        where.got[slot] = got
    return value


def local(
    saved_inputs, arrived_grad, loss_grad, norm_gain, w_gate, w_value, w_out, r_factor, l_factor
):
    count = lax.axis_size("seq")
    pipe = lax.axis_size("pipe")
    _, _, rows, width = saved_inputs.shape
    block = w_gate.shape[1]
    size = rows // count

    whole = pl.BlockSpec((rows, width), lambda j: (0, 0))
    whole3 = pl.BlockSpec((None, rows, width), lambda j: (0, 0, 0))
    cut = pl.BlockSpec((rows, block), lambda j: (0, j))
    cut3 = pl.BlockSpec((None, rows, block), lambda j: (0, 0, j))
    weight = pl.BlockSpec((None, block, block), lambda j: (0, 0, j))
    gain = pl.BlockSpec((1, block), lambda j: (0, j))
    square = pl.BlockSpec((None, rows, rows), lambda j: (0, 0, 0))
    small = pl.BlockSpec((None, size, count * count), lambda j: (0, 0, 0))
    slots = [pl.BlockSpec((size, block), lambda j: (0, j))] * count
    anywhere = pl.BlockSpec(memory_space=pl.ANY)
    x_at = [
        pl.BlockSpec((None, None, rows, width), lambda j: (0, 0, 0, 0)),
        pl.BlockSpec((None, None, rows, width), lambda j: (0, 1, 0, 0)),
    ]

    slot_shapes = [jax.ShapeDtypeStruct((size, width), BF16)] * count
    plain = jax.ShapeDtypeStruct((rows, width), BF16)
    exact = jax.ShapeDtypeStruct((rows, width), F32)
    output = jax.ShapeDtypeStruct(saved_inputs.shape, BF16)

    column = pltpu.VMEM((rows, 1), F32)
    wide = pltpu.VMEM((rows, block), F32)
    full = pltpu.VMEM((rows, width), F32)
    square_plain = pl.BlockSpec((rows, rows), lambda j: (0, 0))
    joining = pltpu.VMEM((rows, block), BF16 if size % 16 == 0 else F32)
    product = 2 * rows * width * block

    def call(name, kernel, cost, ins, outs, scratch, mebibytes=32, aliases=None, steps=None):
        return pl.pallas_call(
            kernel,
            grid=(steps or width // block,),
            in_specs=[spec for spec, _ in ins],
            out_specs=[spec for spec, _ in outs],
            out_shape=[shape for _, shape in outs],
            scratch_shapes=scratch,
            input_output_aliases=aliases or {},
            compiler_params=params(mebibytes),
            cost_estimate=pl.CostEstimate(
                flops=int(cost[0] * product),
                bytes_accessed=cost[1] * rows * width * 2,
                transcendentals=0,
            ),
            name=name,
        )(*(value for _, value in ins))

    gains = (gain, norm_gain)
    value_in, gate_in, out_in = (weight, w_value), (weight, w_gate), (weight, w_out)
    r_in = (square, r_factor)
    slots_out = [*zip(slots, slot_shapes)]
    every = range(1, count)

    def first(tick, mebibytes=32):
        return call(
            f"first_{tick}",
            functools.partial(first_kernel, count),
            (2, 4),
            [(x_at[tick], saved_inputs), gains, value_in, r_in],
            slots_out,
            [column, wide],
            mebibytes,
        )

    def grads(tick, incoming):
        *parts, factor = call(
            f"grads_{tick}",
            functools.partial(grad_kernel, count, len(incoming)),
            (2, 8),
            [(x_at[tick], saved_inputs), gains, gate_in, out_in, *incoming],
            [*slots_out, (cut, exact)],
            [column, wide],
        )
        return parts, factor

    def mix(name, parts, transposed):
        return call(
            name,
            functools.partial(mix_kernel, count, transposed),
            (1, 2),
            [(square_plain, matrix), *zip(slots, parts)],
            slots_out,
            [],
        )

    def back(tick, mixed, factor):
        return call(
            f"back_{tick}",
            functools.partial(back_kernel, count),
            (1, 6),
            [gate_in, (cut, factor), *zip(slots, mixed)],
            [(cut, exact)],
            [joining],
        )[0]

    def result(tick, gate_part, folded, incoming, stacked):
        ins = [(x_at[tick], saved_inputs), gains, value_in, r_in, (cut, gate_part)]
        ins += [*zip(slots, folded), *incoming]
        outs = [(x_at[tick], output)]
        aliases = {}
        if stacked is None:
            outs.append((whole, plain))
        else:
            ins.append((anywhere, stacked))
            aliases = {len(ins) - 1: 0}
        return call(
            f"result_{tick}",
            functools.partial(result_kernel, count, len(incoming)),
            (3, 8),
            ins,
            outs,
            [joining, full, column],
            aliases=aliases,
        )

    first_0 = Exchange(first(0, 60)).send(every)
    (matrix,) = call(
        "matrix",
        functools.partial(matrix_kernel, count),
        (0.3, 1),
        [(small, l_factor)],
        [(square_plain, jax.ShapeDtypeStruct((rows, rows), BF16))],
        [],
        steps=1,
    )
    parts, factor_0 = grads(0, [(cut3, arrived_grad)])
    grad_0 = Exchange(parts).send(every)
    mix_0 = Exchange(mix("mix_0", first_0.all(), False)).send(every)
    fold_0 = Exchange(mix("fold_0", grad_0.all(), True)).send(every)
    gate_0 = back(0, mix_0.all(), factor_0)
    first_1 = Exchange(first(1))
    gate_0, first_1.parts[0] = lax.optimization_barrier((gate_0, first_1.parts[0]))
    first_1.send(every)
    stacked, result_0 = result(0, gate_0, fold_0.all(), [(whole3, arrived_grad)], None)
    result_0 = tied(result_0, [(first_1, slot) for slot in every[: min(4, count // 2)]])
    passed = lax.ppermute(result_0, "pipe", [(s, s - 1) for s in range(1, pipe)])
    mix_1 = Exchange(mix("mix_1", first_1.all(), False)).send(every)
    parts, factor_1 = grads(1, [(cut, passed), (cut3, loss_grad)])
    grad_1 = Exchange(parts).send(every)
    fold_1 = Exchange(mix("fold_1", grad_1.all(), True)).send(every)
    gate_1 = back(1, mix_1.all(), factor_1)
    incoming = [(whole, passed), (whole3, loss_grad)]
    return result(1, gate_1, fold_1.all(), incoming, stacked)[0]


def solution(mesh):
    placed = (
        P("pipe", None, "seq", None),
        P("pipe", "seq", None),
        P(None, "seq", None),
        P("pipe", None),
        P("pipe", None, None),
        P("pipe", None, None),
        P("pipe", None, None),
        P("pipe", "seq", None),
        P("pipe", "seq", None),
    )
    return jax.shard_map(
        local, mesh=mesh, in_specs=placed, out_specs=P("pipe", None, "seq", None), check_vma=False
    )
```

```python
import functools

import jax
import jax.numpy as jnp
from jax import lax
from jax.experimental import pallas as pl
from jax.experimental.pallas import tpu as pltpu
from jax.sharding import PartitionSpec as P

TICKS = 2
EPSILON = 1e-05
F32 = jnp.float32
BF16 = jnp.bfloat16
def params(mebibytes=32):
    return pltpu.CompilerParams(
        dimension_semantics=("arbitrary",), vmem_limit_bytes=mebibytes * 1024 * 1024
    )


def dot(a, b, over=((1,), (0,))):
    return lax.dot_general(a, b, (over, ((), ())), preferred_element_type=F32)


def rows_of(slot, size):
    owner = lax.axis_index("seq") ^ slot
    return pl.ds(pl.multiple_of(owner * size, size), size)


def inverse_rms(x_ref):
    x = x_ref[...].astype(F32)
    return lax.rsqrt(jnp.mean(x * x, axis=-1, keepdims=True) + EPSILON)


def columns(j, width):
    return pl.ds(pl.multiple_of(j * width, 128), width)


def split(outs, wide_ref):
    for slot, out in enumerate(outs):
        out[...] = wide_ref[rows_of(slot, out.shape[0]), :].astype(BF16)


def normed_block(j, x_ref, gain_ref, q_ref, width):
    @pl.when(j == 0)
    def _():
        q_ref[...] = inverse_rms(x_ref)

    x = x_ref[:, columns(j, width)].astype(F32)
    return (x * q_ref[...] * gain_ref[...]).astype(BF16)


def first_of(normed, w_ref, r_ref):
    return dot(r_ref[...], dot(normed, w_ref[...]).astype(BF16))


def grads_of(normed, grad, w_gate_ref, w_out_ref, factor_ref):
    gate = dot(normed, w_gate_ref[...])
    inner = dot(grad, w_out_ref[...], ((1,), (1,)))
    sigmoid = jax.nn.sigmoid(gate)
    factor_ref[...] = inner * sigmoid * (1.0 + gate * (1.0 - sigmoid))
    return inner * gate * sigmoid


def first_kernel(count, x_ref, gain_ref, w_ref, r_ref, *refs):
    outs, (q_ref, wide_ref) = refs[:count], refs[count:]
    normed = normed_block(pl.program_id(0), x_ref, gain_ref, q_ref, w_ref.shape[1])
    wide_ref[...] = first_of(normed, w_ref, r_ref)
    split(outs, wide_ref)


def pick_gradient(refs):
    if len(refs) == 1:
        return refs[0][...]
    last = lax.axis_index("pipe") == lax.axis_size("pipe") - 1
    return jnp.where(last, refs[1][...], refs[0][...])


def grad_kernel(count, sources, x_ref, gain_ref, w_gate_ref, w_out_ref, *refs):
    grads, refs = refs[:sources], refs[sources:]
    outs, (factor_ref, q_ref, wide_ref) = refs[:count], refs[count:]
    normed = normed_block(pl.program_id(0), x_ref, gain_ref, q_ref, w_gate_ref.shape[1])
    wide_ref[...] = grads_of(normed, pick_gradient(grads), w_gate_ref, w_out_ref, factor_ref)
    split(outs, wide_ref)


def matrix_kernel(count, l_ref, out_ref):
    size = l_ref.shape[0]
    wide = count * size
    bits = count.bit_length() - 1
    me = lax.axis_index("seq")
    iota = functools.partial(lax.broadcasted_iota, jnp.int32)

    shape = (count, size, count * count)
    tall = jnp.broadcast_to(l_ref[...].astype(F32)[None], shape)
    tall = jnp.where(iota(shape, 2) >> bits == iota(shape, 0) ^ me, tall, 0.0)
    tall = tall.reshape(wide, count * count).astype(BF16)

    shape = (count * count, wide)
    source = (iota(shape, 1) >> (size.bit_length() - 1)) ^ me
    spread = dot(tall, jnp.where(iota(shape, 0) & (count - 1) == source, 1.0, 0.0).astype(BF16))

    row, column = iota((wide, wide), 0) & (size - 1), iota((wide, wide), 1) & (size - 1)
    out_ref[...] = jnp.where(row == column, spread, 0.0).astype(BF16)


def stacked_slots(ins):
    if ins[0].shape[0] % 16 == 0:
        return jnp.concatenate([part[...] for part in ins], axis=0)
    return jnp.concatenate([part[...].astype(F32) for part in ins], axis=0).astype(BF16)


def spread_slots(outs, value):
    size = outs[0].shape[0]
    for slot, out in enumerate(outs):
        out[...] = value[slot * size : (slot + 1) * size].astype(BF16)


def joined(ins, wide_ref):
    for slot, part in enumerate(ins):
        wide_ref[rows_of(slot, part.shape[0]), :] = part[...].astype(wide_ref.dtype)
    return wide_ref[...]


def mix_kernel(count, transposed, m_ref, *refs):
    ins, outs = refs[:count], refs[count:]
    over = ((0,), (0,)) if transposed else ((1,), (0,))
    spread_slots(outs, dot(m_ref[...], stacked_slots(ins), over))


def back_kernel(count, w_gate_ref, factor_ref, *refs):
    mixed, (out_ref, wide_ref) = refs[:count], refs[count:]
    gate_grad = (factor_ref[...] * joined(mixed, wide_ref).astype(F32)).astype(BF16)
    out_ref[...] = dot(gate_grad, w_gate_ref[...], ((1,), (1,)))


def finish(j, back, folded, grads, outs, x_ref, gain_ref, w_value_ref, r_ref, e_ref, sum_ref):
    at = columns(j, w_value_ref.shape[1])
    value_grad = dot(r_ref[...], folded.astype(BF16), ((0,), (0,))).astype(BF16)
    e = (back + dot(value_grad, w_value_ref[...], ((1,), (1,)))) * gain_ref[...]
    e_ref[:, at] = e
    part = jnp.sum(e * x_ref[:, at].astype(F32), axis=-1, keepdims=True)

    @pl.when(j == 0)
    def _():
        sum_ref[...] = part

    @pl.when(j > 0)
    def _():
        sum_ref[...] += part

    @pl.when(j == pl.num_programs(0) - 1)
    def _():
        x = x_ref[...].astype(F32)
        q = inverse_rms(x_ref)
        mean = sum_ref[...] / x.shape[1]
        result = pick_gradient(grads).astype(F32) + q * e_ref[...] - q * q * q * x * mean
        for out in outs:
            out[...] = result.astype(BF16)


def result_kernel(count, sources, x_ref, gain_ref, w_value_ref, r_ref, back_ref, *refs):
    folded, refs = refs[:count], refs[count:]
    grads, refs = refs[:sources], refs[sources:]
    outs, (wide_ref, e_ref, sum_ref) = refs[sources - 1 : -3], refs[-3:]
    finish(
        pl.program_id(0), back_ref[...], joined(folded, wide_ref), grads, outs,
        x_ref, gain_ref, w_value_ref, r_ref, e_ref, sum_ref,
    )


WINDOW = 5


class Exchange:
    def __init__(self, parts):
        self.parts = list(parts)
        self.got = {0: parts[0]}

    def send(self, slots, lane=None):
        for slot in slots:
            pairs = [(i, i ^ slot) for i in range(len(self.parts))]
            after = lane[-WINDOW:][:1] if lane is not None and len(lane) >= WINDOW else []
            self.got[slot] = lax.ppermute(tied(self.parts[slot], after), "seq", pairs)
            if lane is not None:
                lane.append((self, slot))
        return self

    def all(self):
        return [self.got[slot] for slot in range(len(self.parts))]


def tied(value, after):
    if not after:
        return value
    value, *ended = lax.optimization_barrier((value, *(where.got[slot] for where, slot in after)))
    for (where, slot), got in zip(after, ended):
        where.got[slot] = got
    return value


def local(
    saved_inputs, arrived_grad, loss_grad, norm_gain, w_gate, w_value, w_out, r_factor, l_factor
):
    count = lax.axis_size("seq")
    pipe = lax.axis_size("pipe")
    _, _, rows, width = saved_inputs.shape
    block = w_gate.shape[1]
    size = rows // count

    whole = pl.BlockSpec((rows, width), lambda j: (0, 0))
    whole3 = pl.BlockSpec((None, rows, width), lambda j: (0, 0, 0))
    cut = pl.BlockSpec((rows, block), lambda j: (0, j))
    cut3 = pl.BlockSpec((None, rows, block), lambda j: (0, 0, j))
    weight = pl.BlockSpec((None, block, block), lambda j: (0, 0, j))
    gain = pl.BlockSpec((1, block), lambda j: (0, j))
    square = pl.BlockSpec((None, rows, rows), lambda j: (0, 0, 0))
    small = pl.BlockSpec((None, size, count * count), lambda j: (0, 0, 0))
    slots = [pl.BlockSpec((size, block), lambda j: (0, j))] * count
    anywhere = pl.BlockSpec(memory_space=pl.ANY)
    x_at = [
        pl.BlockSpec((None, None, rows, width), lambda j: (0, 0, 0, 0)),
        pl.BlockSpec((None, None, rows, width), lambda j: (0, 1, 0, 0)),
    ]

    slot_shapes = [jax.ShapeDtypeStruct((size, width), BF16)] * count
    plain = jax.ShapeDtypeStruct((rows, width), BF16)
    exact = jax.ShapeDtypeStruct((rows, width), F32)
    output = jax.ShapeDtypeStruct(saved_inputs.shape, BF16)

    column = pltpu.VMEM((rows, 1), F32)
    wide = pltpu.VMEM((rows, block), F32)
    full = pltpu.VMEM((rows, width), F32)
    square_plain = pl.BlockSpec((rows, rows), lambda j: (0, 0))
    joining = pltpu.VMEM((rows, block), BF16 if size % 16 == 0 else F32)
    product = 2 * rows * width * block

    def call(name, kernel, cost, ins, outs, scratch, mebibytes=32, aliases=None, steps=None):
        return pl.pallas_call(
            kernel,
            grid=(steps or width // block,),
            in_specs=[spec for spec, _ in ins],
            out_specs=[spec for spec, _ in outs],
            out_shape=[shape for _, shape in outs],
            scratch_shapes=scratch,
            input_output_aliases=aliases or {},
            compiler_params=params(mebibytes),
            cost_estimate=pl.CostEstimate(
                flops=int(cost[0] * product),
                bytes_accessed=cost[1] * rows * width * 2,
                transcendentals=0,
            ),
            name=name,
        )(*(value for _, value in ins))

    gains = (gain, norm_gain)
    value_in, gate_in, out_in = (weight, w_value), (weight, w_gate), (weight, w_out)
    r_in = (square, r_factor)
    slots_out = [*zip(slots, slot_shapes)]
    every = range(1, count)

    def first(tick, mebibytes=32):
        return call(
            f"first_{tick}",
            functools.partial(first_kernel, count),
            (2, 4),
            [(x_at[tick], saved_inputs), gains, value_in, r_in],
            slots_out,
            [column, wide],
            mebibytes,
        )

    def grads(tick, incoming):
        *parts, factor = call(
            f"grads_{tick}",
            functools.partial(grad_kernel, count, len(incoming)),
            (2, 8),
            [(x_at[tick], saved_inputs), gains, gate_in, out_in, *incoming],
            [*slots_out, (cut, exact)],
            [column, wide],
        )
        return parts, factor

    def mix(name, parts, transposed):
        return call(
            name,
            functools.partial(mix_kernel, count, transposed),
            (1, 2),
            [(square_plain, matrix), *zip(slots, parts)],
            slots_out,
            [],
        )

    def back(tick, mixed, factor):
        return call(
            f"back_{tick}",
            functools.partial(back_kernel, count),
            (1, 6),
            [gate_in, (cut, factor), *zip(slots, mixed)],
            [(cut, exact)],
            [joining],
        )[0]

    def result(tick, gate_part, folded, incoming, stacked):
        ins = [(x_at[tick], saved_inputs), gains, value_in, r_in, (cut, gate_part)]
        ins += [*zip(slots, folded), *incoming]
        outs = [(x_at[tick], output)]
        aliases = {}
        if stacked is None:
            outs.append((whole, plain))
        else:
            ins.append((anywhere, stacked))
            aliases = {len(ins) - 1: 0}
        return call(
            f"result_{tick}",
            functools.partial(result_kernel, count, len(incoming)),
            (3, 8),
            ins,
            outs,
            [joining, full, column],
            aliases=aliases,
        )

    half = count // 2
    turns = [slot for pair in zip(range(half, count), [*range(1, half), 0]) for slot in pair]
    turns.remove(0)
    lane = []
    first_0 = Exchange(first(0, 60)).send(turns, lane)
    (matrix,) = call(
        "matrix",
        functools.partial(matrix_kernel, count),
        (0.3, 1),
        [(small, l_factor)],
        [(square_plain, jax.ShapeDtypeStruct((rows, rows), BF16))],
        [],
        steps=1,
    )
    parts, factor_0 = grads(0, [(cut3, arrived_grad)])
    grad_0 = Exchange(parts).send(turns, lane)
    mix_0 = Exchange(mix("mix_0", first_0.all(), False)).send(turns, lane)
    fold_0 = Exchange(mix("fold_0", grad_0.all(), True)).send(turns, lane)
    gate_0 = back(0, mix_0.all(), factor_0)
    first_1 = Exchange(first(1))
    gate_0, first_1.parts[0] = lax.optimization_barrier((gate_0, first_1.parts[0]))
    first_1.send(turns, lane)
    gate_0 = tied(gate_0, [(first_1, slot) for slot in turns[:1]])
    stacked, result_0 = result(0, gate_0, fold_0.all(), [(whole3, arrived_grad)], None)
    result_0 = tied(result_0, [(first_1, slot) for slot in turns[1:-1]])
    passed = lax.ppermute(result_0, "pipe", [(s, s - 1) for s in range(1, pipe)])
    mix_1 = Exchange(mix("mix_1", first_1.all(), False)).send(range(half, count)).send(range(1, half))
    passed, mix_1.parts[0] = lax.optimization_barrier((passed, mix_1.parts[0]))
    parts, factor_1 = grads(1, [(cut, passed), (cut3, loss_grad)])
    for slot, other in zip([count - 1, half - 1, half - 2], range(half, count)):
        parts[slot] = tied(parts[slot], [(mix_1, other)])
    grad_1 = Exchange(parts).send(every)
    fold_1 = Exchange(mix("fold_1", grad_1.all(), True)).send(every)
    gate_1 = back(1, mix_1.all(), factor_1)
    incoming = [(whole, passed), (whole3, loss_grad)]
    return result(1, gate_1, fold_1.all(), incoming, stacked)[0]


def solution(mesh):
    placed = (
        P("pipe", None, "seq", None),
        P("pipe", "seq", None),
        P(None, "seq", None),
        P("pipe", None),
        P("pipe", None, None),
        P("pipe", None, None),
        P("pipe", None, None),
        P("pipe", "seq", None),
        P("pipe", "seq", None),
    )
    return jax.shard_map(
        local, mesh=mesh, in_specs=placed, out_specs=P("pipe", None, "seq", None), check_vma=False
    )
```

```python
import functools

import jax
import jax.numpy as jnp
from jax import lax
from jax.experimental import pallas as pl
from jax.experimental.pallas import tpu as pltpu
from jax.sharding import PartitionSpec as P

TICKS = 2
EPSILON = 1e-05
F32 = jnp.float32
BF16 = jnp.bfloat16
def params(mebibytes=32):
    return pltpu.CompilerParams(
        dimension_semantics=("arbitrary",), vmem_limit_bytes=mebibytes * 1024 * 1024
    )


def dot(a, b, over=((1,), (0,))):
    return lax.dot_general(a, b, (over, ((), ())), preferred_element_type=F32)


PAIRINGS = (
    ((0, 7), (1, 6), (2, 5), (3, 4)),
    ((0, 1), (2, 4), (3, 7), (5, 6)),
    ((0, 3), (1, 5), (2, 6), (4, 7)),
    ((0, 4), (1, 2), (3, 5), (6, 7)),
    ((0, 2), (1, 7), (3, 6), (4, 5)),
    ((0, 6), (1, 4), (2, 3), (5, 7)),
    ((0, 5), (1, 3), (2, 7), (4, 6)),
)


def partners(slot, count):
    if slot == 0 or count != 8:
        return [device ^ slot for device in range(count)]
    both = dict(PAIRINGS[slot - 1])
    both.update({b: a for a, b in both.items()})
    return [both[device] for device in range(count)]


def owner_of(slot, count):
    me = lax.axis_index("seq")
    if slot == 0 or count != 8:
        return me ^ slot
    packed = sum(partner << (3 * device) for device, partner in enumerate(partners(slot, count)))
    return (packed >> (3 * me)) & 7


def owners_of(slots, count):
    if count != 8:
        return slots ^ lax.axis_index("seq")
    owners = jnp.zeros_like(slots)
    for slot in range(count):
        owners = jnp.where(slots == slot, owner_of(slot, count), owners)
    return owners


def rows_of(slot, size):
    owner = owner_of(slot, lax.axis_size("seq"))
    return pl.ds(pl.multiple_of(owner * size, size), size)


def inverse_rms(x_ref):
    x = x_ref[...].astype(F32)
    return lax.rsqrt(jnp.mean(x * x, axis=-1, keepdims=True) + EPSILON)


def columns(j, width):
    return pl.ds(pl.multiple_of(j * width, 128), width)


def split(outs, wide_ref):
    for slot, out in enumerate(outs):
        out[...] = wide_ref[rows_of(slot, out.shape[0]), :].astype(BF16)


def normed_block(j, x_ref, gain_ref, q_ref, width):
    @pl.when(j == 0)
    def _():
        q_ref[...] = inverse_rms(x_ref)

    x = x_ref[:, columns(j, width)].astype(F32)
    return (x * q_ref[...] * gain_ref[...]).astype(BF16)


def first_of(normed, w_ref, r_ref):
    return dot(r_ref[...], dot(normed, w_ref[...]).astype(BF16))


def grads_of(normed, grad, w_gate_ref, w_out_ref, factor_ref):
    gate = dot(normed, w_gate_ref[...])
    inner = dot(grad, w_out_ref[...], ((1,), (1,)))
    sigmoid = jax.nn.sigmoid(gate)
    factor_ref[...] = inner * sigmoid * (1.0 + gate * (1.0 - sigmoid))
    return inner * gate * sigmoid


def first_kernel(count, x_ref, gain_ref, w_ref, r_ref, *refs):
    outs, (q_ref, wide_ref) = refs[:count], refs[count:]
    normed = normed_block(pl.program_id(0), x_ref, gain_ref, q_ref, w_ref.shape[1])
    wide_ref[...] = first_of(normed, w_ref, r_ref)
    split(outs, wide_ref)


def pick_gradient(refs):
    if len(refs) == 1:
        return refs[0][...]
    last = lax.axis_index("pipe") == lax.axis_size("pipe") - 1
    return jnp.where(last, refs[1][...], refs[0][...])


def grad_kernel(count, sources, x_ref, gain_ref, w_gate_ref, w_out_ref, *refs):
    grads, refs = refs[:sources], refs[sources:]
    outs, (factor_ref, q_ref, wide_ref) = refs[:count], refs[count:]
    normed = normed_block(pl.program_id(0), x_ref, gain_ref, q_ref, w_gate_ref.shape[1])
    wide_ref[...] = grads_of(normed, pick_gradient(grads), w_gate_ref, w_out_ref, factor_ref)
    split(outs, wide_ref)


def matrix_kernel(count, l_ref, out_ref):
    size = l_ref.shape[0]
    wide = count * size
    bits = count.bit_length() - 1
    iota = functools.partial(lax.broadcasted_iota, jnp.int32)

    shape = (count, size, count * count)
    tall = jnp.broadcast_to(l_ref[...].astype(F32)[None], shape)
    tall = jnp.where(iota(shape, 2) >> bits == owners_of(iota(shape, 0), count), tall, 0.0)
    tall = tall.reshape(wide, count * count).astype(BF16)

    shape = (count * count, wide)
    source = owners_of(iota(shape, 1) >> (size.bit_length() - 1), count)
    spread = dot(tall, jnp.where(iota(shape, 0) & (count - 1) == source, 1.0, 0.0).astype(BF16))

    row, column = iota((wide, wide), 0) & (size - 1), iota((wide, wide), 1) & (size - 1)
    out_ref[...] = jnp.where(row == column, spread, 0.0).astype(BF16)


def stacked_slots(ins):
    if ins[0].shape[0] % 16 == 0:
        return jnp.concatenate([part[...] for part in ins], axis=0)
    return jnp.concatenate([part[...].astype(F32) for part in ins], axis=0).astype(BF16)


def spread_slots(outs, value):
    size = outs[0].shape[0]
    for slot, out in enumerate(outs):
        out[...] = value[slot * size : (slot + 1) * size].astype(BF16)


def joined(ins, wide_ref):
    for slot, part in enumerate(ins):
        wide_ref[rows_of(slot, part.shape[0]), :] = part[...].astype(wide_ref.dtype)
    return wide_ref[...]


def mix_kernel(count, transposed, m_ref, *refs):
    ins, outs = refs[:count], refs[count:]
    over = ((0,), (0,)) if transposed else ((1,), (0,))
    spread_slots(outs, dot(m_ref[...], stacked_slots(ins), over))


def back_kernel(count, w_gate_ref, factor_ref, *refs):
    mixed, (out_ref, wide_ref) = refs[:count], refs[count:]
    gate_grad = (factor_ref[...] * joined(mixed, wide_ref).astype(F32)).astype(BF16)
    out_ref[...] = dot(gate_grad, w_gate_ref[...], ((1,), (1,)))


def finish(j, back, folded, grads, outs, x_ref, gain_ref, w_value_ref, r_ref, e_ref, sum_ref):
    at = columns(j, w_value_ref.shape[1])
    value_grad = dot(r_ref[...], folded.astype(BF16), ((0,), (0,))).astype(BF16)
    e = (back + dot(value_grad, w_value_ref[...], ((1,), (1,)))) * gain_ref[...]
    e_ref[:, at] = e
    part = jnp.sum(e * x_ref[:, at].astype(F32), axis=-1, keepdims=True)

    @pl.when(j == 0)
    def _():
        sum_ref[...] = part

    @pl.when(j > 0)
    def _():
        sum_ref[...] += part

    @pl.when(j == pl.num_programs(0) - 1)
    def _():
        x = x_ref[...].astype(F32)
        q = inverse_rms(x_ref)
        mean = sum_ref[...] / x.shape[1]
        result = pick_gradient(grads).astype(F32) + q * e_ref[...] - q * q * q * x * mean
        for out in outs:
            out[...] = result.astype(BF16)


def result_kernel(count, sources, x_ref, gain_ref, w_value_ref, r_ref, back_ref, *refs):
    folded, refs = refs[:count], refs[count:]
    grads, refs = refs[:sources], refs[sources:]
    outs, (wide_ref, e_ref, sum_ref) = refs[sources - 1 : -3], refs[-3:]
    finish(
        pl.program_id(0), back_ref[...], joined(folded, wide_ref), grads, outs,
        x_ref, gain_ref, w_value_ref, r_ref, e_ref, sum_ref,
    )


class Exchange:
    def __init__(self, parts):
        self.parts = list(parts)
        self.got = {0: parts[0]}

    def send(self, slots, after=()):
        for slot in slots:
            pairs = [*enumerate(partners(slot, len(self.parts)))]
            self.got[slot] = lax.ppermute(tied(self.parts[slot], after), "seq", pairs)
        return self

    def all(self):
        return [self.got[slot] for slot in range(len(self.parts))]


def tied(value, after):
    if not after:
        return value
    value, *ended = lax.optimization_barrier((value, *(where.got[slot] for where, slot in after)))
    for (where, slot), got in zip(after, ended):
        where.got[slot] = got
    return value


def local(
    saved_inputs, arrived_grad, loss_grad, norm_gain, w_gate, w_value, w_out, r_factor, l_factor
):
    count = lax.axis_size("seq")
    pipe = lax.axis_size("pipe")
    _, _, rows, width = saved_inputs.shape
    block = w_gate.shape[1]
    size = rows // count

    whole = pl.BlockSpec((rows, width), lambda j: (0, 0))
    whole3 = pl.BlockSpec((None, rows, width), lambda j: (0, 0, 0))
    cut = pl.BlockSpec((rows, block), lambda j: (0, j))
    cut3 = pl.BlockSpec((None, rows, block), lambda j: (0, 0, j))
    weight = pl.BlockSpec((None, block, block), lambda j: (0, 0, j))
    gain = pl.BlockSpec((1, block), lambda j: (0, j))
    square = pl.BlockSpec((None, rows, rows), lambda j: (0, 0, 0))
    small = pl.BlockSpec((None, size, count * count), lambda j: (0, 0, 0))
    slots = [pl.BlockSpec((size, block), lambda j: (0, j))] * count
    anywhere = pl.BlockSpec(memory_space=pl.ANY)
    x_at = [
        pl.BlockSpec((None, None, rows, width), lambda j: (0, 0, 0, 0)),
        pl.BlockSpec((None, None, rows, width), lambda j: (0, 1, 0, 0)),
    ]

    slot_shapes = [jax.ShapeDtypeStruct((size, width), BF16)] * count
    plain = jax.ShapeDtypeStruct((rows, width), BF16)
    exact = jax.ShapeDtypeStruct((rows, width), F32)
    output = jax.ShapeDtypeStruct(saved_inputs.shape, BF16)

    column = pltpu.VMEM((rows, 1), F32)
    wide = pltpu.VMEM((rows, block), F32)
    full = pltpu.VMEM((rows, width), F32)
    square_plain = pl.BlockSpec((rows, rows), lambda j: (0, 0))
    joining = pltpu.VMEM((rows, block), BF16 if size % 16 == 0 else F32)
    product = 2 * rows * width * block

    def call(name, kernel, cost, ins, outs, scratch, mebibytes=32, aliases=None, steps=None):
        return pl.pallas_call(
            kernel,
            grid=(steps or width // block,),
            in_specs=[spec for spec, _ in ins],
            out_specs=[spec for spec, _ in outs],
            out_shape=[shape for _, shape in outs],
            scratch_shapes=scratch,
            input_output_aliases=aliases or {},
            compiler_params=params(mebibytes),
            cost_estimate=pl.CostEstimate(
                flops=int(cost[0] * product),
                bytes_accessed=cost[1] * rows * width * 2,
                transcendentals=0,
            ),
            name=name,
        )(*(value for _, value in ins))

    gains = (gain, norm_gain)
    value_in, gate_in, out_in = (weight, w_value), (weight, w_gate), (weight, w_out)
    r_in = (square, r_factor)
    slots_out = [*zip(slots, slot_shapes)]
    every = range(1, count)

    def first(tick, mebibytes=32):
        return call(
            f"first_{tick}",
            functools.partial(first_kernel, count),
            (2, 4),
            [(x_at[tick], saved_inputs), gains, value_in, r_in],
            slots_out,
            [column, wide],
            mebibytes,
        )

    def grads(tick, incoming):
        *parts, factor = call(
            f"grads_{tick}",
            functools.partial(grad_kernel, count, len(incoming)),
            (2, 8),
            [(x_at[tick], saved_inputs), gains, gate_in, out_in, *incoming],
            [*slots_out, (cut, exact)],
            [column, wide],
        )
        return parts, factor

    def mix(name, parts, transposed):
        return call(
            name,
            functools.partial(mix_kernel, count, transposed),
            (1, 2),
            [(square_plain, matrix), *zip(slots, parts)],
            slots_out,
            [],
        )

    def back(tick, mixed, factor):
        return call(
            f"back_{tick}",
            functools.partial(back_kernel, count),
            (1, 6),
            [gate_in, (cut, factor), *zip(slots, mixed)],
            [(cut, exact)],
            [joining],
        )[0]

    def result(tick, gate_part, folded, incoming, stacked):
        ins = [(x_at[tick], saved_inputs), gains, value_in, r_in, (cut, gate_part)]
        ins += [*zip(slots, folded), *incoming]
        outs = [(x_at[tick], output)]
        aliases = {}
        if stacked is None:
            outs.append((whole, plain))
        else:
            ins.append((anywhere, stacked))
            aliases = {len(ins) - 1: 0}
        return call(
            f"result_{tick}",
            functools.partial(result_kernel, count, len(incoming)),
            (3, 8),
            ins,
            outs,
            [joining, full, column],
            aliases=aliases,
        )

    first_0 = Exchange(first(0, 60)).send(every)
    (matrix,) = call(
        "matrix",
        functools.partial(matrix_kernel, count),
        (0.3, 1),
        [(small, l_factor)],
        [(square_plain, jax.ShapeDtypeStruct((rows, rows), BF16))],
        [],
        steps=1,
    )
    parts, factor_0 = grads(0, [(cut3, arrived_grad)])
    grad_0 = Exchange(parts).send(every)
    mix_0 = Exchange(mix("mix_0", first_0.all(), False)).send(every)
    fold_0 = Exchange(mix("fold_0", grad_0.all(), True)).send(every)
    gate_0 = back(0, mix_0.all(), factor_0)
    first_1 = Exchange(first(1))
    gate_0, first_1.parts[0] = lax.optimization_barrier((gate_0, first_1.parts[0]))
    first_1.send(every)
    stacked, result_0 = result(0, gate_0, fold_0.all(), [(whole3, arrived_grad)], None)
    result_0 = tied(result_0, [(first_1, slot) for slot in every[: min(3, count // 2)]])
    passed = lax.ppermute(result_0, "pipe", [(s, s - 1) for s in range(1, pipe)])
    mix_1 = Exchange(mix("mix_1", first_1.all(), False)).send(every)
    parts, factor_1 = grads(1, [(cut, passed), (cut3, loss_grad)])
    grad_1 = Exchange(parts).send(every)
    fold_1 = Exchange(mix("fold_1", grad_1.all(), True)).send(every)
    gate_1 = back(1, mix_1.all(), factor_1)
    incoming = [(whole, passed), (whole3, loss_grad)]
    return result(1, gate_1, fold_1.all(), incoming, stacked)[0]


def solution(mesh):
    placed = (
        P("pipe", None, "seq", None),
        P("pipe", "seq", None),
        P(None, "seq", None),
        P("pipe", None),
        P("pipe", None, None),
        P("pipe", None, None),
        P("pipe", None, None),
        P("pipe", "seq", None),
        P("pipe", "seq", None),
    )
    return jax.shard_map(
        local, mesh=mesh, in_specs=placed, out_specs=P("pipe", None, "seq", None), check_vma=False
    )
```

```python
import functools

import jax
import jax.numpy as jnp
from jax import lax
from jax.experimental import pallas as pl
from jax.experimental.pallas import tpu as pltpu
from jax.sharding import PartitionSpec as P

TICKS = 2
EPSILON = 1e-05
F32 = jnp.float32
BF16 = jnp.bfloat16
def params(mebibytes=32):
    return pltpu.CompilerParams(
        dimension_semantics=("arbitrary",), vmem_limit_bytes=mebibytes * 1024 * 1024
    )


def dot(a, b, over=((1,), (0,))):
    return lax.dot_general(a, b, (over, ((), ())), preferred_element_type=F32)


PAIRINGS = (
    ((0, 7), (1, 6), (2, 5), (3, 4)),
    ((0, 1), (2, 4), (3, 7), (5, 6)),
    ((0, 3), (1, 5), (2, 6), (4, 7)),
    ((0, 4), (1, 2), (3, 5), (6, 7)),
    ((0, 2), (1, 7), (3, 6), (4, 5)),
    ((0, 6), (1, 4), (2, 3), (5, 7)),
    ((0, 5), (1, 3), (2, 7), (4, 6)),
)


def partners(slot, count):
    if slot == 0 or count != 8:
        return [device ^ slot for device in range(count)]
    both = dict(PAIRINGS[slot - 1])
    both.update({b: a for a, b in both.items()})
    return [both[device] for device in range(count)]


def owner_of(slot, count):
    me = lax.axis_index("seq")
    if slot == 0 or count != 8:
        return me ^ slot
    packed = sum(partner << (3 * device) for device, partner in enumerate(partners(slot, count)))
    return (packed >> (3 * me)) & 7


def owners_of(slots, count):
    if count != 8:
        return slots ^ lax.axis_index("seq")
    owners = jnp.zeros_like(slots)
    for slot in range(count):
        owners = jnp.where(slots == slot, owner_of(slot, count), owners)
    return owners


def rows_of(slot, size):
    owner = owner_of(slot, lax.axis_size("seq"))
    return pl.ds(pl.multiple_of(owner * size, size), size)


def inverse_rms(x_ref):
    x = x_ref[...].astype(F32)
    return lax.rsqrt(jnp.mean(x * x, axis=-1, keepdims=True) + EPSILON)


def columns(j, width):
    return pl.ds(pl.multiple_of(j * width, 128), width)


def split(outs, wide_ref):
    for slot, out in enumerate(outs):
        out[...] = wide_ref[rows_of(slot, out.shape[0]), :].astype(BF16)


def normed_block(j, x_ref, gain_ref, q_ref, width):
    @pl.when(j == 0)
    def _():
        q_ref[...] = inverse_rms(x_ref)

    x = x_ref[:, columns(j, width)].astype(F32)
    return (x * q_ref[...] * gain_ref[...]).astype(BF16)


def first_of(normed, w_ref, r_ref):
    return dot(r_ref[...], dot(normed, w_ref[...]).astype(BF16))


def grads_of(normed, grad, w_gate_ref, w_out_ref, factor_ref):
    gate = dot(normed, w_gate_ref[...])
    inner = dot(grad, w_out_ref[...], ((1,), (1,)))
    sigmoid = jax.nn.sigmoid(gate)
    factor_ref[...] = inner * sigmoid * (1.0 + gate * (1.0 - sigmoid))
    return inner * gate * sigmoid


def first_kernel(count, x_ref, gain_ref, w_ref, r_ref, *refs):
    outs, (q_ref, wide_ref) = refs[:count], refs[count:]
    normed = normed_block(pl.program_id(0), x_ref, gain_ref, q_ref, w_ref.shape[1])
    wide_ref[...] = first_of(normed, w_ref, r_ref)
    split(outs, wide_ref)


def both_kernel(
    count, x_ref, gain_ref, w_value_ref, r_ref, w_gate_ref, w_out_ref, grad_ref, *refs
):
    outs, (factor_ref, q_ref, wide_ref) = refs[:count], refs[count:]
    normed = normed_block(pl.program_id(0), x_ref, gain_ref, q_ref, w_gate_ref.shape[1])
    wide_ref[...] = grads_of(normed, grad_ref[...], w_gate_ref, w_out_ref, factor_ref)
    split([out.at[1] for out in outs], wide_ref)
    wide_ref[...] = first_of(normed, w_value_ref, r_ref)
    split([out.at[0] for out in outs], wide_ref)


def pick_gradient(refs):
    if len(refs) == 1:
        return refs[0][...]
    last = lax.axis_index("pipe") == lax.axis_size("pipe") - 1
    return jnp.where(last, refs[1][...], refs[0][...])


def matrix_kernel(count, l_ref, out_ref):
    size = l_ref.shape[0]
    wide = count * size
    bits = count.bit_length() - 1
    iota = functools.partial(lax.broadcasted_iota, jnp.int32)

    shape = (count, size, count * count)
    tall = jnp.broadcast_to(l_ref[...].astype(F32)[None], shape)
    tall = jnp.where(iota(shape, 2) >> bits == owners_of(iota(shape, 0), count), tall, 0.0)
    tall = tall.reshape(wide, count * count).astype(BF16)

    shape = (count * count, wide)
    source = owners_of(iota(shape, 1) >> (size.bit_length() - 1), count)
    spread = dot(tall, jnp.where(iota(shape, 0) & (count - 1) == source, 1.0, 0.0).astype(BF16))

    row, column = iota((wide, wide), 0) & (size - 1), iota((wide, wide), 1) & (size - 1)
    out_ref[...] = jnp.where(row == column, spread, 0.0).astype(BF16)


def stacked_slots(ins):
    if ins[0].shape[0] % 16 == 0:
        return jnp.concatenate([part[...] for part in ins], axis=0)
    return jnp.concatenate([part[...].astype(F32) for part in ins], axis=0).astype(BF16)


def spread_slots(outs, value):
    size = outs[0].shape[0]
    for slot, out in enumerate(outs):
        out[...] = value[slot * size : (slot + 1) * size].astype(BF16)


def joined(ins, wide_ref):
    for slot, part in enumerate(ins):
        wide_ref[rows_of(slot, part.shape[0]), :] = part[...].astype(wide_ref.dtype)
    return wide_ref[...]


def fold_kernel(count, m_ref, *refs):
    ins, outs = refs[:count], refs[count:]
    spread_slots(outs, dot(m_ref[...], stacked_slots(ins), ((0,), (0,))))


def mix_fold_kernel(count, m_ref, *refs):
    ins, outs = refs[:count], refs[count:]
    for half, over in ((0, ((1,), (0,))), (1, ((0,), (0,)))):
        value = stacked_slots([part.at[half] for part in ins])
        spread_slots([out.at[half] for out in outs], dot(m_ref[...], value, over))


def mix_grads_kernel(
    count, x_ref, gain_ref, w_gate_ref, w_out_ref, passed_ref, loss_ref, m_ref, *refs
):
    ins, outs, (factor_ref, q_ref, wide_ref) = refs[:count], refs[count : 2 * count], refs[2 * count :]
    normed = normed_block(pl.program_id(0), x_ref, gain_ref, q_ref, w_gate_ref.shape[1])
    grad = pick_gradient((passed_ref, loss_ref))
    wide_ref[...] = grads_of(normed, grad, w_gate_ref, w_out_ref, factor_ref)
    split([out.at[1] for out in outs], wide_ref)
    spread_slots([out.at[0] for out in outs], dot(m_ref[...], stacked_slots(ins)))


def back_of(w_gate_ref, factor_ref, mixed):
    gate_grad = (factor_ref[...] * mixed.astype(F32)).astype(BF16)
    return dot(gate_grad, w_gate_ref[...], ((1,), (1,)))


def back_kernel(count, w_gate_ref, factor_ref, *refs):
    mixed, (out_ref, wide_ref) = refs[:count], refs[count:]
    out_ref[...] = back_of(w_gate_ref, factor_ref, joined(mixed, wide_ref))


def finish(j, back, folded, grads, outs, x_ref, gain_ref, w_value_ref, r_ref, e_ref, sum_ref):
    at = columns(j, w_value_ref.shape[1])
    value_grad = dot(r_ref[...], folded.astype(BF16), ((0,), (0,))).astype(BF16)
    e = (back + dot(value_grad, w_value_ref[...], ((1,), (1,)))) * gain_ref[...]
    e_ref[:, at] = e
    part = jnp.sum(e * x_ref[:, at].astype(F32), axis=-1, keepdims=True)

    @pl.when(j == 0)
    def _():
        sum_ref[...] = part

    @pl.when(j > 0)
    def _():
        sum_ref[...] += part

    @pl.when(j == pl.num_programs(0) - 1)
    def _():
        x = x_ref[...].astype(F32)
        q = inverse_rms(x_ref)
        mean = sum_ref[...] / x.shape[1]
        result = pick_gradient(grads).astype(F32) + q * e_ref[...] - q * q * q * x * mean
        for out in outs:
            out[...] = result.astype(BF16)


def result_both_kernel(
    count, x_ref, gain_ref, w_value_ref, r_ref, w_gate_ref, factor_ref, grad_ref, *refs
):
    ins, (stacked_ref, out_ref, wide_ref, e_ref, sum_ref) = refs[:count], refs[count:]
    back = back_of(w_gate_ref, factor_ref, joined([part.at[0] for part in ins], wide_ref))
    folded = joined([part.at[1] for part in ins], wide_ref)
    finish(
        pl.program_id(0), back, folded, (grad_ref,), (stacked_ref, out_ref),
        x_ref, gain_ref, w_value_ref, r_ref, e_ref, sum_ref,
    )


def result_kernel(count, x_ref, gain_ref, w_value_ref, r_ref, back_ref, *refs):
    folded, refs = refs[:count], refs[count:]
    passed_ref, loss_ref, _, out_ref, wide_ref, e_ref, sum_ref = refs
    finish(
        pl.program_id(0), back_ref[...], joined(folded, wide_ref), (passed_ref, loss_ref),
        (out_ref,), x_ref, gain_ref, w_value_ref, r_ref, e_ref, sum_ref,
    )


class Exchange:
    def __init__(self, parts):
        self.parts = list(parts)
        self.got = {0: parts[0]}

    def send(self, slots, after=()):
        for slot in slots:
            pairs = [*enumerate(partners(slot, len(self.parts)))]
            self.got[slot] = lax.ppermute(tied(self.parts[slot], after), "seq", pairs)
        return self

    def all(self):
        return [self.got[slot] for slot in range(len(self.parts))]


def tied(value, after):
    if not after:
        return value
    value, *ended = lax.optimization_barrier((value, *(where.got[slot] for where, slot in after)))
    for (where, slot), got in zip(after, ended):
        where.got[slot] = got
    return value


def local(
    saved_inputs, arrived_grad, loss_grad, norm_gain, w_gate, w_value, w_out, r_factor, l_factor
):
    count = lax.axis_size("seq")
    pipe = lax.axis_size("pipe")
    _, _, rows, width = saved_inputs.shape
    block = w_gate.shape[1]
    size = rows // count

    whole = pl.BlockSpec((rows, width), lambda j: (0, 0))
    whole3 = pl.BlockSpec((None, rows, width), lambda j: (0, 0, 0))
    cut = pl.BlockSpec((rows, block), lambda j: (0, j))
    cut3 = pl.BlockSpec((None, rows, block), lambda j: (0, 0, j))
    weight = pl.BlockSpec((None, block, block), lambda j: (0, 0, j))
    gain = pl.BlockSpec((1, block), lambda j: (0, j))
    square = pl.BlockSpec((None, rows, rows), lambda j: (0, 0, 0))
    small = pl.BlockSpec((None, size, count * count), lambda j: (0, 0, 0))
    slots = [pl.BlockSpec((size, block), lambda j: (0, j))] * count
    pairs = [pl.BlockSpec((2, size, block), lambda j: (0, 0, j))] * count
    upper = [pl.BlockSpec((None, size, block), lambda j: (0, 0, j))] * count
    lower = [pl.BlockSpec((None, size, block), lambda j: (1, 0, j))] * count
    anywhere = pl.BlockSpec(memory_space=pl.ANY)
    x_at = [
        pl.BlockSpec((None, None, rows, width), lambda j: (0, 0, 0, 0)),
        pl.BlockSpec((None, None, rows, width), lambda j: (0, 1, 0, 0)),
    ]

    slot_shapes = [jax.ShapeDtypeStruct((size, width), BF16)] * count
    pair_shapes = [jax.ShapeDtypeStruct((2, size, width), BF16)] * count
    plain = jax.ShapeDtypeStruct((rows, width), BF16)
    exact = jax.ShapeDtypeStruct((rows, width), F32)
    output = jax.ShapeDtypeStruct(saved_inputs.shape, BF16)

    column = pltpu.VMEM((rows, 1), F32)
    wide = pltpu.VMEM((rows, block), F32)
    full = pltpu.VMEM((rows, width), F32)
    square_plain = pl.BlockSpec((rows, rows), lambda j: (0, 0))
    joining = pltpu.VMEM((rows, block), BF16 if size % 16 == 0 else F32)
    product = 2 * rows * width * block

    def call(name, kernel, cost, ins, outs, scratch, mebibytes=32, aliases=None, steps=None):
        return pl.pallas_call(
            kernel,
            grid=(steps or width // block,),
            in_specs=[spec for spec, _ in ins],
            out_specs=[spec for spec, _ in outs],
            out_shape=[shape for _, shape in outs],
            scratch_shapes=scratch,
            input_output_aliases=aliases or {},
            compiler_params=params(mebibytes),
            cost_estimate=pl.CostEstimate(
                flops=int(cost[0] * product),
                bytes_accessed=cost[1] * rows * width * 2,
                transcendentals=0,
            ),
            name=name,
        )(*(value for _, value in ins))

    gains = (gain, norm_gain)
    value_in, gate_in, out_in = (weight, w_value), (weight, w_gate), (weight, w_out)
    r_in = (square, r_factor)
    slots_out, pairs_out = [*zip(slots, slot_shapes)], [*zip(pairs, pair_shapes)]
    every = range(1, count)

    *parts, factor_0 = call(
        "both_0",
        functools.partial(both_kernel, count),
        (4, 10),
        [(x_at[0], saved_inputs), gains, value_in, r_in, gate_in, out_in, (cut3, arrived_grad)],
        [*pairs_out, (cut, exact)],
        [column, wide],
        60,
    )
    out_0 = Exchange(parts).send(every)
    (matrix,) = call(
        "matrix",
        functools.partial(matrix_kernel, count),
        (0.3, 1),
        [(small, l_factor)],
        [(square_plain, jax.ShapeDtypeStruct((rows, rows), BF16))],
        [],
        steps=1,
    )
    m_in = (square_plain, matrix)
    first_1 = Exchange(
        call(
            "first_1",
            functools.partial(first_kernel, count),
            (2, 4),
            [(x_at[1], saved_inputs), gains, value_in, r_in],
            slots_out,
            [column, wide],
        )
    )
    ins = out_0.all()
    ins[0], first_1.parts[0] = lax.optimization_barrier((ins[0], first_1.parts[0]))
    first_1 = Exchange(first_1.parts).send(every)
    parts = call(
        "mixfold_0",
        functools.partial(mix_fold_kernel, count),
        (2, 4),
        [m_in, *zip(pairs, ins)],
        pairs_out,
        [],
    )
    back_0 = Exchange(parts).send(every)
    stacked, result_0 = call(
        "result_0",
        functools.partial(result_both_kernel, count),
        (4, 10),
        [
            (x_at[0], saved_inputs), gains, value_in, r_in, gate_in, (cut, factor_0),
            (whole3, arrived_grad), *zip(pairs, back_0.all()),
        ],
        [(x_at[0], output), (whole, plain)],
        [joining, full, column],
    )
    result_0 = tied(result_0, [(first_1, slot) for slot in every[:4]])
    passed = lax.ppermute(result_0, "pipe", [(s, s - 1) for s in range(1, pipe)])
    *parts, factor_1 = call(
        "mixgrads_1",
        functools.partial(mix_grads_kernel, count),
        (3, 10),
        [
            (x_at[1], saved_inputs), gains, gate_in, out_in, (cut, passed), (cut3, loss_grad),
            m_in, *zip(slots, first_1.all()),
        ],
        [*pairs_out, (cut, exact)],
        [column, wide],
    )
    out_1 = Exchange(parts).send(every)
    fold_1 = Exchange(
        call(
            "fold_1",
            functools.partial(fold_kernel, count),
            (1, 2),
            [m_in, *zip(lower, out_1.all())],
            slots_out,
            [],
        )
    ).send(every)
    (gate_1,) = call(
        "back_1",
        functools.partial(back_kernel, count),
        (1, 6),
        [gate_in, (cut, factor_1), *zip(upper, out_1.all())],
        [(cut, exact)],
        [joining],
    )
    ins = [
        (x_at[1], saved_inputs), gains, value_in, r_in, (cut, gate_1),
        *zip(slots, fold_1.all()), (whole, passed), (whole3, loss_grad), (anywhere, stacked),
    ]
    (out,) = call(
        "result_1",
        functools.partial(result_kernel, count),
        (3, 8),
        ins,
        [(x_at[1], output)],
        [joining, full, column],
        aliases={len(ins) - 1: 0},
    )
    return out


def solution(mesh):
    placed = (
        P("pipe", None, "seq", None),
        P("pipe", "seq", None),
        P(None, "seq", None),
        P("pipe", None),
        P("pipe", None, None),
        P("pipe", None, None),
        P("pipe", None, None),
        P("pipe", "seq", None),
        P("pipe", "seq", None),
    )
    return jax.shard_map(
        local, mesh=mesh, in_specs=placed, out_specs=P("pipe", None, "seq", None), check_vma=False
    )
```

```python
import functools

import jax
import jax.numpy as jnp
from jax import lax
from jax.experimental import pallas as pl
from jax.experimental.pallas import tpu as pltpu
from jax.sharding import PartitionSpec as P

TICKS = 2
EPSILON = 1e-05
F32 = jnp.float32
BF16 = jnp.bfloat16
def params(mebibytes=32):
    return pltpu.CompilerParams(
        dimension_semantics=("arbitrary",), vmem_limit_bytes=mebibytes * 1024 * 1024
    )


def dot(a, b, over=((1,), (0,))):
    return lax.dot_general(a, b, (over, ((), ())), preferred_element_type=F32)


PAIRINGS = (
    ((0, 7), (1, 6), (2, 5), (3, 4)),
    ((0, 1), (2, 4), (3, 7), (5, 6)),
    ((0, 3), (1, 5), (2, 6), (4, 7)),
    ((0, 4), (1, 2), (3, 5), (6, 7)),
    ((0, 2), (1, 7), (3, 6), (4, 5)),
    ((0, 6), (1, 4), (2, 3), (5, 7)),
    ((0, 5), (1, 3), (2, 7), (4, 6)),
)


def partners(slot, count):
    if slot == 0 or count != 8:
        return [device ^ slot for device in range(count)]
    both = dict(PAIRINGS[slot - 1])
    both.update({b: a for a, b in both.items()})
    return [both[device] for device in range(count)]


def owner_of(slot, count):
    me = lax.axis_index("seq")
    if slot == 0 or count != 8:
        return me ^ slot
    packed = sum(partner << (3 * device) for device, partner in enumerate(partners(slot, count)))
    return (packed >> (3 * me)) & 7


def owners_of(slots, count):
    if count != 8:
        return slots ^ lax.axis_index("seq")
    owners = jnp.zeros_like(slots)
    for slot in range(count):
        owners = jnp.where(slots == slot, owner_of(slot, count), owners)
    return owners


def rows_of(slot, size):
    owner = owner_of(slot, lax.axis_size("seq"))
    return pl.ds(pl.multiple_of(owner * size, size), size)


def inverse_rms(x_ref):
    x = x_ref[...].astype(F32)
    return lax.rsqrt(jnp.mean(x * x, axis=-1, keepdims=True) + EPSILON)


def columns(j, width):
    return pl.ds(pl.multiple_of(j * width, 128), width)


def split(outs, wide_ref):
    for slot, out in enumerate(outs):
        out[...] = wide_ref[rows_of(slot, out.shape[0]), :].astype(BF16)


def normed_block(j, x_ref, gain_ref, q_ref, width):
    @pl.when(j == 0)
    def _():
        q_ref[...] = inverse_rms(x_ref)

    x = x_ref[:, columns(j, width)].astype(F32)
    return (x * q_ref[...] * gain_ref[...]).astype(BF16)


def first_of(normed, w_ref, r_ref):
    return dot(r_ref[...], dot(normed, w_ref[...]).astype(BF16))


def grads_of(normed, grad, w_gate_ref, w_out_ref, factor_ref):
    gate = dot(normed, w_gate_ref[...])
    inner = dot(grad, w_out_ref[...], ((1,), (1,)))
    sigmoid = jax.nn.sigmoid(gate)
    factor_ref[...] = inner * sigmoid * (1.0 + gate * (1.0 - sigmoid))
    return inner * gate * sigmoid


def first_kernel(count, x_ref, gain_ref, w_ref, r_ref, *refs):
    outs, (q_ref, wide_ref) = refs[:count], refs[count:]
    normed = normed_block(pl.program_id(0), x_ref, gain_ref, q_ref, w_ref.shape[1])
    wide_ref[...] = first_of(normed, w_ref, r_ref)
    split(outs, wide_ref)


def pick_gradient(refs):
    if len(refs) == 1:
        return refs[0][...]
    last = lax.axis_index("pipe") == lax.axis_size("pipe") - 1
    return jnp.where(last, refs[1][...], refs[0][...])


def grad_kernel(count, sources, x_ref, gain_ref, w_gate_ref, w_out_ref, *refs):
    grads, refs = refs[:sources], refs[sources:]
    outs, (factor_ref, q_ref, wide_ref) = refs[:count], refs[count:]
    normed = normed_block(pl.program_id(0), x_ref, gain_ref, q_ref, w_gate_ref.shape[1])
    wide_ref[...] = grads_of(normed, pick_gradient(grads), w_gate_ref, w_out_ref, factor_ref)
    split(outs, wide_ref)


def matrix_kernel(count, l_ref, out_ref):
    size = l_ref.shape[0]
    wide = count * size
    bits = count.bit_length() - 1
    iota = functools.partial(lax.broadcasted_iota, jnp.int32)

    shape = (count, size, count * count)
    tall = jnp.broadcast_to(l_ref[...].astype(F32)[None], shape)
    tall = jnp.where(iota(shape, 2) >> bits == owners_of(iota(shape, 0), count), tall, 0.0)
    tall = tall.reshape(wide, count * count).astype(BF16)

    shape = (count * count, wide)
    source = owners_of(iota(shape, 1) >> (size.bit_length() - 1), count)
    spread = dot(tall, jnp.where(iota(shape, 0) & (count - 1) == source, 1.0, 0.0).astype(BF16))

    row, column = iota((wide, wide), 0) & (size - 1), iota((wide, wide), 1) & (size - 1)
    out_ref[...] = jnp.where(row == column, spread, 0.0).astype(BF16)


def halves(ins):
    me, size = lax.axis_index("seq"), ins[0].shape[0]
    values = [ins[0][...]]
    for slot, part in enumerate(ins[1:], 1):
        both = part[...]
        if both.shape[0] > size:
            both = jnp.where(owner_of(slot, len(ins)) > me, both[size:], both[:size])
        values.append(both)
    return values


def stacked_slots(ins):
    ins = halves(ins)
    if ins[0].shape[0] % 16 == 0:
        return jnp.concatenate(ins, axis=0)
    return jnp.concatenate([part.astype(F32) for part in ins], axis=0).astype(BF16)


def spread_slots(outs, value):
    size = outs[0].shape[0]
    for slot, out in enumerate(outs):
        out[...] = value[slot * size : (slot + 1) * size].astype(BF16)


def joined(ins, wide_ref):
    for slot, part in enumerate(halves(ins)):
        wide_ref[rows_of(slot, part.shape[0]), :] = part.astype(wide_ref.dtype)
    return wide_ref[...]


def mix_kernel(count, transposed, m_ref, *refs):
    ins, outs = refs[:count], refs[count:]
    over = ((0,), (0,)) if transposed else ((1,), (0,))
    spread_slots(outs, dot(m_ref[...], stacked_slots(ins), over))


def back_kernel(count, w_gate_ref, factor_ref, *refs):
    mixed, (out_ref, wide_ref) = refs[:count], refs[count:]
    gate_grad = (factor_ref[...] * joined(mixed, wide_ref).astype(F32)).astype(BF16)
    out_ref[...] = dot(gate_grad, w_gate_ref[...], ((1,), (1,)))


def finish(j, back, folded, grads, outs, x_ref, gain_ref, w_value_ref, r_ref, e_ref, sum_ref):
    at = columns(j, w_value_ref.shape[1])
    value_grad = dot(r_ref[...], folded.astype(BF16), ((0,), (0,))).astype(BF16)
    e = (back + dot(value_grad, w_value_ref[...], ((1,), (1,)))) * gain_ref[...]
    e_ref[:, at] = e
    part = jnp.sum(e * x_ref[:, at].astype(F32), axis=-1, keepdims=True)

    @pl.when(j == 0)
    def _():
        sum_ref[...] = part

    @pl.when(j > 0)
    def _():
        sum_ref[...] += part

    @pl.when(j == pl.num_programs(0) - 1)
    def _():
        x = x_ref[...].astype(F32)
        q = inverse_rms(x_ref)
        mean = sum_ref[...] / x.shape[1]
        result = pick_gradient(grads).astype(F32) + q * e_ref[...] - q * q * q * x * mean
        for out in outs:
            out[...] = result.astype(BF16)


def result_kernel(count, sources, x_ref, gain_ref, w_value_ref, r_ref, back_ref, *refs):
    folded, refs = refs[:count], refs[count:]
    grads, refs = refs[:sources], refs[sources:]
    outs, (wide_ref, e_ref, sum_ref) = refs[sources - 1 : -3], refs[-3:]
    finish(
        pl.program_id(0), back_ref[...], joined(folded, wide_ref), grads, outs,
        x_ref, gain_ref, w_value_ref, r_ref, e_ref, sum_ref,
    )


class Exchange:
    def __init__(self, parts):
        self.parts = list(parts)
        self.got = {0: parts[0]}

    def send(self, slots, after=()):
        for slot in slots:
            pairs = [*enumerate(partners(slot, len(self.parts)))]
            self.got[slot] = lax.ppermute(tied(self.parts[slot], after), "seq", pairs)
        return self

    def swap(self, slots):
        for slot in slots:
            other = partners(slot, len(self.parts))
            groups = [[i, j] for i, j in enumerate(other) if i < j]
            self.got[slot] = lax.all_gather(
                self.parts[slot], "seq", axis_index_groups=groups, tiled=True
            )
        return self

    def all(self):
        return [self.got[slot] for slot in range(len(self.parts))]


def tied(value, after):
    if not after:
        return value
    value, *ended = lax.optimization_barrier((value, *(where.got[slot] for where, slot in after)))
    for (where, slot), got in zip(after, ended):
        where.got[slot] = got
    return value


def local(
    saved_inputs, arrived_grad, loss_grad, norm_gain, w_gate, w_value, w_out, r_factor, l_factor
):
    count = lax.axis_size("seq")
    pipe = lax.axis_size("pipe")
    _, _, rows, width = saved_inputs.shape
    block = w_gate.shape[1]
    size = rows // count

    whole = pl.BlockSpec((rows, width), lambda j: (0, 0))
    whole3 = pl.BlockSpec((None, rows, width), lambda j: (0, 0, 0))
    cut = pl.BlockSpec((rows, block), lambda j: (0, j))
    cut3 = pl.BlockSpec((None, rows, block), lambda j: (0, 0, j))
    weight = pl.BlockSpec((None, block, block), lambda j: (0, 0, j))
    gain = pl.BlockSpec((1, block), lambda j: (0, j))
    square = pl.BlockSpec((None, rows, rows), lambda j: (0, 0, 0))
    small = pl.BlockSpec((None, size, count * count), lambda j: (0, 0, 0))
    slots = [pl.BlockSpec((size, block), lambda j: (0, j))] * count
    double = pl.BlockSpec((2 * size, block), lambda j: (0, j))
    anywhere = pl.BlockSpec(memory_space=pl.ANY)
    x_at = [
        pl.BlockSpec((None, None, rows, width), lambda j: (0, 0, 0, 0)),
        pl.BlockSpec((None, None, rows, width), lambda j: (0, 1, 0, 0)),
    ]

    slot_shapes = [jax.ShapeDtypeStruct((size, width), BF16)] * count
    plain = jax.ShapeDtypeStruct((rows, width), BF16)
    exact = jax.ShapeDtypeStruct((rows, width), F32)
    output = jax.ShapeDtypeStruct(saved_inputs.shape, BF16)

    column = pltpu.VMEM((rows, 1), F32)
    wide = pltpu.VMEM((rows, block), F32)
    full = pltpu.VMEM((rows, width), F32)
    square_plain = pl.BlockSpec((rows, rows), lambda j: (0, 0))
    joining = pltpu.VMEM((rows, block), BF16 if size % 16 == 0 else F32)
    product = 2 * rows * width * block

    def call(name, kernel, cost, ins, outs, scratch, mebibytes=32, aliases=None, steps=None):
        return pl.pallas_call(
            kernel,
            grid=(steps or width // block,),
            in_specs=[spec for spec, _ in ins],
            out_specs=[spec for spec, _ in outs],
            out_shape=[shape for _, shape in outs],
            scratch_shapes=scratch,
            input_output_aliases=aliases or {},
            compiler_params=params(mebibytes),
            cost_estimate=pl.CostEstimate(
                flops=int(cost[0] * product),
                bytes_accessed=cost[1] * rows * width * 2,
                transcendentals=0,
            ),
            name=name,
        )(*(value for _, value in ins))

    gains = (gain, norm_gain)
    value_in, gate_in, out_in = (weight, w_value), (weight, w_gate), (weight, w_out)
    r_in = (square, r_factor)
    slots_out = [*zip(slots, slot_shapes)]
    every = range(1, count)

    def first(tick, mebibytes=32, gains=gains):
        return call(
            f"first_{tick}",
            functools.partial(first_kernel, count),
            (2, 4),
            [(x_at[tick], saved_inputs), gains, value_in, r_in],
            slots_out,
            [column, wide],
            mebibytes,
        )

    def grads(tick, incoming):
        *parts, factor = call(
            f"grads_{tick}",
            functools.partial(grad_kernel, count, len(incoming)),
            (2, 8),
            [(x_at[tick], saved_inputs), gains, gate_in, out_in, *incoming],
            [*slots_out, (cut, exact)],
            [column, wide],
        )
        return parts, factor

    def slots_in(parts):
        return [(slots[0] if part.shape[0] == size else double, part) for part in parts]

    def mix(name, parts, transposed):
        return call(
            name,
            functools.partial(mix_kernel, count, transposed),
            (1, 2),
            [(square_plain, matrix), *slots_in(parts)],
            slots_out,
            [],
        )

    def back(tick, mixed, factor):
        return call(
            f"back_{tick}",
            functools.partial(back_kernel, count),
            (1, 6),
            [gate_in, (cut, factor), *slots_in(mixed)],
            [(cut, exact)],
            [joining],
        )[0]

    def result(tick, gate_part, folded, incoming, stacked):
        ins = [(x_at[tick], saved_inputs), gains, value_in, r_in, (cut, gate_part)]
        ins += [*slots_in(folded), *incoming]
        outs = [(x_at[tick], output)]
        aliases = {}
        if stacked is None:
            outs.append((whole, plain))
        else:
            ins.append((anywhere, stacked))
            aliases = {len(ins) - 1: 0}
        return call(
            f"result_{tick}",
            functools.partial(result_kernel, count, len(incoming)),
            (3, 8),
            ins,
            outs,
            [joining, full, column],
            aliases=aliases,
        )

    first_0 = Exchange(first(0, 60)).send(every)
    (matrix,) = call(
        "matrix",
        functools.partial(matrix_kernel, count),
        (0.3, 1),
        [(small, l_factor)],
        [(square_plain, jax.ShapeDtypeStruct((rows, rows), BF16))],
        [],
        steps=1,
    )
    parts, factor_0 = grads(0, [(cut3, arrived_grad)])
    grad_0 = Exchange(parts).send(every)
    mix_0 = Exchange(mix("mix_0", first_0.all(), False)).send(every)
    fold_0 = Exchange(mix("fold_0", grad_0.all(), True)).send(every)
    later_gain, fold_0.parts[0] = lax.optimization_barrier((norm_gain, fold_0.parts[0]))
    fold_0.got[0] = fold_0.parts[0]
    first_1 = Exchange(first(1, gains=(gain, later_gain))).swap(every)
    gate_0 = back(0, mix_0.all(), factor_0)
    gate_0, first_1.parts[0] = lax.optimization_barrier((gate_0, first_1.parts[0]))
    first_1.got[0] = first_1.parts[0]
    stacked, result_0 = result(0, gate_0, fold_0.all(), [(whole3, arrived_grad)], None)
    passed = lax.ppermute(result_0, "pipe", [(s, s - 1) for s in range(1, pipe)])
    mix_1 = Exchange(mix("mix_1", first_1.all(), False)).swap(every)
    parts, factor_1 = grads(1, [(cut, passed), (cut3, loss_grad)])
    grad_1 = Exchange(parts).send(every)
    fold_1 = Exchange(mix("fold_1", grad_1.all(), True)).send(every)
    gate_1 = back(1, mix_1.all(), factor_1)
    incoming = [(whole, passed), (whole3, loss_grad)]
    return result(1, gate_1, fold_1.all(), incoming, stacked)[0]


def solution(mesh):
    placed = (
        P("pipe", None, "seq", None),
        P("pipe", "seq", None),
        P(None, "seq", None),
        P("pipe", None),
        P("pipe", None, None),
        P("pipe", None, None),
        P("pipe", None, None),
        P("pipe", "seq", None),
        P("pipe", "seq", None),
    )
    return jax.shard_map(
        local, mesh=mesh, in_specs=placed, out_specs=P("pipe", None, "seq", None), check_vma=False
    )
```

```python
import functools

import jax
import jax.numpy as jnp
from jax import lax
from jax.experimental import pallas as pl
from jax.experimental.pallas import tpu as pltpu
from jax.sharding import PartitionSpec as P

TICKS = 2
EPSILON = 1e-05
F32 = jnp.float32
BF16 = jnp.bfloat16
def params(mebibytes=32):
    return pltpu.CompilerParams(
        dimension_semantics=("arbitrary",), vmem_limit_bytes=mebibytes * 1024 * 1024
    )


def dot(a, b, over=((1,), (0,))):
    return lax.dot_general(a, b, (over, ((), ())), preferred_element_type=F32)


PAIRINGS = (
    ((0, 7), (1, 6), (2, 5), (3, 4)),
    ((0, 1), (2, 4), (3, 7), (5, 6)),
    ((0, 3), (1, 5), (2, 6), (4, 7)),
    ((0, 4), (1, 2), (3, 5), (6, 7)),
    ((0, 2), (1, 7), (3, 6), (4, 5)),
    ((0, 6), (1, 4), (2, 3), (5, 7)),
    ((0, 5), (1, 3), (2, 7), (4, 6)),
)


def partners(slot, count):
    if slot == 0 or count != 8:
        return [device ^ slot for device in range(count)]
    both = dict(PAIRINGS[slot - 1])
    both.update({b: a for a, b in both.items()})
    return [both[device] for device in range(count)]


def owner_of(slot, count):
    me = lax.axis_index("seq")
    if slot == 0 or count != 8:
        return me ^ slot
    packed = sum(partner << (3 * device) for device, partner in enumerate(partners(slot, count)))
    return (packed >> (3 * me)) & 7


def owners_of(slots, count):
    if count != 8:
        return slots ^ lax.axis_index("seq")
    owners = jnp.zeros_like(slots)
    for slot in range(count):
        owners = jnp.where(slots == slot, owner_of(slot, count), owners)
    return owners


def rows_of(slot, size):
    owner = owner_of(slot, lax.axis_size("seq"))
    return pl.ds(pl.multiple_of(owner * size, size), size)


def inverse_rms(x_ref):
    x = x_ref[...].astype(F32)
    return lax.rsqrt(jnp.mean(x * x, axis=-1, keepdims=True) + EPSILON)


def columns(j, width):
    return pl.ds(pl.multiple_of(j * width, 128), width)


def split(outs, wide_ref):
    for slot, out in enumerate(outs):
        out[...] = wide_ref[rows_of(slot, out.shape[0]), :].astype(BF16)


def normed_block(j, x_ref, gain_ref, q_ref, width):
    @pl.when(j == 0)
    def _():
        q_ref[...] = inverse_rms(x_ref)

    x = x_ref[:, columns(j, width)].astype(F32)
    return (x * q_ref[...] * gain_ref[...]).astype(BF16)


def first_of(normed, w_ref, r_ref):
    return dot(r_ref[...], dot(normed, w_ref[...]).astype(BF16))


def grads_of(normed, grad, w_gate_ref, w_out_ref, factor_ref):
    gate = dot(normed, w_gate_ref[...])
    inner = dot(grad, w_out_ref[...], ((1,), (1,)))
    sigmoid = jax.nn.sigmoid(gate)
    factor_ref[...] = inner * sigmoid * (1.0 + gate * (1.0 - sigmoid))
    return inner * gate * sigmoid


def first_kernel(count, x_ref, gain_ref, w_ref, r_ref, *refs):
    outs, (q_ref, wide_ref) = refs[:count], refs[count:]
    normed = normed_block(pl.program_id(0), x_ref, gain_ref, q_ref, w_ref.shape[1])
    wide_ref[...] = first_of(normed, w_ref, r_ref)
    split(outs, wide_ref)


def pick_gradient(refs):
    if len(refs) == 1:
        return refs[0][...]
    last = lax.axis_index("pipe") == lax.axis_size("pipe") - 1
    return jnp.where(last, refs[1][...], refs[0][...])


def grad_kernel(count, sources, x_ref, gain_ref, w_gate_ref, w_out_ref, *refs):
    grads, refs = refs[:sources], refs[sources:]
    outs, (factor_ref, q_ref, wide_ref) = refs[:count], refs[count:]
    normed = normed_block(pl.program_id(0), x_ref, gain_ref, q_ref, w_gate_ref.shape[1])
    wide_ref[...] = grads_of(normed, pick_gradient(grads), w_gate_ref, w_out_ref, factor_ref)
    split(outs, wide_ref)


def matrix_kernel(count, l_ref, out_ref):
    size = l_ref.shape[0]
    wide = count * size
    bits = count.bit_length() - 1
    iota = functools.partial(lax.broadcasted_iota, jnp.int32)

    shape = (count, size, count * count)
    tall = jnp.broadcast_to(l_ref[...].astype(F32)[None], shape)
    tall = jnp.where(iota(shape, 2) >> bits == owners_of(iota(shape, 0), count), tall, 0.0)
    tall = tall.reshape(wide, count * count).astype(BF16)

    shape = (count * count, wide)
    source = owners_of(iota(shape, 1) >> (size.bit_length() - 1), count)
    spread = dot(tall, jnp.where(iota(shape, 0) & (count - 1) == source, 1.0, 0.0).astype(BF16))

    row, column = iota((wide, wide), 0) & (size - 1), iota((wide, wide), 1) & (size - 1)
    out_ref[...] = jnp.where(row == column, spread, 0.0).astype(BF16)


def stacked_slots(ins):
    if ins[0].shape[0] % 16 == 0:
        return jnp.concatenate([part[...] for part in ins], axis=0)
    return jnp.concatenate([part[...].astype(F32) for part in ins], axis=0).astype(BF16)


def spread_slots(outs, value):
    size = outs[0].shape[0]
    for slot, out in enumerate(outs):
        out[...] = value[slot * size : (slot + 1) * size].astype(BF16)


def joined(ins, wide_ref):
    for slot, part in enumerate(ins):
        wide_ref[rows_of(slot, part.shape[0]), :] = part[...].astype(wide_ref.dtype)
    return wide_ref[...]


def mix_kernel(count, transposed, m_ref, *refs):
    ins, outs = refs[:count], refs[count:]
    over = ((0,), (0,)) if transposed else ((1,), (0,))
    spread_slots(outs, dot(m_ref[...], stacked_slots(ins), over))


def back_kernel(count, w_gate_ref, factor_ref, *refs):
    mixed, (out_ref, wide_ref) = refs[:count], refs[count:]
    gate_grad = (factor_ref[...] * joined(mixed, wide_ref).astype(F32)).astype(BF16)
    out_ref[...] = dot(gate_grad, w_gate_ref[...], ((1,), (1,)))


def finish(j, back, folded, grads, outs, x_ref, gain_ref, w_value_ref, r_ref, e_ref, sum_ref):
    at = columns(j, w_value_ref.shape[1])
    value_grad = dot(r_ref[...], folded.astype(BF16), ((0,), (0,))).astype(BF16)
    e = (back + dot(value_grad, w_value_ref[...], ((1,), (1,)))) * gain_ref[...]
    e_ref[:, at] = e
    part = jnp.sum(e * x_ref[:, at].astype(F32), axis=-1, keepdims=True)

    @pl.when(j == 0)
    def _():
        sum_ref[...] = part

    @pl.when(j > 0)
    def _():
        sum_ref[...] += part

    @pl.when(j == pl.num_programs(0) - 1)
    def _():
        x = x_ref[...].astype(F32)
        q = inverse_rms(x_ref)
        mean = sum_ref[...] / x.shape[1]
        result = pick_gradient(grads).astype(F32) + q * e_ref[...] - q * q * q * x * mean
        for out in outs:
            out[...] = result.astype(BF16)


def result_kernel(count, sources, x_ref, gain_ref, w_value_ref, r_ref, back_ref, *refs):
    folded, refs = refs[:count], refs[count:]
    grads, refs = refs[:sources], refs[sources:]
    outs, (wide_ref, e_ref, sum_ref) = refs[sources - 1 : -3], refs[-3:]
    finish(
        pl.program_id(0), back_ref[...], joined(folded, wide_ref), grads, outs,
        x_ref, gain_ref, w_value_ref, r_ref, e_ref, sum_ref,
    )


class Exchange:
    def __init__(self, parts):
        self.parts = list(parts)
        self.got = {0: parts[0]}

    def send(self, slots, after=()):
        for slot in slots:
            pairs = [*enumerate(partners(slot, len(self.parts)))]
            self.got[slot] = lax.ppermute(tied(self.parts[slot], after), "seq", pairs)
        return self

    def all(self):
        return [self.got[slot] for slot in range(len(self.parts))]


def tied(value, after):
    if not after:
        return value
    value, *ended = lax.optimization_barrier((value, *(where.got[slot] for where, slot in after)))
    for (where, slot), got in zip(after, ended):
        where.got[slot] = got
    return value


def local(
    saved_inputs, arrived_grad, loss_grad, norm_gain, w_gate, w_value, w_out, r_factor, l_factor
):
    count = lax.axis_size("seq")
    pipe = lax.axis_size("pipe")
    _, _, rows, width = saved_inputs.shape
    block = w_gate.shape[1]
    size = rows // count

    whole = pl.BlockSpec((rows, width), lambda j: (0, 0))
    whole3 = pl.BlockSpec((None, rows, width), lambda j: (0, 0, 0))
    cut = pl.BlockSpec((rows, block), lambda j: (0, j))
    cut3 = pl.BlockSpec((None, rows, block), lambda j: (0, 0, j))
    weight = pl.BlockSpec((None, block, block), lambda j: (0, 0, j))
    gain = pl.BlockSpec((1, block), lambda j: (0, j))
    square = pl.BlockSpec((None, rows, rows), lambda j: (0, 0, 0))
    small = pl.BlockSpec((None, size, count * count), lambda j: (0, 0, 0))
    slots = [pl.BlockSpec((size, block), lambda j: (0, j))] * count
    anywhere = pl.BlockSpec(memory_space=pl.ANY)
    x_at = [
        pl.BlockSpec((None, None, rows, width), lambda j: (0, 0, 0, 0)),
        pl.BlockSpec((None, None, rows, width), lambda j: (0, 1, 0, 0)),
    ]

    slot_shapes = [jax.ShapeDtypeStruct((size, width), BF16)] * count
    plain = jax.ShapeDtypeStruct((rows, width), BF16)
    exact = jax.ShapeDtypeStruct((rows, width), F32)
    output = jax.ShapeDtypeStruct(saved_inputs.shape, BF16)

    column = pltpu.VMEM((rows, 1), F32)
    wide = pltpu.VMEM((rows, block), F32)
    full = pltpu.VMEM((rows, width), F32)
    square_plain = pl.BlockSpec((rows, rows), lambda j: (0, 0))
    joining = pltpu.VMEM((rows, block), BF16 if size % 16 == 0 else F32)
    product = 2 * rows * width * block

    def call(name, kernel, cost, ins, outs, scratch, mebibytes=32, aliases=None, steps=None):
        return pl.pallas_call(
            kernel,
            grid=(steps or width // block,),
            in_specs=[spec for spec, _ in ins],
            out_specs=[spec for spec, _ in outs],
            out_shape=[shape for _, shape in outs],
            scratch_shapes=scratch,
            input_output_aliases=aliases or {},
            compiler_params=params(mebibytes),
            cost_estimate=pl.CostEstimate(
                flops=int(cost[0] * product),
                bytes_accessed=cost[1] * rows * width * 2,
                transcendentals=0,
            ),
            name=name,
        )(*(value for _, value in ins))

    gains = (gain, norm_gain)
    value_in, gate_in, out_in = (weight, w_value), (weight, w_gate), (weight, w_out)
    r_in = (square, r_factor)
    slots_out = [*zip(slots, slot_shapes)]
    every = range(1, count)

    def first(tick, mebibytes=32):
        return call(
            f"first_{tick}",
            functools.partial(first_kernel, count),
            (2, 4),
            [(x_at[tick], saved_inputs), gains, value_in, r_in],
            slots_out,
            [column, wide],
            mebibytes,
        )

    def grads(tick, incoming):
        *parts, factor = call(
            f"grads_{tick}",
            functools.partial(grad_kernel, count, len(incoming)),
            (2, 8),
            [(x_at[tick], saved_inputs), gains, gate_in, out_in, *incoming],
            [*slots_out, (cut, exact)],
            [column, wide],
        )
        return parts, factor

    def mix(name, parts, transposed):
        return call(
            name,
            functools.partial(mix_kernel, count, transposed),
            (1, 2),
            [(square_plain, matrix), *zip(slots, parts)],
            slots_out,
            [],
        )

    def back(tick, mixed, factor):
        return call(
            f"back_{tick}",
            functools.partial(back_kernel, count),
            (1, 6),
            [gate_in, (cut, factor), *zip(slots, mixed)],
            [(cut, exact)],
            [joining],
        )[0]

    def result(tick, gate_part, folded, incoming, stacked):
        ins = [(x_at[tick], saved_inputs), gains, value_in, r_in, (cut, gate_part)]
        ins += [*zip(slots, folded), *incoming]
        outs = [(x_at[tick], output)]
        aliases = {}
        if stacked is None:
            outs.append((whole, plain))
        else:
            ins.append((anywhere, stacked))
            aliases = {len(ins) - 1: 0}
        return call(
            f"result_{tick}",
            functools.partial(result_kernel, count, len(incoming)),
            (3, 8),
            ins,
            outs,
            [joining, full, column],
            aliases=aliases,
        )

    first_0 = Exchange(first(0, 60)).send(every)
    (matrix,) = call(
        "matrix",
        functools.partial(matrix_kernel, count),
        (0.3, 1),
        [(small, l_factor)],
        [(square_plain, jax.ShapeDtypeStruct((rows, rows), BF16))],
        [],
        steps=1,
    )
    parts, factor_0 = grads(0, [(cut3, arrived_grad)])
    grad_0 = Exchange(parts).send(every)
    mix_0 = Exchange(mix("mix_0", first_0.all(), False)).send(every)
    fold_0 = Exchange(mix("fold_0", grad_0.all(), True)).send(every)
    gate_0 = back(0, mix_0.all(), factor_0)
    first_1 = Exchange(first(1))
    gate_0, first_1.parts[0] = lax.optimization_barrier((gate_0, first_1.parts[0]))
    first_1.send(every)
    stacked, result_0 = result(0, gate_0, fold_0.all(), [(whole3, arrived_grad)], None)
    result_0 = tied(result_0, [(first_1, slot) for slot in every[: min(4, count // 2)]])
    passed = lax.ppermute(result_0, "pipe", [(s, s - 1) for s in range(1, pipe)])
    mix_1 = Exchange(mix("mix_1", first_1.all(), False)).send(every)
    passed, mix_1.parts[0] = lax.optimization_barrier((passed, mix_1.parts[0]))
    mix_1.got[0] = mix_1.parts[0]
    parts, factor_1 = grads(1, [(cut, passed), (cut3, loss_grad)])
    for slot in every[:3]:
        parts[count - slot] = tied(parts[count - slot], [(mix_1, slot)])
    grad_1 = Exchange(parts).send(every)
    fold_1 = Exchange(mix("fold_1", grad_1.all(), True)).send(every)
    gate_1 = back(1, mix_1.all(), factor_1)
    incoming = [(whole, passed), (whole3, loss_grad)]
    return result(1, gate_1, fold_1.all(), incoming, stacked)[0]


def solution(mesh):
    placed = (
        P("pipe", None, "seq", None),
        P("pipe", "seq", None),
        P(None, "seq", None),
        P("pipe", None),
        P("pipe", None, None),
        P("pipe", None, None),
        P("pipe", None, None),
        P("pipe", "seq", None),
        P("pipe", "seq", None),
    )
    return jax.shard_map(
        local, mesh=mesh, in_specs=placed, out_specs=P("pipe", None, "seq", None), check_vma=False
    )
```

```python
import functools

import jax
import jax.numpy as jnp
from jax import lax
from jax.experimental import pallas as pl
from jax.experimental.pallas import tpu as pltpu
from jax.sharding import PartitionSpec as P

TICKS = 2
EPSILON = 1e-05
F32 = jnp.float32
BF16 = jnp.bfloat16
def params(mebibytes=32):
    return pltpu.CompilerParams(
        dimension_semantics=("arbitrary",), vmem_limit_bytes=mebibytes * 1024 * 1024
    )


def dot(a, b, over=((1,), (0,))):
    return lax.dot_general(a, b, (over, ((), ())), preferred_element_type=F32)


PAIRINGS = (
    ((0, 7), (1, 6), (2, 5), (3, 4)),
    ((0, 1), (2, 4), (3, 7), (5, 6)),
    ((0, 3), (1, 5), (2, 6), (4, 7)),
    ((0, 4), (1, 2), (3, 5), (6, 7)),
    ((0, 2), (1, 7), (3, 6), (4, 5)),
    ((0, 6), (1, 4), (2, 3), (5, 7)),
    ((0, 5), (1, 3), (2, 7), (4, 6)),
)


def partners(slot, count):
    if slot == 0 or count != 8:
        return [device ^ slot for device in range(count)]
    both = dict(PAIRINGS[slot - 1])
    both.update({b: a for a, b in both.items()})
    return [both[device] for device in range(count)]


def owner_of(slot, count):
    me = lax.axis_index("seq")
    if slot == 0 or count != 8:
        return me ^ slot
    packed = sum(partner << (3 * device) for device, partner in enumerate(partners(slot, count)))
    return (packed >> (3 * me)) & 7


def owners_of(slots, count):
    if count != 8:
        return slots ^ lax.axis_index("seq")
    owners = jnp.zeros_like(slots)
    for slot in range(count):
        owners = jnp.where(slots == slot, owner_of(slot, count), owners)
    return owners


def rows_of(slot, size):
    owner = owner_of(slot, lax.axis_size("seq"))
    return pl.ds(pl.multiple_of(owner * size, size), size)


def inverse_rms(x_ref):
    x = x_ref[...].astype(F32)
    return lax.rsqrt(jnp.mean(x * x, axis=-1, keepdims=True) + EPSILON)


def columns(j, width):
    return pl.ds(pl.multiple_of(j * width, 128), width)


def split(outs, wide_ref):
    for slot, out in enumerate(outs):
        out[...] = wide_ref[rows_of(slot, out.shape[0]), :].astype(BF16)


def normed_block(j, x_ref, gain_ref, q_ref, width):
    @pl.when(j == 0)
    def _():
        q_ref[...] = inverse_rms(x_ref)

    x = x_ref[:, columns(j, width)].astype(F32)
    return (x * q_ref[...] * gain_ref[...]).astype(BF16)


def first_of(normed, w_ref, r_ref):
    return dot(r_ref[...], dot(normed, w_ref[...]).astype(BF16))


def grads_of(normed, grad, w_gate_ref, w_out_ref, factor_ref):
    gate = dot(normed, w_gate_ref[...])
    inner = dot(grad, w_out_ref[...], ((1,), (1,)))
    sigmoid = jax.nn.sigmoid(gate)
    factor_ref[...] = inner * sigmoid * (1.0 + gate * (1.0 - sigmoid))
    return inner * gate * sigmoid


def first_kernel(count, x_ref, gain_ref, w_ref, r_ref, *refs):
    outs, (q_ref, wide_ref) = refs[:count], refs[count:]
    normed = normed_block(pl.program_id(0), x_ref, gain_ref, q_ref, w_ref.shape[1])
    wide_ref[...] = first_of(normed, w_ref, r_ref)
    split(outs, wide_ref)


def pick_gradient(refs):
    if len(refs) == 1:
        return refs[0][...]
    last = lax.axis_index("pipe") == lax.axis_size("pipe") - 1
    return jnp.where(last, refs[1][...], refs[0][...])


def grad_kernel(count, sources, x_ref, gain_ref, w_gate_ref, w_out_ref, *refs):
    grads, refs = refs[:sources], refs[sources:]
    outs, (factor_ref, q_ref, wide_ref) = refs[:count], refs[count:]
    normed = normed_block(pl.program_id(0), x_ref, gain_ref, q_ref, w_gate_ref.shape[1])
    wide_ref[...] = grads_of(normed, pick_gradient(grads), w_gate_ref, w_out_ref, factor_ref)
    split(outs, wide_ref)


def matrix_kernel(count, l_ref, out_ref):
    size = l_ref.shape[0]
    wide = count * size
    bits = count.bit_length() - 1
    iota = functools.partial(lax.broadcasted_iota, jnp.int32)

    shape = (count, size, count * count)
    tall = jnp.broadcast_to(l_ref[...].astype(F32)[None], shape)
    tall = jnp.where(iota(shape, 2) >> bits == owners_of(iota(shape, 0), count), tall, 0.0)
    tall = tall.reshape(wide, count * count).astype(BF16)

    shape = (count * count, wide)
    source = owners_of(iota(shape, 1) >> (size.bit_length() - 1), count)
    spread = dot(tall, jnp.where(iota(shape, 0) & (count - 1) == source, 1.0, 0.0).astype(BF16))

    row, column = iota((wide, wide), 0) & (size - 1), iota((wide, wide), 1) & (size - 1)
    out_ref[...] = jnp.where(row == column, spread, 0.0).astype(BF16)


def stacked_slots(ins):
    if ins[0].shape[0] % 16 == 0:
        return jnp.concatenate([part[...] for part in ins], axis=0)
    return jnp.concatenate([part[...].astype(F32) for part in ins], axis=0).astype(BF16)


def spread_slots(outs, value):
    size = outs[0].shape[0]
    for slot, out in enumerate(outs):
        out[...] = value[slot * size : (slot + 1) * size].astype(BF16)


def joined(ins, wide_ref):
    for slot, part in enumerate(ins):
        wide_ref[rows_of(slot, part.shape[0]), :] = part[...].astype(wide_ref.dtype)
    return wide_ref[...]


def mix_kernel(count, transposed, m_ref, *refs):
    ins, outs = refs[:count], refs[count:]
    over = ((0,), (0,)) if transposed else ((1,), (0,))
    spread_slots(outs, dot(m_ref[...], stacked_slots(ins), over))


def back_kernel(count, w_gate_ref, factor_ref, *refs):
    mixed, (out_ref, wide_ref) = refs[:count], refs[count:]
    gate_grad = (factor_ref[...] * joined(mixed, wide_ref).astype(F32)).astype(BF16)
    out_ref[...] = dot(gate_grad, w_gate_ref[...], ((1,), (1,)))


def finish(j, back, folded, grads, outs, x_ref, gain_ref, w_value_ref, r_ref, e_ref, sum_ref):
    at = columns(j, w_value_ref.shape[1])
    value_grad = dot(r_ref[...], folded.astype(BF16), ((0,), (0,))).astype(BF16)
    e = (back + dot(value_grad, w_value_ref[...], ((1,), (1,)))) * gain_ref[...]
    e_ref[:, at] = e
    part = jnp.sum(e * x_ref[:, at].astype(F32), axis=-1, keepdims=True)

    @pl.when(j == 0)
    def _():
        sum_ref[...] = part

    @pl.when(j > 0)
    def _():
        sum_ref[...] += part

    @pl.when(j == pl.num_programs(0) - 1)
    def _():
        x = x_ref[...].astype(F32)
        q = inverse_rms(x_ref)
        mean = sum_ref[...] / x.shape[1]
        result = pick_gradient(grads).astype(F32) + q * e_ref[...] - q * q * q * x * mean
        for out in outs:
            out[...] = result.astype(BF16)


def result_kernel(count, sources, x_ref, gain_ref, w_value_ref, r_ref, back_ref, *refs):
    folded, refs = refs[:count], refs[count:]
    grads, refs = refs[:sources], refs[sources:]
    outs, (wide_ref, e_ref, sum_ref) = refs[sources - 1 : -3], refs[-3:]
    finish(
        pl.program_id(0), back_ref[...], joined(folded, wide_ref), grads, outs,
        x_ref, gain_ref, w_value_ref, r_ref, e_ref, sum_ref,
    )


class Exchange:
    def __init__(self, parts):
        self.parts = list(parts)
        self.got = {0: parts[0]}

    def send(self, slots, after=()):
        for slot in slots:
            pairs = [*enumerate(partners(slot, len(self.parts)))]
            self.got[slot] = lax.ppermute(tied(self.parts[slot], after), "seq", pairs)
        return self

    def all(self):
        return [self.got[slot] for slot in range(len(self.parts))]


def tied(value, after):
    if not after:
        return value
    value, *ended = lax.optimization_barrier((value, *(where.got[slot] for where, slot in after)))
    for (where, slot), got in zip(after, ended):
        where.got[slot] = got
    return value


def local(
    saved_inputs, arrived_grad, loss_grad, norm_gain, w_gate, w_value, w_out, r_factor, l_factor
):
    count = lax.axis_size("seq")
    pipe = lax.axis_size("pipe")
    _, _, rows, width = saved_inputs.shape
    block = w_gate.shape[1]
    size = rows // count

    whole = pl.BlockSpec((rows, width), lambda j: (0, 0))
    whole3 = pl.BlockSpec((None, rows, width), lambda j: (0, 0, 0))
    cut = pl.BlockSpec((rows, block), lambda j: (0, j))
    cut3 = pl.BlockSpec((None, rows, block), lambda j: (0, 0, j))
    weight = pl.BlockSpec((None, block, block), lambda j: (0, 0, j))
    gain = pl.BlockSpec((1, block), lambda j: (0, j))
    square = pl.BlockSpec((None, rows, rows), lambda j: (0, 0, 0))
    small = pl.BlockSpec((None, size, count * count), lambda j: (0, 0, 0))
    slots = [pl.BlockSpec((size, block), lambda j: (0, j))] * count
    anywhere = pl.BlockSpec(memory_space=pl.ANY)
    x_at = [
        pl.BlockSpec((None, None, rows, width), lambda j: (0, 0, 0, 0)),
        pl.BlockSpec((None, None, rows, width), lambda j: (0, 1, 0, 0)),
    ]

    slot_shapes = [jax.ShapeDtypeStruct((size, width), BF16)] * count
    plain = jax.ShapeDtypeStruct((rows, width), BF16)
    exact = jax.ShapeDtypeStruct((rows, width), F32)
    output = jax.ShapeDtypeStruct(saved_inputs.shape, BF16)

    column = pltpu.VMEM((rows, 1), F32)
    wide = pltpu.VMEM((rows, block), F32)
    full = pltpu.VMEM((rows, width), F32)
    square_plain = pl.BlockSpec((rows, rows), lambda j: (0, 0))
    joining = pltpu.VMEM((rows, block), BF16 if size % 16 == 0 else F32)
    product = 2 * rows * width * block

    def call(name, kernel, cost, ins, outs, scratch, mebibytes=32, aliases=None, steps=None):
        return pl.pallas_call(
            kernel,
            grid=(steps or width // block,),
            in_specs=[spec for spec, _ in ins],
            out_specs=[spec for spec, _ in outs],
            out_shape=[shape for _, shape in outs],
            scratch_shapes=scratch,
            input_output_aliases=aliases or {},
            compiler_params=params(mebibytes),
            cost_estimate=pl.CostEstimate(
                flops=int(cost[0] * product),
                bytes_accessed=cost[1] * rows * width * 2,
                transcendentals=0,
            ),
            name=name,
        )(*(value for _, value in ins))

    gains = (gain, norm_gain)
    value_in, gate_in, out_in = (weight, w_value), (weight, w_gate), (weight, w_out)
    r_in = (square, r_factor)
    slots_out = [*zip(slots, slot_shapes)]
    every = range(1, count)

    def first(tick, mebibytes=32):
        return call(
            f"first_{tick}",
            functools.partial(first_kernel, count),
            (2, 4),
            [(x_at[tick], saved_inputs), gains, value_in, r_in],
            slots_out,
            [column, wide],
            mebibytes,
        )

    def grads(tick, incoming):
        *parts, factor = call(
            f"grads_{tick}",
            functools.partial(grad_kernel, count, len(incoming)),
            (2, 8),
            [(x_at[tick], saved_inputs), gains, gate_in, out_in, *incoming],
            [*slots_out, (cut, exact)],
            [column, wide],
        )
        return parts, factor

    def mix(name, parts, transposed):
        return call(
            name,
            functools.partial(mix_kernel, count, transposed),
            (40 if name == "mix_1" else 1, 2),
            [(square_plain, matrix), *zip(slots, parts)],
            slots_out,
            [],
        )

    def back(tick, mixed, factor):
        return call(
            f"back_{tick}",
            functools.partial(back_kernel, count),
            (1, 6),
            [gate_in, (cut, factor), *zip(slots, mixed)],
            [(cut, exact)],
            [joining],
        )[0]

    def result(tick, gate_part, folded, incoming, stacked):
        ins = [(x_at[tick], saved_inputs), gains, value_in, r_in, (cut, gate_part)]
        ins += [*zip(slots, folded), *incoming]
        outs = [(x_at[tick], output)]
        aliases = {}
        if stacked is None:
            outs.append((whole, plain))
        else:
            ins.append((anywhere, stacked))
            aliases = {len(ins) - 1: 0}
        return call(
            f"result_{tick}",
            functools.partial(result_kernel, count, len(incoming)),
            (3, 8),
            ins,
            outs,
            [joining, full, column],
            aliases=aliases,
        )

    first_0 = Exchange(first(0, 60)).send(every)
    (matrix,) = call(
        "matrix",
        functools.partial(matrix_kernel, count),
        (0.3, 1),
        [(small, l_factor)],
        [(square_plain, jax.ShapeDtypeStruct((rows, rows), BF16))],
        [],
        steps=1,
    )
    parts, factor_0 = grads(0, [(cut3, arrived_grad)])
    grad_0 = Exchange(parts).send(every)
    mix_0 = Exchange(mix("mix_0", first_0.all(), False)).send(every)
    fold_0 = Exchange(mix("fold_0", grad_0.all(), True)).send(every)
    gate_0 = back(0, mix_0.all(), factor_0)
    first_1 = Exchange(first(1))
    gate_0, first_1.parts[0] = lax.optimization_barrier((gate_0, first_1.parts[0]))
    first_1.send(every)
    stacked, result_0 = result(0, gate_0, fold_0.all(), [(whole3, arrived_grad)], None)
    passed = lax.ppermute(result_0, "pipe", [(s, s - 1) for s in range(1, pipe)])
    mix_1 = Exchange(mix("mix_1", first_1.all(), False)).send(every)
    passed, mix_1.parts[0] = lax.optimization_barrier((passed, mix_1.parts[0]))
    mix_1.got[0] = mix_1.parts[0]
    parts, factor_1 = grads(1, [(cut, passed), (cut3, loss_grad)])
    for slot in every[:2]:
        parts[count - slot] = tied(parts[count - slot], [(mix_1, slot)])
    grad_1 = Exchange(parts).send(every)
    fold_1 = Exchange(mix("fold_1", grad_1.all(), True)).send(every)
    gate_1 = back(1, mix_1.all(), factor_1)
    incoming = [(whole, passed), (whole3, loss_grad)]
    return result(1, gate_1, fold_1.all(), incoming, stacked)[0]


def solution(mesh):
    placed = (
        P("pipe", None, "seq", None),
        P("pipe", "seq", None),
        P(None, "seq", None),
        P("pipe", None),
        P("pipe", None, None),
        P("pipe", None, None),
        P("pipe", None, None),
        P("pipe", "seq", None),
        P("pipe", "seq", None),
    )
    return jax.shard_map(
        local, mesh=mesh, in_specs=placed, out_specs=P("pipe", None, "seq", None), check_vma=False
    )
```

```python
import functools

import jax
import jax.numpy as jnp
from jax import lax
from jax.experimental import pallas as pl
from jax.experimental.pallas import tpu as pltpu
from jax.sharding import PartitionSpec as P

TICKS = 2
EPSILON = 1e-05
F32 = jnp.float32
BF16 = jnp.bfloat16
def params(mebibytes=32):
    return pltpu.CompilerParams(
        dimension_semantics=("arbitrary",), vmem_limit_bytes=mebibytes * 1024 * 1024
    )


def dot(a, b, over=((1,), (0,))):
    return lax.dot_general(a, b, (over, ((), ())), preferred_element_type=F32)


PAIRINGS = (
    ((0, 7), (1, 6), (2, 5), (3, 4)),
    ((0, 1), (2, 4), (3, 7), (5, 6)),
    ((0, 3), (1, 5), (2, 6), (4, 7)),
    ((0, 4), (1, 2), (3, 5), (6, 7)),
    ((0, 2), (1, 7), (3, 6), (4, 5)),
    ((0, 6), (1, 4), (2, 3), (5, 7)),
    ((0, 5), (1, 3), (2, 7), (4, 6)),
)


def partners(slot, count, plain):
    if slot == 0 or count != 8 or plain:
        return [device ^ slot for device in range(count)]
    both = dict(PAIRINGS[slot - 1])
    both.update({b: a for a, b in both.items()})
    return [both[device] for device in range(count)]


def owner_of(slot, count, plain):
    me = lax.axis_index("seq")
    if slot == 0 or count != 8 or plain:
        return me ^ slot
    packed = sum(partner << (3 * device) for device, partner in enumerate(partners(slot, count, plain)))
    return (packed >> (3 * me)) & 7


def owners_of(slots, count, plain):
    if count != 8 or plain:
        return slots ^ lax.axis_index("seq")
    owners = jnp.zeros_like(slots)
    for slot in range(count):
        owners = jnp.where(slots == slot, owner_of(slot, count, plain), owners)
    return owners


def rows_of(slot, size, plain):
    owner = owner_of(slot, lax.axis_size("seq"), plain)
    return pl.ds(pl.multiple_of(owner * size, size), size)


def inverse_rms(x_ref):
    x = x_ref[...].astype(F32)
    return lax.rsqrt(jnp.mean(x * x, axis=-1, keepdims=True) + EPSILON)


def columns(j, width):
    return pl.ds(pl.multiple_of(j * width, 128), width)


def split(outs, wide_ref, plain):
    for slot, out in enumerate(outs):
        out[...] = wide_ref[rows_of(slot, out.shape[0], plain), :].astype(BF16)


def normed_block(j, x_ref, gain_ref, q_ref, width):
    @pl.when(j == 0)
    def _():
        q_ref[...] = inverse_rms(x_ref)

    x = x_ref[:, columns(j, width)].astype(F32)
    return (x * q_ref[...] * gain_ref[...]).astype(BF16)


def first_of(normed, w_ref, r_ref):
    return dot(r_ref[...], dot(normed, w_ref[...]).astype(BF16))


def grads_of(normed, grad, w_gate_ref, w_out_ref, factor_ref):
    gate = dot(normed, w_gate_ref[...])
    inner = dot(grad, w_out_ref[...], ((1,), (1,)))
    sigmoid = jax.nn.sigmoid(gate)
    factor_ref[...] = inner * sigmoid * (1.0 + gate * (1.0 - sigmoid))
    return inner * gate * sigmoid


def first_kernel(count, plain, x_ref, gain_ref, w_ref, r_ref, *refs):
    outs, (q_ref, wide_ref) = refs[:count], refs[count:]
    normed = normed_block(pl.program_id(0), x_ref, gain_ref, q_ref, w_ref.shape[1])
    wide_ref[...] = first_of(normed, w_ref, r_ref)
    split(outs, wide_ref, plain)


def pick_gradient(refs):
    if len(refs) == 1:
        return refs[0][...]
    last = lax.axis_index("pipe") == lax.axis_size("pipe") - 1
    return jnp.where(last, refs[1][...], refs[0][...])


def grad_kernel(count, sources, x_ref, gain_ref, w_gate_ref, w_out_ref, *refs):
    grads, refs = refs[:sources], refs[sources:]
    outs, (factor_ref, q_ref, wide_ref) = refs[:count], refs[count:]
    normed = normed_block(pl.program_id(0), x_ref, gain_ref, q_ref, w_gate_ref.shape[1])
    wide_ref[...] = grads_of(normed, pick_gradient(grads), w_gate_ref, w_out_ref, factor_ref)
    split(outs, wide_ref, False)


def matrix_kernel(count, plain, l_ref, out_ref):
    size = l_ref.shape[0]
    wide = count * size
    bits = count.bit_length() - 1
    iota = functools.partial(lax.broadcasted_iota, jnp.int32)

    shape = (count, size, count * count)
    tall = jnp.broadcast_to(l_ref[...].astype(F32)[None], shape)
    tall = jnp.where(iota(shape, 2) >> bits == owners_of(iota(shape, 0), count, plain), tall, 0.0)
    tall = tall.reshape(wide, count * count).astype(BF16)

    shape = (count * count, wide)
    source = owners_of(iota(shape, 1) >> (size.bit_length() - 1), count, plain)
    spread = dot(tall, jnp.where(iota(shape, 0) & (count - 1) == source, 1.0, 0.0).astype(BF16))

    row, column = iota((wide, wide), 0) & (size - 1), iota((wide, wide), 1) & (size - 1)
    out_ref[...] = jnp.where(row == column, spread, 0.0).astype(BF16)


def stacked_slots(ins):
    if ins[0].shape[0] % 16 == 0:
        return jnp.concatenate([part[...] for part in ins], axis=0)
    return jnp.concatenate([part[...].astype(F32) for part in ins], axis=0).astype(BF16)


def spread_slots(outs, value):
    size = outs[0].shape[0]
    for slot, out in enumerate(outs):
        out[...] = value[slot * size : (slot + 1) * size].astype(BF16)


def joined(ins, wide_ref, plain):
    for slot, part in enumerate(ins):
        wide_ref[rows_of(slot, part.shape[0], plain), :] = part[...].astype(wide_ref.dtype)
    return wide_ref[...]


def mix_kernel(count, transposed, m_ref, *refs):
    ins, outs = refs[:count], refs[count:]
    over = ((0,), (0,)) if transposed else ((1,), (0,))
    spread_slots(outs, dot(m_ref[...], stacked_slots(ins), over))


def back_kernel(count, plain, w_gate_ref, factor_ref, *refs):
    mixed, (out_ref, wide_ref) = refs[:count], refs[count:]
    gate_grad = (factor_ref[...] * joined(mixed, wide_ref, plain).astype(F32)).astype(BF16)
    out_ref[...] = dot(gate_grad, w_gate_ref[...], ((1,), (1,)))


def finish(j, back, folded, grads, outs, x_ref, gain_ref, w_value_ref, r_ref, e_ref, sum_ref):
    at = columns(j, w_value_ref.shape[1])
    value_grad = dot(r_ref[...], folded.astype(BF16), ((0,), (0,))).astype(BF16)
    e = (back + dot(value_grad, w_value_ref[...], ((1,), (1,)))) * gain_ref[...]
    e_ref[:, at] = e
    part = jnp.sum(e * x_ref[:, at].astype(F32), axis=-1, keepdims=True)

    @pl.when(j == 0)
    def _():
        sum_ref[...] = part

    @pl.when(j > 0)
    def _():
        sum_ref[...] += part

    @pl.when(j == pl.num_programs(0) - 1)
    def _():
        x = x_ref[...].astype(F32)
        q = inverse_rms(x_ref)
        mean = sum_ref[...] / x.shape[1]
        result = pick_gradient(grads).astype(F32) + q * e_ref[...] - q * q * q * x * mean
        for out in outs:
            out[...] = result.astype(BF16)


def result_kernel(count, sources, x_ref, gain_ref, w_value_ref, r_ref, back_ref, *refs):
    folded, refs = refs[:count], refs[count:]
    grads, refs = refs[:sources], refs[sources:]
    outs, (wide_ref, e_ref, sum_ref) = refs[sources - 1 : -3], refs[-3:]
    finish(
        pl.program_id(0), back_ref[...], joined(folded, wide_ref, False), grads, outs,
        x_ref, gain_ref, w_value_ref, r_ref, e_ref, sum_ref,
    )


class Exchange:
    def __init__(self, parts, plain=False):
        self.parts, self.plain = list(parts), plain
        self.got = {0: parts[0]}

    def send(self, slots, after=()):
        for slot in slots:
            pairs = [*enumerate(partners(slot, len(self.parts), self.plain))]
            self.got[slot] = lax.ppermute(tied(self.parts[slot], after), "seq", pairs)
        return self

    def all(self):
        return [self.got[slot] for slot in range(len(self.parts))]


def tied(value, after):
    if not after:
        return value
    value, *ended = lax.optimization_barrier((value, *(where.got[slot] for where, slot in after)))
    for (where, slot), got in zip(after, ended):
        where.got[slot] = got
    return value


def local(
    saved_inputs, arrived_grad, loss_grad, norm_gain, w_gate, w_value, w_out, r_factor, l_factor
):
    count = lax.axis_size("seq")
    pipe = lax.axis_size("pipe")
    _, _, rows, width = saved_inputs.shape
    block = w_gate.shape[1]
    size = rows // count

    whole = pl.BlockSpec((rows, width), lambda j: (0, 0))
    whole3 = pl.BlockSpec((None, rows, width), lambda j: (0, 0, 0))
    cut = pl.BlockSpec((rows, block), lambda j: (0, j))
    cut3 = pl.BlockSpec((None, rows, block), lambda j: (0, 0, j))
    weight = pl.BlockSpec((None, block, block), lambda j: (0, 0, j))
    gain = pl.BlockSpec((1, block), lambda j: (0, j))
    square = pl.BlockSpec((None, rows, rows), lambda j: (0, 0, 0))
    small = pl.BlockSpec((None, size, count * count), lambda j: (0, 0, 0))
    slots = [pl.BlockSpec((size, block), lambda j: (0, j))] * count
    anywhere = pl.BlockSpec(memory_space=pl.ANY)
    x_at = [
        pl.BlockSpec((None, None, rows, width), lambda j: (0, 0, 0, 0)),
        pl.BlockSpec((None, None, rows, width), lambda j: (0, 1, 0, 0)),
    ]

    slot_shapes = [jax.ShapeDtypeStruct((size, width), BF16)] * count
    plain = jax.ShapeDtypeStruct((rows, width), BF16)
    exact = jax.ShapeDtypeStruct((rows, width), F32)
    output = jax.ShapeDtypeStruct(saved_inputs.shape, BF16)

    column = pltpu.VMEM((rows, 1), F32)
    wide = pltpu.VMEM((rows, block), F32)
    full = pltpu.VMEM((rows, width), F32)
    square_plain = pl.BlockSpec((rows, rows), lambda j: (0, 0))
    joining = pltpu.VMEM((rows, block), BF16 if size % 16 == 0 else F32)
    product = 2 * rows * width * block

    def call(name, kernel, cost, ins, outs, scratch, mebibytes=32, aliases=None, steps=None):
        return pl.pallas_call(
            kernel,
            grid=(steps or width // block,),
            in_specs=[spec for spec, _ in ins],
            out_specs=[spec for spec, _ in outs],
            out_shape=[shape for _, shape in outs],
            scratch_shapes=scratch,
            input_output_aliases=aliases or {},
            compiler_params=params(mebibytes),
            cost_estimate=pl.CostEstimate(
                flops=int(cost[0] * product),
                bytes_accessed=cost[1] * rows * width * 2,
                transcendentals=0,
            ),
            name=name,
        )(*(value for _, value in ins))

    gains = (gain, norm_gain)
    value_in, gate_in, out_in = (weight, w_value), (weight, w_gate), (weight, w_out)
    r_in = (square, r_factor)
    slots_out = [*zip(slots, slot_shapes)]
    every = range(1, count)

    def first(tick, mebibytes=32):
        return call(
            f"first_{tick}",
            functools.partial(first_kernel, count, tick > 0),
            (2, 4),
            [(x_at[tick], saved_inputs), gains, value_in, r_in],
            slots_out,
            [column, wide],
            mebibytes,
        )

    def grads(tick, incoming):
        *parts, factor = call(
            f"grads_{tick}",
            functools.partial(grad_kernel, count, len(incoming)),
            (2, 8),
            [(x_at[tick], saved_inputs), gains, gate_in, out_in, *incoming],
            [*slots_out, (cut, exact)],
            [column, wide],
        )
        return parts, factor

    def mix(name, parts, transposed, matrix):
        return call(
            name,
            functools.partial(mix_kernel, count, transposed),
            (40 if name == "mix_1" else 1, 2),
            [(square_plain, matrix), *zip(slots, parts)],
            slots_out,
            [],
        )

    def back(tick, mixed, factor):
        return call(
            f"back_{tick}",
            functools.partial(back_kernel, count, tick > 0),
            (1, 6),
            [gate_in, (cut, factor), *zip(slots, mixed)],
            [(cut, exact)],
            [joining],
        )[0]

    def result(tick, gate_part, folded, incoming, stacked):
        ins = [(x_at[tick], saved_inputs), gains, value_in, r_in, (cut, gate_part)]
        ins += [*zip(slots, folded), *incoming]
        outs = [(x_at[tick], output)]
        aliases = {}
        if stacked is None:
            outs.append((whole, plain))
        else:
            ins.append((anywhere, stacked))
            aliases = {len(ins) - 1: 0}
        return call(
            f"result_{tick}",
            functools.partial(result_kernel, count, len(incoming)),
            (3, 8),
            ins,
            outs,
            [joining, full, column],
            aliases=aliases,
        )

    first_0 = Exchange(first(0, 60)).send(every)
    matrix, plain_matrix = (
        call(
            f"matrix_{plain}",
            functools.partial(matrix_kernel, count, plain),
            (0.3, 1),
            [(small, l_factor)],
            [(square_plain, jax.ShapeDtypeStruct((rows, rows), BF16))],
            [],
            steps=1,
        )[0]
        for plain in (False, True)
    )
    parts, factor_0 = grads(0, [(cut3, arrived_grad)])
    grad_0 = Exchange(parts).send(every)
    mix_0 = Exchange(mix("mix_0", first_0.all(), False, matrix)).send(every)
    fold_0 = Exchange(mix("fold_0", grad_0.all(), True, matrix)).send(every)
    gate_0 = back(0, mix_0.all(), factor_0)
    first_1 = Exchange(first(1), True)
    gate_0, first_1.parts[0] = lax.optimization_barrier((gate_0, first_1.parts[0]))
    first_1.send(every)
    stacked, result_0 = result(0, gate_0, fold_0.all(), [(whole3, arrived_grad)], None)
    passed = lax.ppermute(result_0, "pipe", [(s, s - 1) for s in range(1, pipe)])
    mix_1 = Exchange(mix("mix_1", first_1.all(), False, plain_matrix), True).send(every)
    passed, mix_1.parts[0] = lax.optimization_barrier((passed, mix_1.parts[0]))
    mix_1.got[0] = mix_1.parts[0]
    parts, factor_1 = grads(1, [(cut, passed), (cut3, loss_grad)])
    for slot in every[:2]:
        parts[count - slot] = tied(parts[count - slot], [(mix_1, count // 2 - 1 + slot)])
    grad_1 = Exchange(parts).send(every)
    fold_1 = Exchange(mix("fold_1", grad_1.all(), True, matrix)).send(every)
    gate_1 = back(1, mix_1.all(), factor_1)
    incoming = [(whole, passed), (whole3, loss_grad)]
    return result(1, gate_1, fold_1.all(), incoming, stacked)[0]


def solution(mesh):
    placed = (
        P("pipe", None, "seq", None),
        P("pipe", "seq", None),
        P(None, "seq", None),
        P("pipe", None),
        P("pipe", None, None),
        P("pipe", None, None),
        P("pipe", None, None),
        P("pipe", "seq", None),
        P("pipe", "seq", None),
    )
    return jax.shard_map(
        local, mesh=mesh, in_specs=placed, out_specs=P("pipe", None, "seq", None), check_vma=False
    )
```

```python
import functools

import jax
import jax.numpy as jnp
from jax import lax
from jax.experimental import pallas as pl
from jax.experimental.pallas import tpu as pltpu
from jax.sharding import PartitionSpec as P

TICKS = 2
EPSILON = 1e-05
F32 = jnp.float32
BF16 = jnp.bfloat16
def params(mebibytes=32):
    return pltpu.CompilerParams(
        dimension_semantics=("arbitrary",), vmem_limit_bytes=mebibytes * 1024 * 1024
    )


def dot(a, b, over=((1,), (0,))):
    return lax.dot_general(a, b, (over, ((), ())), preferred_element_type=F32)


PAIRINGS = (
    ((0, 7), (1, 6), (2, 5), (3, 4)),
    ((0, 1), (2, 4), (3, 7), (5, 6)),
    ((0, 3), (1, 5), (2, 6), (4, 7)),
    ((0, 4), (1, 2), (3, 5), (6, 7)),
    ((0, 2), (1, 7), (3, 6), (4, 5)),
    ((0, 6), (1, 4), (2, 3), (5, 7)),
    ((0, 5), (1, 3), (2, 7), (4, 6)),
)


def partners(slot, count):
    if slot == 0 or count != 8:
        return [device ^ slot for device in range(count)]
    both = dict(PAIRINGS[slot - 1])
    both.update({b: a for a, b in both.items()})
    return [both[device] for device in range(count)]


def owner_of(slot, count):
    me = lax.axis_index("seq")
    if slot == 0 or count != 8:
        return me ^ slot
    packed = sum(partner << (3 * device) for device, partner in enumerate(partners(slot, count)))
    return (packed >> (3 * me)) & 7


def owners_of(slots, count):
    if count != 8:
        return slots ^ lax.axis_index("seq")
    owners = jnp.zeros_like(slots)
    for slot in range(count):
        owners = jnp.where(slots == slot, owner_of(slot, count), owners)
    return owners


def rows_of(slot, size):
    owner = owner_of(slot, lax.axis_size("seq"))
    return pl.ds(pl.multiple_of(owner * size, size), size)


def inverse_rms(x_ref):
    x = x_ref[...].astype(F32)
    return lax.rsqrt(jnp.mean(x * x, axis=-1, keepdims=True) + EPSILON)


def columns(j, width):
    return pl.ds(pl.multiple_of(j * width, 128), width)


def split(outs, wide_ref):
    for slot, out in enumerate(outs):
        out[...] = wide_ref[rows_of(slot, out.shape[0]), :].astype(BF16)


def normed_block(j, x_ref, gain_ref, q_ref, width):
    @pl.when(j == 0)
    def _():
        q_ref[...] = inverse_rms(x_ref)

    x = x_ref[:, columns(j, width)].astype(F32)
    return (x * q_ref[...] * gain_ref[...]).astype(BF16)


def first_of(normed, w_ref, r_ref):
    return dot(r_ref[...], dot(normed, w_ref[...]).astype(BF16))


def grads_of(normed, grad, w_gate_ref, w_out_ref, factor_ref):
    gate = dot(normed, w_gate_ref[...])
    inner = dot(grad, w_out_ref[...], ((1,), (1,)))
    sigmoid = jax.nn.sigmoid(gate)
    factor_ref[...] = inner * sigmoid * (1.0 + gate * (1.0 - sigmoid))
    return inner * gate * sigmoid


def first_kernel(count, x_ref, gain_ref, w_ref, r_ref, *refs):
    outs, (q_ref, wide_ref) = refs[:count], refs[count:]
    normed = normed_block(pl.program_id(0), x_ref, gain_ref, q_ref, w_ref.shape[1])
    wide_ref[...] = first_of(normed, w_ref, r_ref)
    split(outs, wide_ref)


def pick_gradient(refs):
    if len(refs) == 1:
        return refs[0][...]
    last = lax.axis_index("pipe") == lax.axis_size("pipe") - 1
    return jnp.where(last, refs[1][...], refs[0][...])


def grad_kernel(count, sources, x_ref, gain_ref, w_gate_ref, w_out_ref, *refs):
    grads, refs = refs[:sources], refs[sources:]
    outs, (factor_ref, q_ref, wide_ref) = refs[:count], refs[count:]
    normed = normed_block(pl.program_id(0), x_ref, gain_ref, q_ref, w_gate_ref.shape[1])
    wide_ref[...] = grads_of(normed, pick_gradient(grads), w_gate_ref, w_out_ref, factor_ref)
    split(outs, wide_ref)


def matrix_kernel(count, l_ref, out_ref):
    size = l_ref.shape[0]
    wide = count * size
    bits = count.bit_length() - 1
    iota = functools.partial(lax.broadcasted_iota, jnp.int32)

    shape = (count, size, count * count)
    tall = jnp.broadcast_to(l_ref[...].astype(F32)[None], shape)
    tall = jnp.where(iota(shape, 2) >> bits == owners_of(iota(shape, 0), count), tall, 0.0)
    tall = tall.reshape(wide, count * count).astype(BF16)

    shape = (count * count, wide)
    source = owners_of(iota(shape, 1) >> (size.bit_length() - 1), count)
    spread = dot(tall, jnp.where(iota(shape, 0) & (count - 1) == source, 1.0, 0.0).astype(BF16))

    row, column = iota((wide, wide), 0) & (size - 1), iota((wide, wide), 1) & (size - 1)
    out_ref[...] = jnp.where(row == column, spread, 0.0).astype(BF16)


def stacked_slots(ins):
    if ins[0].shape[0] % 16 == 0:
        return jnp.concatenate([part[...] for part in ins], axis=0)
    return jnp.concatenate([part[...].astype(F32) for part in ins], axis=0).astype(BF16)


def spread_slots(outs, value):
    size = outs[0].shape[0]
    for slot, out in enumerate(outs):
        out[...] = value[slot * size : (slot + 1) * size].astype(BF16)


def joined(ins, wide_ref):
    for slot, part in enumerate(ins):
        wide_ref[rows_of(slot, part.shape[0]), :] = part[...].astype(wide_ref.dtype)
    return wide_ref[...]


def mix_kernel(count, transposed, m_ref, *refs):
    ins, outs = refs[:count], refs[count:]
    over = ((0,), (0,)) if transposed else ((1,), (0,))
    spread_slots(outs, dot(m_ref[...], stacked_slots(ins), over))


def mix_first_kernel(count, x_ref, gain_ref, w_ref, r_ref, m_ref, *refs):
    ins, outs, (q_ref, wide_ref) = refs[:count], refs[count : 2 * count], refs[2 * count :]
    spread_slots([out.at[0] for out in outs], dot(m_ref[...], stacked_slots(ins)))
    normed = normed_block(pl.program_id(0), x_ref, gain_ref, q_ref, w_ref.shape[1])
    wide_ref[...] = first_of(normed, w_ref, r_ref)
    split([out.at[1] for out in outs], wide_ref)


def back_kernel(count, w_gate_ref, factor_ref, *refs):
    mixed, (out_ref, wide_ref) = refs[:count], refs[count:]
    gate_grad = (factor_ref[...] * joined(mixed, wide_ref).astype(F32)).astype(BF16)
    out_ref[...] = dot(gate_grad, w_gate_ref[...], ((1,), (1,)))


def finish(j, back, folded, grads, outs, x_ref, gain_ref, w_value_ref, r_ref, e_ref, sum_ref):
    at = columns(j, w_value_ref.shape[1])
    value_grad = dot(r_ref[...], folded.astype(BF16), ((0,), (0,))).astype(BF16)
    e = (back + dot(value_grad, w_value_ref[...], ((1,), (1,)))) * gain_ref[...]
    e_ref[:, at] = e
    part = jnp.sum(e * x_ref[:, at].astype(F32), axis=-1, keepdims=True)

    @pl.when(j == 0)
    def _():
        sum_ref[...] = part

    @pl.when(j > 0)
    def _():
        sum_ref[...] += part

    @pl.when(j == pl.num_programs(0) - 1)
    def _():
        x = x_ref[...].astype(F32)
        q = inverse_rms(x_ref)
        mean = sum_ref[...] / x.shape[1]
        result = pick_gradient(grads).astype(F32) + q * e_ref[...] - q * q * q * x * mean
        for out in outs:
            out[...] = result.astype(BF16)


def result_kernel(count, sources, x_ref, gain_ref, w_value_ref, r_ref, back_ref, *refs):
    folded, refs = refs[:count], refs[count:]
    grads, refs = refs[:sources], refs[sources:]
    outs, (wide_ref, e_ref, sum_ref) = refs[sources - 1 : -3], refs[-3:]
    finish(
        pl.program_id(0), back_ref[...], joined(folded, wide_ref), grads, outs,
        x_ref, gain_ref, w_value_ref, r_ref, e_ref, sum_ref,
    )


class Exchange:
    def __init__(self, parts):
        self.parts = list(parts)
        self.got = {0: parts[0]}

    def send(self, slots, after=()):
        for slot in slots:
            pairs = [*enumerate(partners(slot, len(self.parts)))]
            self.got[slot] = lax.ppermute(tied(self.parts[slot], after), "seq", pairs)
        return self

    def all(self):
        return [self.got[slot] for slot in range(len(self.parts))]


def tied(value, after):
    if not after:
        return value
    value, *ended = lax.optimization_barrier((value, *(where.got[slot] for where, slot in after)))
    for (where, slot), got in zip(after, ended):
        where.got[slot] = got
    return value


def local(
    saved_inputs, arrived_grad, loss_grad, norm_gain, w_gate, w_value, w_out, r_factor, l_factor
):
    count = lax.axis_size("seq")
    pipe = lax.axis_size("pipe")
    _, _, rows, width = saved_inputs.shape
    block = w_gate.shape[1]
    size = rows // count

    whole = pl.BlockSpec((rows, width), lambda j: (0, 0))
    whole3 = pl.BlockSpec((None, rows, width), lambda j: (0, 0, 0))
    cut = pl.BlockSpec((rows, block), lambda j: (0, j))
    cut3 = pl.BlockSpec((None, rows, block), lambda j: (0, 0, j))
    weight = pl.BlockSpec((None, block, block), lambda j: (0, 0, j))
    gain = pl.BlockSpec((1, block), lambda j: (0, j))
    square = pl.BlockSpec((None, rows, rows), lambda j: (0, 0, 0))
    small = pl.BlockSpec((None, size, count * count), lambda j: (0, 0, 0))
    slots = [pl.BlockSpec((size, block), lambda j: (0, j))] * count
    pairs = [pl.BlockSpec((2, size, block), lambda j: (0, 0, j))] * count
    upper = [pl.BlockSpec((None, size, block), lambda j: (0, 0, j))] * count
    lower = [pl.BlockSpec((None, size, block), lambda j: (1, 0, j))] * count
    anywhere = pl.BlockSpec(memory_space=pl.ANY)
    x_at = [
        pl.BlockSpec((None, None, rows, width), lambda j: (0, 0, 0, 0)),
        pl.BlockSpec((None, None, rows, width), lambda j: (0, 1, 0, 0)),
    ]

    slot_shapes = [jax.ShapeDtypeStruct((size, width), BF16)] * count
    pair_shapes = [jax.ShapeDtypeStruct((2, size, width), BF16)] * count
    plain = jax.ShapeDtypeStruct((rows, width), BF16)
    exact = jax.ShapeDtypeStruct((rows, width), F32)
    output = jax.ShapeDtypeStruct(saved_inputs.shape, BF16)

    column = pltpu.VMEM((rows, 1), F32)
    wide = pltpu.VMEM((rows, block), F32)
    full = pltpu.VMEM((rows, width), F32)
    square_plain = pl.BlockSpec((rows, rows), lambda j: (0, 0))
    joining = pltpu.VMEM((rows, block), BF16 if size % 16 == 0 else F32)
    product = 2 * rows * width * block

    def call(name, kernel, cost, ins, outs, scratch, mebibytes=32, aliases=None, steps=None):
        return pl.pallas_call(
            kernel,
            grid=(steps or width // block,),
            in_specs=[spec for spec, _ in ins],
            out_specs=[spec for spec, _ in outs],
            out_shape=[shape for _, shape in outs],
            scratch_shapes=scratch,
            input_output_aliases=aliases or {},
            compiler_params=params(mebibytes),
            cost_estimate=pl.CostEstimate(
                flops=int(cost[0] * product),
                bytes_accessed=cost[1] * rows * width * 2,
                transcendentals=0,
            ),
            name=name,
        )(*(value for _, value in ins))

    gains = (gain, norm_gain)
    value_in, gate_in, out_in = (weight, w_value), (weight, w_gate), (weight, w_out)
    r_in = (square, r_factor)
    slots_out = [*zip(slots, slot_shapes)]
    every = range(1, count)

    def first(tick, mebibytes=32):
        return call(
            f"first_{tick}",
            functools.partial(first_kernel, count),
            (2, 4),
            [(x_at[tick], saved_inputs), gains, value_in, r_in],
            slots_out,
            [column, wide],
            mebibytes,
        )

    def grads(tick, incoming):
        *parts, factor = call(
            f"grads_{tick}",
            functools.partial(grad_kernel, count, len(incoming)),
            (2, 8),
            [(x_at[tick], saved_inputs), gains, gate_in, out_in, *incoming],
            [*slots_out, (cut, exact)],
            [column, wide],
        )
        return parts, factor

    def mix(name, parts, transposed, slots_in=slots):
        return call(
            name,
            functools.partial(mix_kernel, count, transposed),
            (1, 2),
            [(square_plain, matrix), *zip(slots_in, parts)],
            slots_out,
            [],
        )

    def back(tick, mixed, factor, slots_in=slots):
        return call(
            f"back_{tick}",
            functools.partial(back_kernel, count),
            (1, 6),
            [gate_in, (cut, factor), *zip(slots_in, mixed)],
            [(cut, exact)],
            [joining],
        )[0]

    def result(tick, gate_part, folded, incoming, stacked):
        ins = [(x_at[tick], saved_inputs), gains, value_in, r_in, (cut, gate_part)]
        ins += [*zip(slots, folded), *incoming]
        outs = [(x_at[tick], output)]
        aliases = {}
        if stacked is None:
            outs.append((whole, plain))
        else:
            ins.append((anywhere, stacked))
            aliases = {len(ins) - 1: 0}
        return call(
            f"result_{tick}",
            functools.partial(result_kernel, count, len(incoming)),
            (3, 8),
            ins,
            outs,
            [joining, full, column],
            aliases=aliases,
        )

    first_0 = Exchange(first(0, 60)).send(every)
    (matrix,) = call(
        "matrix",
        functools.partial(matrix_kernel, count),
        (0.3, 1),
        [(small, l_factor)],
        [(square_plain, jax.ShapeDtypeStruct((rows, rows), BF16))],
        [],
        steps=1,
    )
    parts, factor_0 = grads(0, [(cut3, arrived_grad)])
    grad_0 = Exchange(parts).send(every)
    there = Exchange(
        call(
            "mixfirst_0",
            functools.partial(mix_first_kernel, count),
            (3, 6),
            [
                (x_at[1], saved_inputs), gains, value_in, r_in, (square_plain, matrix),
                *zip(slots, first_0.all()),
            ],
            [*zip(pairs, pair_shapes)],
            [column, wide],
        )
    ).send(every)
    fold_0 = Exchange(mix("fold_0", grad_0.all(), True)).send(every)
    gate_0 = back(0, there.all(), factor_0, upper)
    mix_1 = Exchange(mix("mix_1", there.all(), False, lower))
    gate_0, mix_1.parts[0] = lax.optimization_barrier((gate_0, mix_1.parts[0]))
    mix_1.got[0] = mix_1.parts[0]
    mix_1.send(every)
    stacked, result_0 = result(0, gate_0, fold_0.all(), [(whole3, arrived_grad)], None)
    result_0 = tied(result_0, [(mix_1, slot) for slot in every[: min(4, count // 2)]])
    passed = lax.ppermute(result_0, "pipe", [(s, s - 1) for s in range(1, pipe)])
    parts, factor_1 = grads(1, [(cut, passed), (cut3, loss_grad)])
    grad_1 = Exchange(parts).send(every)
    fold_1 = Exchange(mix("fold_1", grad_1.all(), True)).send(every)
    gate_1 = back(1, mix_1.all(), factor_1)
    incoming = [(whole, passed), (whole3, loss_grad)]
    return result(1, gate_1, fold_1.all(), incoming, stacked)[0]


def solution(mesh):
    placed = (
        P("pipe", None, "seq", None),
        P("pipe", "seq", None),
        P(None, "seq", None),
        P("pipe", None),
        P("pipe", None, None),
        P("pipe", None, None),
        P("pipe", None, None),
        P("pipe", "seq", None),
        P("pipe", "seq", None),
    )
    return jax.shard_map(
        local, mesh=mesh, in_specs=placed, out_specs=P("pipe", None, "seq", None), check_vma=False
    )
```

```python
import functools

import jax
import jax.numpy as jnp
from jax import lax
from jax.experimental import pallas as pl
from jax.experimental.pallas import tpu as pltpu
from jax.sharding import PartitionSpec as P

TICKS = 2
EPSILON = 1e-05
F32 = jnp.float32
BF16 = jnp.bfloat16
def params(mebibytes=32):
    return pltpu.CompilerParams(
        dimension_semantics=("arbitrary",), vmem_limit_bytes=mebibytes * 1024 * 1024
    )


def dot(a, b, over=((1,), (0,))):
    return lax.dot_general(a, b, (over, ((), ())), preferred_element_type=F32)


PAIRINGS = (
    ((0, 7), (1, 6), (2, 5), (3, 4)),
    ((0, 1), (2, 4), (3, 7), (5, 6)),
    ((0, 3), (1, 5), (2, 6), (4, 7)),
    ((0, 4), (1, 2), (3, 5), (6, 7)),
    ((0, 2), (1, 7), (3, 6), (4, 5)),
    ((0, 6), (1, 4), (2, 3), (5, 7)),
    ((0, 5), (1, 3), (2, 7), (4, 6)),
)


def partners(slot, count):
    if slot == 0 or count != 8:
        return [device ^ slot for device in range(count)]
    both = dict(PAIRINGS[slot - 1])
    both.update({b: a for a, b in both.items()})
    return [both[device] for device in range(count)]


def owner_of(slot, count):
    me = lax.axis_index("seq")
    if slot == 0 or count != 8:
        return me ^ slot
    packed = sum(partner << (3 * device) for device, partner in enumerate(partners(slot, count)))
    return (packed >> (3 * me)) & 7


def owners_of(slots, count):
    if count != 8:
        return slots ^ lax.axis_index("seq")
    owners = jnp.zeros_like(slots)
    for slot in range(count):
        owners = jnp.where(slots == slot, owner_of(slot, count), owners)
    return owners


def rows_of(slot, size):
    owner = owner_of(slot, lax.axis_size("seq"))
    return pl.ds(pl.multiple_of(owner * size, size), size)


def inverse_rms(x_ref):
    x = x_ref[...].astype(F32)
    return lax.rsqrt(jnp.mean(x * x, axis=-1, keepdims=True) + EPSILON)


def columns(j, width):
    return pl.ds(pl.multiple_of(j * width, 128), width)


def split(outs, wide_ref):
    for slot, out in enumerate(outs):
        out[...] = wide_ref[rows_of(slot, out.shape[0]), :].astype(BF16)


def normed_block(j, x_ref, gain_ref, q_ref, width):
    @pl.when(j == 0)
    def _():
        q_ref[...] = inverse_rms(x_ref)

    x = x_ref[:, columns(j, width)].astype(F32)
    return (x * q_ref[...] * gain_ref[...]).astype(BF16)


def first_of(normed, w_ref, r_ref):
    return dot(r_ref[...], dot(normed, w_ref[...]).astype(BF16))


def grads_of(normed, grad, w_gate_ref, w_out_ref, factor_ref):
    gate = dot(normed, w_gate_ref[...])
    inner = dot(grad, w_out_ref[...], ((1,), (1,)))
    sigmoid = jax.nn.sigmoid(gate)
    factor_ref[...] = inner * sigmoid * (1.0 + gate * (1.0 - sigmoid))
    return inner * gate * sigmoid


def first_kernel(count, x_ref, gain_ref, w_ref, r_ref, *refs):
    outs, (q_ref, wide_ref) = refs[:count], refs[count:]
    normed = normed_block(pl.program_id(0), x_ref, gain_ref, q_ref, w_ref.shape[1])
    wide_ref[...] = first_of(normed, w_ref, r_ref)
    split(outs, wide_ref)


def pick_gradient(refs):
    if len(refs) == 1:
        return refs[0][...]
    last = lax.axis_index("pipe") == lax.axis_size("pipe") - 1
    return jnp.where(last, refs[1][...], refs[0][...])


def grad_kernel(count, sources, x_ref, gain_ref, w_gate_ref, w_out_ref, *refs):
    grads, refs = refs[:sources], refs[sources:]
    outs, (factor_ref, q_ref, wide_ref) = refs[:count], refs[count:]
    normed = normed_block(pl.program_id(0), x_ref, gain_ref, q_ref, w_gate_ref.shape[1])
    wide_ref[...] = grads_of(normed, pick_gradient(grads), w_gate_ref, w_out_ref, factor_ref)
    split(outs, wide_ref)


def matrix_kernel(count, l_ref, out_ref):
    size = l_ref.shape[0]
    wide = count * size
    bits = count.bit_length() - 1
    iota = functools.partial(lax.broadcasted_iota, jnp.int32)

    shape = (count, size, count * count)
    tall = jnp.broadcast_to(l_ref[...].astype(F32)[None], shape)
    tall = jnp.where(iota(shape, 2) >> bits == owners_of(iota(shape, 0), count), tall, 0.0)
    tall = tall.reshape(wide, count * count).astype(BF16)

    shape = (count * count, wide)
    source = owners_of(iota(shape, 1) >> (size.bit_length() - 1), count)
    spread = dot(tall, jnp.where(iota(shape, 0) & (count - 1) == source, 1.0, 0.0).astype(BF16))

    row, column = iota((wide, wide), 0) & (size - 1), iota((wide, wide), 1) & (size - 1)
    out_ref[...] = jnp.where(row == column, spread, 0.0).astype(BF16)


def stacked_slots(ins):
    if ins[0].shape[0] % 16 == 0:
        return jnp.concatenate([part[...] for part in ins], axis=0)
    return jnp.concatenate([part[...].astype(F32) for part in ins], axis=0).astype(BF16)


def spread_slots(outs, value):
    size = outs[0].shape[0]
    for slot, out in enumerate(outs):
        out[...] = value[slot * size : (slot + 1) * size].astype(BF16)


def joined(ins, wide_ref):
    for slot, part in enumerate(ins):
        wide_ref[rows_of(slot, part.shape[0]), :] = part[...].astype(wide_ref.dtype)
    return wide_ref[...]


def mix_kernel(count, transposed, m_ref, *refs):
    ins, outs = refs[:count], refs[count:]
    over = ((0,), (0,)) if transposed else ((1,), (0,))
    spread_slots(outs, dot(m_ref[...], stacked_slots(ins), over))


def mix_first_kernel(count, x_ref, gain_ref, w_ref, r_ref, m_ref, *refs):
    ins, outs, (q_ref, wide_ref) = refs[:count], refs[count : 2 * count], refs[2 * count :]
    spread_slots([out.at[0] for out in outs], dot(m_ref[...], stacked_slots(ins)))
    normed = normed_block(pl.program_id(0), x_ref, gain_ref, q_ref, w_ref.shape[1])
    wide_ref[...] = first_of(normed, w_ref, r_ref)
    split([out.at[1] for out in outs], wide_ref)


def back_kernel(count, w_gate_ref, factor_ref, *refs):
    mixed, (out_ref, wide_ref) = refs[:count], refs[count:]
    gate_grad = (factor_ref[...] * joined(mixed, wide_ref).astype(F32)).astype(BF16)
    out_ref[...] = dot(gate_grad, w_gate_ref[...], ((1,), (1,)))


def finish(j, back, folded, grads, outs, x_ref, gain_ref, w_value_ref, r_ref, e_ref, sum_ref):
    at = columns(j, w_value_ref.shape[1])
    value_grad = dot(r_ref[...], folded.astype(BF16), ((0,), (0,))).astype(BF16)
    e = (back + dot(value_grad, w_value_ref[...], ((1,), (1,)))) * gain_ref[...]
    e_ref[:, at] = e
    part = jnp.sum(e * x_ref[:, at].astype(F32), axis=-1, keepdims=True)

    @pl.when(j == 0)
    def _():
        sum_ref[...] = part

    @pl.when(j > 0)
    def _():
        sum_ref[...] += part

    @pl.when(j == pl.num_programs(0) - 1)
    def _():
        x = x_ref[...].astype(F32)
        q = inverse_rms(x_ref)
        mean = sum_ref[...] / x.shape[1]
        result = pick_gradient(grads).astype(F32) + q * e_ref[...] - q * q * q * x * mean
        for out in outs:
            out[...] = result.astype(BF16)


def result_kernel(count, sources, x_ref, gain_ref, w_value_ref, r_ref, back_ref, *refs):
    folded, refs = refs[:count], refs[count:]
    grads, refs = refs[:sources], refs[sources:]
    outs, (wide_ref, e_ref, sum_ref) = refs[sources - 1 : -3], refs[-3:]
    finish(
        pl.program_id(0), back_ref[...], joined(folded, wide_ref), grads, outs,
        x_ref, gain_ref, w_value_ref, r_ref, e_ref, sum_ref,
    )


class Exchange:
    def __init__(self, parts):
        self.parts = list(parts)
        self.got = {0: parts[0]}

    def send(self, slots, after=()):
        for slot in slots:
            pairs = [*enumerate(partners(slot, len(self.parts)))]
            self.got[slot] = lax.ppermute(tied(self.parts[slot], after), "seq", pairs)
        return self

    def all(self):
        return [self.got[slot] for slot in range(len(self.parts))]


def tied(value, after):
    if not after:
        return value
    value, *ended = lax.optimization_barrier((value, *(where.got[slot] for where, slot in after)))
    for (where, slot), got in zip(after, ended):
        where.got[slot] = got
    return value


def local(
    saved_inputs, arrived_grad, loss_grad, norm_gain, w_gate, w_value, w_out, r_factor, l_factor
):
    count = lax.axis_size("seq")
    pipe = lax.axis_size("pipe")
    _, _, rows, width = saved_inputs.shape
    block = w_gate.shape[1]
    size = rows // count

    whole = pl.BlockSpec((rows, width), lambda j: (0, 0))
    whole3 = pl.BlockSpec((None, rows, width), lambda j: (0, 0, 0))
    cut = pl.BlockSpec((rows, block), lambda j: (0, j))
    cut3 = pl.BlockSpec((None, rows, block), lambda j: (0, 0, j))
    weight = pl.BlockSpec((None, block, block), lambda j: (0, 0, j))
    gain = pl.BlockSpec((1, block), lambda j: (0, j))
    square = pl.BlockSpec((None, rows, rows), lambda j: (0, 0, 0))
    small = pl.BlockSpec((None, size, count * count), lambda j: (0, 0, 0))
    slots = [pl.BlockSpec((size, block), lambda j: (0, j))] * count
    pairs = [pl.BlockSpec((2, size, block), lambda j: (0, 0, j))] * count
    upper = [pl.BlockSpec((None, size, block), lambda j: (0, 0, j))] * count
    lower = [pl.BlockSpec((None, size, block), lambda j: (1, 0, j))] * count
    anywhere = pl.BlockSpec(memory_space=pl.ANY)
    x_at = [
        pl.BlockSpec((None, None, rows, width), lambda j: (0, 0, 0, 0)),
        pl.BlockSpec((None, None, rows, width), lambda j: (0, 1, 0, 0)),
    ]

    slot_shapes = [jax.ShapeDtypeStruct((size, width), BF16)] * count
    pair_shapes = [jax.ShapeDtypeStruct((2, size, width), BF16)] * count
    plain = jax.ShapeDtypeStruct((rows, width), BF16)
    exact = jax.ShapeDtypeStruct((rows, width), F32)
    output = jax.ShapeDtypeStruct(saved_inputs.shape, BF16)

    column = pltpu.VMEM((rows, 1), F32)
    wide = pltpu.VMEM((rows, block), F32)
    full = pltpu.VMEM((rows, width), F32)
    square_plain = pl.BlockSpec((rows, rows), lambda j: (0, 0))
    joining = pltpu.VMEM((rows, block), BF16 if size % 16 == 0 else F32)
    product = 2 * rows * width * block

    def call(name, kernel, cost, ins, outs, scratch, mebibytes=32, aliases=None, steps=None):
        return pl.pallas_call(
            kernel,
            grid=(steps or width // block,),
            in_specs=[spec for spec, _ in ins],
            out_specs=[spec for spec, _ in outs],
            out_shape=[shape for _, shape in outs],
            scratch_shapes=scratch,
            input_output_aliases=aliases or {},
            compiler_params=params(mebibytes),
            cost_estimate=pl.CostEstimate(
                flops=int(cost[0] * product),
                bytes_accessed=cost[1] * rows * width * 2,
                transcendentals=0,
            ),
            name=name,
        )(*(value for _, value in ins))

    gains = (gain, norm_gain)
    value_in, gate_in, out_in = (weight, w_value), (weight, w_gate), (weight, w_out)
    r_in = (square, r_factor)
    slots_out = [*zip(slots, slot_shapes)]
    every = range(1, count)

    def first(tick, mebibytes=32):
        return call(
            f"first_{tick}",
            functools.partial(first_kernel, count),
            (2, 4),
            [(x_at[tick], saved_inputs), gains, value_in, r_in],
            slots_out,
            [column, wide],
            mebibytes,
        )

    def grads(tick, incoming):
        *parts, factor = call(
            f"grads_{tick}",
            functools.partial(grad_kernel, count, len(incoming)),
            (2, 8),
            [(x_at[tick], saved_inputs), gains, gate_in, out_in, *incoming],
            [*slots_out, (cut, exact)],
            [column, wide],
        )
        return parts, factor

    def mix(name, parts, transposed, slots_in=slots):
        return call(
            name,
            functools.partial(mix_kernel, count, transposed),
            (1, 2),
            [(square_plain, matrix), *zip(slots_in, parts)],
            slots_out,
            [],
        )

    def back(tick, mixed, factor, slots_in=slots):
        return call(
            f"back_{tick}",
            functools.partial(back_kernel, count),
            (1, 6),
            [gate_in, (cut, factor), *zip(slots_in, mixed)],
            [(cut, exact)],
            [joining],
        )[0]

    def result(tick, gate_part, folded, incoming, stacked):
        ins = [(x_at[tick], saved_inputs), gains, value_in, r_in, (cut, gate_part)]
        ins += [*zip(slots, folded), *incoming]
        outs = [(x_at[tick], output)]
        aliases = {}
        if stacked is None:
            outs.append((whole, plain))
        else:
            ins.append((anywhere, stacked))
            aliases = {len(ins) - 1: 0}
        return call(
            f"result_{tick}",
            functools.partial(result_kernel, count, len(incoming)),
            (3, 8),
            ins,
            outs,
            [joining, full, column],
            aliases=aliases,
        )

    first_0 = Exchange(first(0, 60)).send(every)
    (matrix,) = call(
        "matrix",
        functools.partial(matrix_kernel, count),
        (0.3, 1),
        [(small, l_factor)],
        [(square_plain, jax.ShapeDtypeStruct((rows, rows), BF16))],
        [],
        steps=1,
    )
    parts, factor_0 = grads(0, [(cut3, arrived_grad)])
    grad_0 = Exchange(parts).send(every)
    there = Exchange(
        call(
            "mixfirst_0",
            functools.partial(mix_first_kernel, count),
            (3, 6),
            [
                (x_at[1], saved_inputs), gains, value_in, r_in, (square_plain, matrix),
                *zip(slots, first_0.all()),
            ],
            [*zip(pairs, pair_shapes)],
            [column, wide],
        )
    ).send(every)
    fold_0 = Exchange(mix("fold_0", grad_0.all(), True)).send(every)
    gate_0 = back(0, there.all(), factor_0, upper)
    mix_1 = Exchange(mix("mix_1", there.all(), False, lower))
    gate_0, mix_1.parts[0] = lax.optimization_barrier((gate_0, mix_1.parts[0]))
    mix_1.got[0] = mix_1.parts[0]
    mix_1.send(every)
    stacked, result_0 = result(0, gate_0, fold_0.all(), [(whole3, arrived_grad)], None)
    result_0 = tied(result_0, [(mix_1, slot) for slot in every[: min(4, count // 2)]])
    passed = lax.ppermute(result_0, "pipe", [(s, s - 1) for s in range(1, pipe)])
    passed = tied(passed, [(mix_1, slot) for slot in every[4:]])
    parts, factor_1 = grads(1, [(cut, passed), (cut3, loss_grad)])
    grad_1 = Exchange(parts).send(every)
    fold_1 = Exchange(mix("fold_1", grad_1.all(), True)).send(every)
    gate_1 = back(1, mix_1.all(), factor_1)
    incoming = [(whole, passed), (whole3, loss_grad)]
    return result(1, gate_1, fold_1.all(), incoming, stacked)[0]


def solution(mesh):
    placed = (
        P("pipe", None, "seq", None),
        P("pipe", "seq", None),
        P(None, "seq", None),
        P("pipe", None),
        P("pipe", None, None),
        P("pipe", None, None),
        P("pipe", None, None),
        P("pipe", "seq", None),
        P("pipe", "seq", None),
    )
    return jax.shard_map(
        local, mesh=mesh, in_specs=placed, out_specs=P("pipe", None, "seq", None), check_vma=False
    )
```
